32 devices in a mesh: seq: 8 (over z, y), batch: 4 (over x, core).
Axes of the slice: x: 2, y: 2, z: 4, core: 2. Of those that a mesh axis runs over, the one named last changes fastest.
Arguments:
- incoming_symbols: bfloat16 [8, 2048, 1024], P('batch', 'seq'), may hold values from -6 to 6
- article_sizes: int32 [8, 8], P('batch'), may hold values from 1 to 2041, as said below
- mixer_norm_scale: float32 [1024], replicated, may hold values from 0.1 to 1.9
- mixer_norm_offset: float32 [1024], replicated, may hold values from -2 to 2
- temporal_lookup_share: float32 [1024], replicated, may hold values from 0 to 1
- temporal_payload_share: float32 [1024], replicated, may hold values from 0 to 1
- temporal_gate_share: float32 [1024], replicated, may hold values from 0 to 1
- fading_log_rates: float32 [1024], replicated
- present_reward_vector: float32 [1024], replicated, may hold values from -1 to 1
- lookup_matrix: bfloat16 [1024, 1024], replicated, may hold values from -0.1875 to 0.1875
- payload_matrix: bfloat16 [1024, 1024], replicated, may hold values from -0.1875 to 0.1875
- gate_matrix: bfloat16 [1024, 1024], replicated, may hold values from -0.1875 to 0.1875
- emission_matrix: bfloat16 [1024, 1024], replicated, may hold values from -1.5 to 1.5
- channel_norm_scale: float32 [1024], replicated, may hold values from 0.1 to 1.9
- channel_norm_offset: float32 [1024], replicated, may hold values from -2 to 2
- channel_lookup_share: float32 [1024], replicated, may hold values from 0 to 1
- channel_gate_share: float32 [1024], replicated, may hold values from 0 to 1
- channel_lookup_matrix: bfloat16 [1024, 4096], replicated, may hold values from -0.1875 to 0.1875
- channel_payload_matrix: bfloat16 [4096, 1024], replicated, may hold values from -0.09375 to 0.09375
- channel_gate_matrix: bfloat16 [1024, 1024], replicated, may hold values from -0.1875 to 0.1875
- final_cotangent: bfloat16 [8, 2048, 1024], P('batch', 'seq'), may hold values from -6 to 6
Outputs:
- layer_out: bfloat16 [8, 2048, 1024], P('batch', 'seq')
- grad_tokens: bfloat16 [8, 2048, 1024], P('batch', 'seq')
- grad_att_ln_gain: float32 [1024], P('seq')
- grad_att_ln_bias: float32 [1024], P('seq')
- grad_mix_key: float32 [1024], P('seq')
- grad_mix_value: float32 [1024], P('seq')
- grad_mix_recep: float32 [1024], P('seq')
- grad_time_decay: float32 [1024], P('seq')
- reward_slope_array: float32 [1024], P('seq')
- grad_key_weight: float32 [1024, 1024], P('seq')
- grad_value_weight: float32 [1024, 1024], P('seq')
- grad_recep_weight: float32 [1024, 1024], P('seq')
- grad_output_weight: float32 [1024, 1024], P('seq')
- grad_ffn_ln_gain: float32 [1024], P('seq')
- grad_ffn_ln_bias: float32 [1024], P('seq')
- grad_ffn_mix_key: float32 [1024], P('seq')
- grad_ffn_mix_recep: float32 [1024], P('seq')
- grad_ffn_key_weight: float32 [1024, 4096], P('seq')
- grad_ffn_value_weight: float32 [4096, 1024], P('seq')
- grad_ffn_recep_weight: float32 [1024, 1024], P('seq')
The draws below stay inside these ranges and needn't reach their ends.
Inputs may be any that keep to these rules, and one draw needn't show every extreme that they name: `article_sizes`: each row's lengths sum to 2048. In each row one document, whose place in the row is drawn from the seed, is longer than 1792; every other one has at most 32 positions. In one row, drawn from the seed, every other document has exactly one position.
All inputs are finite; a program needn't handle non-finite values.
Results may differ from the reference program's by a relative error of at most 0.009.
Values sent between devices are 32-bit elements; how exact they have to be, the bound alone decides.
No kernel may reach another device: no remote copies, remote signals or barrier semaphores. Data moves between devices by JAX's collectives and lax.ppermute only.
A program may use at most 192 MiB of HBM per device.

```python
import math
from functools import partial
import jax
import jax.numpy as jnp
from jax import lax

EMBED_WIDTH = 1024
FF = 4096
TOK_DEV = 256
DOCS = 8
SEQLEN = 2048
PACKED_LINES = 8
N_SEQ = 8


def draw_article_sizes(key, part):
    key = jax.random.fold_in(key, 11)
    short_key, place_key, row_key = jax.random.split(key, 3)
    shorts = jax.random.randint(short_key, (PACKED_LINES, DOCS), 1, TOK_DEV // 8 + 1)
    tight_row = jax.random.randint(row_key, (), 0, PACKED_LINES)
    row_index = jnp.arange(PACKED_LINES)[:, None]
    shorts = jnp.where(row_index == tight_row, 1, shorts)
    longest = jax.random.randint(place_key, (PACKED_LINES, 1), 0, DOCS)
    column = jnp.arange(DOCS)[None, :]
    chosen = column == longest
    others = jnp.sum(jnp.where(chosen, 0, shorts), axis=1, keepdims=True)
    return jnp.where(chosen, SEQLEN - others, shorts).astype(jnp.int32)


def draw_fading_log_rates(key, part):
    key = jax.random.fold_in(key, 23)
    pick_key, slow_key, fast_key = jax.random.split(key, 3)
    slow_share = 0.5
    slow_rates = jax.random.uniform(slow_key, (EMBED_WIDTH,), jnp.float32, math.log(0.3 / SEQLEN), math.log(2.0 / SEQLEN))
    fast_rates = jax.random.uniform(fast_key, (EMBED_WIDTH,), jnp.float32, math.log(1.0 / 50.0), math.log(1.0 / 15.0))
    return jnp.where(jax.random.uniform(pick_key, (EMBED_WIDTH,)) < slow_share, slow_rates, fast_rates)


def level_of(stream_key, shape, shards, low, top_value):
    gain, own = 1.0, jax.random.fold_in(stream_key, 6)
    for dim, parts in shards:
        steps = jnp.exp(jax.random.uniform(jax.random.fold_in(own, dim), (parts,), jnp.float32, low / len(shards), top_value / len(shards)))
        gain = gain * jnp.repeat(steps, shape[dim] // parts).reshape([-1 if axis == dim else 1 for axis in range(len(shape))])
    return gain


def scatter_about(key, dims, width, most, shards=(), held_as=jnp.bfloat16):
    result = jax.random.normal(key, dims, jnp.float32) * width
    if len(shards) > 0:
        result = level_of(key, dims, shards, -0.22, 0.18) * result
    return jnp.clip(result, min=-most, max=most).astype(held_as)


def setup_inputs(seed: int = 0) -> dict:
    seeds = jax.random.split(jax.random.key(seed), 22)
    incoming_symbols = scatter_about(seeds[0], (PACKED_LINES, SEQLEN, EMBED_WIDTH), 1.0, 6.0, ((0, 4), (1, 8)))
    article_sizes = draw_article_sizes(jax.random.fold_in(seeds[21], 71), 0)
    mixer_norm_scale = jnp.clip(1.0 + 0.18 * jax.random.normal(seeds[2], (EMBED_WIDTH,), jnp.float32), 0.1, 1.9)
    mixer_norm_offset = scatter_about(seeds[3], (EMBED_WIDTH,), 0.3, 2.0, (), jnp.float32)
    temporal_lookup_share = jnp.clip(jax.random.uniform(seeds[4], (EMBED_WIDTH,), jnp.float32, 0.0, 1.0), 0.0, 1.0)
    temporal_payload_share = jnp.clip(jax.random.uniform(seeds[5], (EMBED_WIDTH,), jnp.float32, 0.0, 1.0), 0.0, 1.0)
    temporal_gate_share = jnp.clip(jax.random.uniform(seeds[6], (EMBED_WIDTH,), jnp.float32, 0.0, 1.0), 0.0, 1.0)
    fading_log_rates = draw_fading_log_rates(jax.random.fold_in(seeds[21], 71), 0)
    present_reward_vector = jnp.clip(jax.random.uniform(seeds[8], (EMBED_WIDTH,), jnp.float32, -1.0, 1.0), -1.0, 1.0)
    lookup_matrix = scatter_about(seeds[9], (EMBED_WIDTH, EMBED_WIDTH), EMBED_WIDTH ** -0.5, 0.1875)
    payload_matrix = scatter_about(seeds[10], (EMBED_WIDTH, EMBED_WIDTH), EMBED_WIDTH ** -0.5, 0.1875)
    gate_matrix = scatter_about(seeds[11], (EMBED_WIDTH, EMBED_WIDTH), EMBED_WIDTH ** -0.5, 0.1875)
    emission_matrix = scatter_about(seeds[12], (EMBED_WIDTH, EMBED_WIDTH), (EMBED_WIDTH // 64) ** -0.5, 1.5)
    channel_norm_scale = jnp.clip(1.0 + 0.18 * jax.random.normal(seeds[13], (EMBED_WIDTH,), jnp.float32), 0.1, 1.9)
    channel_norm_offset = scatter_about(seeds[14], (EMBED_WIDTH,), 0.3, 2.0, (), jnp.float32)
    channel_lookup_share = jnp.clip(jax.random.uniform(seeds[15], (EMBED_WIDTH,), jnp.float32, 0.0, 1.0), 0.0, 1.0)
    channel_gate_share = jnp.clip(jax.random.uniform(seeds[16], (EMBED_WIDTH,), jnp.float32, 0.0, 1.0), 0.0, 1.0)
    channel_lookup_matrix = scatter_about(seeds[17], (EMBED_WIDTH, FF), EMBED_WIDTH ** -0.5, 0.1875)
    channel_payload_matrix = scatter_about(seeds[18], (FF, EMBED_WIDTH), FF ** -0.5, 0.09375)
    channel_gate_matrix = scatter_about(seeds[19], (EMBED_WIDTH, EMBED_WIDTH), EMBED_WIDTH ** -0.5, 0.1875)
    final_cotangent = scatter_about(seeds[20], (PACKED_LINES, SEQLEN, EMBED_WIDTH), 1.0, 6.0, ((0, 4), (1, 8)))
    return dict(incoming_symbols=incoming_symbols, article_sizes=article_sizes, mixer_norm_scale=mixer_norm_scale, mixer_norm_offset=mixer_norm_offset, temporal_lookup_share=temporal_lookup_share, temporal_payload_share=temporal_payload_share, temporal_gate_share=temporal_gate_share, fading_log_rates=fading_log_rates, present_reward_vector=present_reward_vector, lookup_matrix=lookup_matrix, payload_matrix=payload_matrix, gate_matrix=gate_matrix, emission_matrix=emission_matrix, channel_norm_scale=channel_norm_scale, channel_norm_offset=channel_norm_offset, channel_lookup_share=channel_lookup_share, channel_gate_share=channel_gate_share, channel_lookup_matrix=channel_lookup_matrix, channel_payload_matrix=channel_payload_matrix, channel_gate_matrix=channel_gate_matrix, final_cotangent=final_cotangent)


@jax.custom_vjp
def low(v):
    return lax.optimization_barrier(v.astype(jnp.bfloat16)).astype(jnp.float32)

@jax.custom_vjp
def low_back(v):
    return v

def low_keep(v):
    return (low(v), None)

def low_pass(kept, grad):
    return (grad,)

def back_keep(v):
    return (v, None)

def back_low(kept, grad):
    return (low(grad),)
low.defvjp(low_keep, low_pass)
low_back.defvjp(back_keep, back_low)

def matmul(left_side, right_side):
    return jnp.einsum('rtd,de->rte', left_side, right_side, precision=lax.Precision.HIGHEST)

def norm_rows(value_rows, gain_vec, bias_vec):
    row_mean = lax.optimization_barrier(jnp.mean(value_rows, axis=-1, keepdims=True))
    centred = value_rows - row_mean
    variance = lax.optimization_barrier(jnp.mean(centred * centred, axis=-1, keepdims=True))
    return centred * lax.rsqrt(variance + 1e-05) * gain_vec + bias_vec

def shifted(value_rows, retain_flags):
    earlier = jnp.concatenate([jnp.zeros_like(value_rows[:, :1]), value_rows[:, :-1]], axis=1)
    return earlier * retain_flags[:, :, None]

def one_token(accumulated_pair, token_item):
    upper_sum_carried, lower_sum_carried, fading_multiplier, reward_summand = accumulated_pair
    lookup_this_moment, payload_this_moment, keep_t = token_item
    upper_sum_carried = upper_sum_carried * keep_t
    lower_sum_carried = lower_sum_carried * keep_t
    reward_power_arg = jnp.exp(reward_summand + lookup_this_moment)
    sublevel_product = (upper_sum_carried + reward_power_arg * payload_this_moment) / (lower_sum_carried + reward_power_arg)
    power_lookup_arg = jnp.exp(lookup_this_moment)
    upper_sum_carried = fading_multiplier * upper_sum_carried + power_lookup_arg * payload_this_moment
    lower_sum_carried = fading_multiplier * lower_sum_carried + power_lookup_arg
    return ((upper_sum_carried, lower_sum_carried, fading_multiplier, reward_summand), sublevel_product)

def block_weighted_value(accumulated_pair, block_data):
    return lax.scan(one_token, accumulated_pair, block_data)

def attention_mixture_full(lookup_mapped, payload_mapped, retain_flags, fading_multiplier, reward_summand):

    def split_into_blocks(value_rows):
        return jnp.transpose(value_rows, (1, 0, 2)).reshape(N_SEQ, TOK_DEV, value_rows.shape[0], value_rows.shape[2])
    block_keep_factors = jnp.transpose(retain_flags)[:, :, None].reshape(N_SEQ, TOK_DEV, PACKED_LINES, 1)
    initial_memory = (jnp.zeros((PACKED_LINES, EMBED_WIDTH), jnp.float32), jnp.zeros((PACKED_LINES, EMBED_WIDTH), jnp.float32), fading_multiplier, reward_summand)
    closing_state, output_rows = lax.scan(jax.checkpoint(block_weighted_value), initial_memory, (split_into_blocks(lookup_mapped), split_into_blocks(payload_mapped), block_keep_factors))
    return jnp.transpose(output_rows.reshape(SEQLEN, PACKED_LINES, EMBED_WIDTH), (1, 0, 2))

def evaluate_ahead(retain_flags, symbol_entries, mixer_norm_scale, mixer_norm_offset, temporal_lookup_share, temporal_payload_share, temporal_gate_share, fading_log_rates, present_reward_vector, lookup_matrix, payload_matrix, gate_matrix, emission_matrix, channel_norm_scale, channel_norm_offset, channel_lookup_share, channel_gate_share, channel_lookup_matrix, channel_payload_matrix, channel_gate_matrix):
    att_normed = norm_rows(symbol_entries, mixer_norm_scale, mixer_norm_offset)
    att_prev = shifted(att_normed, retain_flags)
    key_mixed = low(att_normed * temporal_lookup_share + att_prev * (1.0 - temporal_lookup_share))
    value_mixed = low(att_normed * temporal_payload_share + att_prev * (1.0 - temporal_payload_share))
    recep_mixed = low(att_normed * temporal_gate_share + att_prev * (1.0 - temporal_gate_share))
    lookup_mapped = low_back(matmul(key_mixed, lookup_matrix))
    payload_mapped = low_back(matmul(value_mixed, payload_matrix))
    recep_proj = low_back(matmul(recep_mixed, gate_matrix))
    fading_multiplier = jnp.exp(-jnp.exp(fading_log_rates))
    scaled_lookup_payload = attention_mixture_full(lookup_mapped, payload_mapped, retain_flags, fading_multiplier, present_reward_vector)
    gated = low(jax.nn.sigmoid(recep_proj) * scaled_lookup_payload)
    after_att = symbol_entries + low_back(matmul(gated, emission_matrix))
    ffn_normed = norm_rows(after_att, channel_norm_scale, channel_norm_offset)
    ffn_prev = shifted(ffn_normed, retain_flags)
    ffn_key_mixed = low(ffn_normed * channel_lookup_share + ffn_prev * (1.0 - channel_lookup_share))
    ffn_recep_mixed = low(ffn_normed * channel_gate_share + ffn_prev * (1.0 - channel_gate_share))
    hidden_pre = low_back(matmul(ffn_key_mixed, channel_lookup_matrix))
    squared = low(jnp.square(jax.nn.relu(hidden_pre)))
    ffn_value = low_back(matmul(squared, channel_payload_matrix))
    ffn_gate = jax.nn.sigmoid(low_back(matmul(ffn_recep_mixed, channel_gate_matrix)))
    return after_att + ffn_gate * ffn_value

def reference(incoming_symbols, article_sizes, mixer_norm_scale, mixer_norm_offset, temporal_lookup_share, temporal_payload_share, temporal_gate_share, fading_log_rates, present_reward_vector, lookup_matrix, payload_matrix, gate_matrix, emission_matrix, channel_norm_scale, channel_norm_offset, channel_lookup_share, channel_gate_share, channel_lookup_matrix, channel_payload_matrix, channel_gate_matrix, final_cotangent):
    doc_ends = jnp.cumsum(article_sizes, axis=1).astype(jnp.int32)
    begins = (doc_ends - article_sizes).astype(jnp.int32)
    position = jnp.arange(SEQLEN, dtype=jnp.int32)
    hit_table = position[None, :, None] == begins[:, None, :]
    retain_flags = jnp.where(jnp.any(hit_table, axis=2), 0.0, 1.0).astype(jnp.float32)
    forward_arguments = (incoming_symbols.astype(jnp.float32), mixer_norm_scale, mixer_norm_offset, temporal_lookup_share, temporal_payload_share, temporal_gate_share, fading_log_rates, present_reward_vector, lookup_matrix.astype(jnp.float32), payload_matrix.astype(jnp.float32), gate_matrix.astype(jnp.float32), emission_matrix.astype(jnp.float32), channel_norm_scale, channel_norm_offset, channel_lookup_share, channel_gate_share, channel_lookup_matrix.astype(jnp.float32), channel_payload_matrix.astype(jnp.float32), channel_gate_matrix.astype(jnp.float32))
    layer_out, pullback = jax.vjp(partial(evaluate_ahead, retain_flags), *forward_arguments)
    gradients = pullback(final_cotangent.astype(jnp.float32))
    return (layer_out.astype(jnp.bfloat16), gradients[0].astype(jnp.bfloat16), gradients[1], gradients[2], gradients[3], gradients[4], gradients[5], gradients[6], gradients[7], gradients[8], gradients[9], gradients[10], gradients[11], gradients[12], gradients[13], gradients[14], gradients[15], gradients[16], gradients[17], gradients[18])
```

```python
import functools
import math

import jax
import jax.numpy as jnp
from jax import lax
from jax.experimental import pallas as pl
from jax.experimental.pallas import tpu as pltpu
from jax.sharding import PartitionSpec as P

F32, BF16 = jnp.float32, jnp.bfloat16
STEPS = 8


def shifted(value, axis, distance):
    devices = range(lax.axis_size(axis))
    route = [(i - distance, i) for i in devices if i - distance in devices]
    return lax.ppermute(value, axis, route)


def bit_value(bit):
    axis, place = bit
    return (lax.axis_index(axis) >> place) & 1


def exchange(value, bit):
    axis, place = bit
    return lax.ppermute(value, axis, [(i, i ^ (1 << place)) for i in range(lax.axis_size(axis))])


def pick(value, index, dim):
    return lax.dynamic_index_in_dim(value, index, dim, keepdims=False)


def total_of(terms):
    return functools.reduce(lambda a, b: a + b, terms)


def axis_bits(axis):
    return [(axis, k) for k in range(int(math.log2(lax.axis_size(axis))))]


class Partial:
    def __init__(self, terms):
        self.dims = axis_bits("seq")[::-1] + axis_bits("batch")[1:]
        lead = (2,) * len(self.dims)
        self.terms = [t.reshape(*lead, -1, t.shape[-1]) for t in terms]

    def halve(self, bit):
        dim, mine = self.dims.index(bit), bit_value(bit)
        send = total_of([pick(t, 1 - mine, dim) for t in self.terms])
        got = exchange(send, bit)
        self.terms = [pick(t, mine, dim) for t in self.terms] + [got]
        self.dims.pop(dim)

    def gather(self):
        value = total_of(self.terms)
        for bit in axis_bits("batch")[:0:-1]:
            other = exchange(value, bit)
            first = bit_value(bit) == 0
            value = jnp.concatenate(
                [jnp.where(first, value, other), jnp.where(first, other, value)], axis=0
            )
        bit = ("batch", 0)
        other = exchange(value, bit)
        first = bit_value(bit) == 0
        return jnp.concatenate(
            [jnp.where(first, value, other), jnp.where(first, other, value)], axis=1
        )


def weight_grad(left_t, right):
    bit = ("batch", 0)
    half = right.shape[1] // 2
    mine = bit_value(bit)
    dot = lambda cols: lax.dot_general(
        left_t, cols, (((0,), (0,)), ((), ())), preferred_element_type=F32
    )
    theirs = dot(lax.dynamic_slice_in_dim(right, (1 - mine) * half, half, 1))
    got = exchange(theirs, bit)
    own = dot(lax.dynamic_slice_in_dim(right, mine * half, half, 1))
    return Partial([own, got])


def reduce_vectors(vectors):
    count, seq = vectors.shape[0], lax.axis_size("seq")
    bits = axis_bits("seq")
    value = jnp.swapaxes(vectors.reshape(count, seq, -1), 0, 1)
    value = value.reshape(*((2,) * len(bits)), count, -1)
    for bit in axis_bits("batch"):
        value = value + exchange(value, bit)
    for bit in bits[::-1]:
        mine = bit_value(bit)
        value = pick(value, mine, 0) + exchange(pick(value, 1 - mine, 0), bit)
    return value


def entering(tails, begins, decay_rate, group_len, backward):
    count, mine = lax.axis_size("seq"), lax.axis_index("seq")
    sign = -1 if backward else 1

    def gain(lo, hi):
        a, b = (mine + lo, mine + hi) if backward else (mine - hi + 1, mine - lo + 1)
        hit = jnp.any((begins >= a * group_len) & (begins < b * group_len), axis=1, keepdims=True)
        return jnp.where(hit, 0.0, 1.0) * jnp.exp(-float((hi - lo) * group_len) * decay_rate)[None, :]

    reach, window, before = 1, tails, None
    while reach < count:
        got = [
            (j, shifted(window, "seq", sign * j * reach)) for j in range(1, 4) if j * reach < count
        ]
        if before is None:
            before = total_of([v if j == 1 else gain(1, j) * v for j, v in got])
            seen = 1 + len(got)
            window = tails + gain(0, 1) * before if seen < count else None
        else:
            before_more = total_of([gain(1, j * reach) * v for j, v in got])
            seen = reach * (1 + len(got))
            if seen < count:
                window = window + total_of([gain(0, j * reach) * v for j, v in got])
            before = before + before_more
        reach *= 4
    return before


def scan_params():
    return pltpu.CompilerParams(vmem_limit_bytes=48 * 1024 * 1024)


def at_step(ref, row, step, length, lanes):
    return ref[row, pl.ds(step, STEPS, stride=length // STEPS), lanes]


def lane_tiles(width):
    return [slice(i, i + 128) for i in range(0, width, 128)]


def join_pieces(tails, gains, order):
    total = None
    for c in order:
        part = tails[c : c + 1]
        total = part if total is None else gains[c : c + 1] * total + part
    return total


def forward_tails_kernel(k_ref, v_ref, keep_ref, rate_ref, piece_ref, tail_ref):
    rows, length, width = k_ref.shape
    steps = length // STEPS
    tiles = lane_tiles(width)
    chains = [(r, t) for r in range(rows) for t in tiles]
    decay = [jnp.exp(-rate_ref[0:1, t]) for t in tiles]

    def step(j, carry):
        out = []
        flags = [keep_ref[r, pl.ds(j, STEPS, stride=steps), :] for r in range(rows)]
        for i, (r, t) in enumerate(chains):
            num, den, alive = carry[i]
            e = jnp.exp(at_step(k_ref, r, j, length, t))
            v = at_step(v_ref, r, j, length, t)
            f = flags[r] * decay[i % len(tiles)]
            out.append((f * num + e * v, f * den + e, alive * flags[r]))
        return tuple(out)

    zero = jnp.zeros((STEPS, 128), F32)
    done = lax.fori_loop(
        0, steps, step, tuple((zero, zero, jnp.ones((STEPS, 128), F32)) for _ in chains), unroll=4
    )
    for (r, t), (num, den, alive) in zip(chains, done):
        gains = alive * jnp.exp(-float(steps) * rate_ref[0:1, t])
        piece_ref[0, r, :, t] = num
        piece_ref[1, r, :, t] = den
        piece_ref[2, r, :, t] = gains
        tail_ref[0, r : r + 1, t] = join_pieces(num, gains, range(STEPS))
        tail_ref[1, r : r + 1, t] = join_pieces(den, gains, range(STEPS))


def forward_states_kernel(
    k_ref, v_ref, recep_ref, keep_ref, rate_ref, bonus_ref, piece_ref, enter_ref,
    num_ref, den_ref, gated_ref,
):
    rows, length, width = k_ref.shape
    steps = length // STEPS
    tiles = lane_tiles(width)
    chains = [(r, t) for r in range(rows) for t in tiles]
    decay = [jnp.exp(-rate_ref[0:1, t]) for t in tiles]
    carry = []
    for r, t in chains:
        gains = piece_ref[2, r, :, t]
        start = []
        for q in range(2):
            tails, held, parts = piece_ref[q, r, :, t], enter_ref[q, r : r + 1, t], []
            for c in range(STEPS):
                parts.append(held)
                held = gains[c : c + 1] * held + tails[c : c + 1]
            start.append(jnp.concatenate(parts, axis=0))
        carry.append(tuple(start))

    def step(j, carry):
        out = []
        flags = [keep_ref[r, pl.ds(j, STEPS, stride=steps), :] for r in range(rows)]
        for i, (r, t) in enumerate(chains):
            num, den = carry[i]
            num, den = num * flags[r], den * flags[r]
            num_ref[r, pl.ds(j, STEPS, stride=steps), t] = num
            den_ref[r, pl.ds(j, STEPS, stride=steps), t] = den
            e = jnp.exp(at_step(k_ref, r, j, length, t))
            v = at_step(v_ref, r, j, length, t)
            d = decay[i % len(tiles)]
            out.append((d * num + e * v, d * den + e))
        return tuple(out)

    lax.fori_loop(0, steps, step, tuple(carry), unroll=4)
    bonus = bonus_ref[0:1, :]

    def finish(b, _):
        for r in range(rows):
            at = pl.ds(pl.multiple_of(b * 16, 16), 16)
            first = jnp.exp(bonus + k_ref[r, at, :])
            wkv = (num_ref[r, at, :] + first * v_ref[r, at, :]) / (den_ref[r, at, :] + first)
            gated_ref[r, at, :] = (jax.nn.sigmoid(recep_ref[r, at, :]) * wkv).astype(BF16)
        return 0

    lax.fori_loop(0, length // 16, finish, 0)


def backward_tails_kernel(
    grad_ref, k_ref, v_ref, recep_ref, num_ref, den_ref, keep_ref, rate_ref, bonus_ref,
    gnum_ref, gden_ref, grecep_ref, piece_ref, tail_ref,
):
    rows, length, width = k_ref.shape
    steps = length // STEPS
    tiles = lane_tiles(width)
    bonus = bonus_ref[0:1, :]

    def begin(b, _):
        for r in range(rows):
            at = pl.ds(pl.multiple_of(b * 16, 16), 16)
            first = jnp.exp(bonus + k_ref[r, at, :])
            below = den_ref[r, at, :] + first
            wkv = (num_ref[r, at, :] + first * v_ref[r, at, :]) / below
            gate = jax.nn.sigmoid(recep_ref[r, at, :])
            grad = grad_ref[r, at, :]
            grecep_ref[r, at, :] = (grad * wkv * (gate * (1.0 - gate))).astype(BF16)
            up = grad * gate / below
            gnum_ref[r, at, :] = up
            gden_ref[r, at, :] = -up * wkv
        return 0

    lax.fori_loop(0, length // 16, begin, 0)
    chains = [(r, t) for r in range(rows) for t in tiles]
    decay = [jnp.exp(-rate_ref[0:1, t]) for t in tiles]

    def step(i_step, carry):
        j = steps - 1 - i_step
        out = []
        flags = [keep_ref[r, pl.ds(j, STEPS, stride=steps), :] for r in range(rows)]
        for i, (r, t) in enumerate(chains):
            num, den, alive = carry[i]
            d = decay[i % len(tiles)]
            out.append(
                (
                    flags[r] * (at_step(gnum_ref, r, j, length, t) + d * num),
                    flags[r] * (at_step(gden_ref, r, j, length, t) + d * den),
                    alive * flags[r],
                )
            )
        return tuple(out)

    zero = jnp.zeros((STEPS, 128), F32)
    done = lax.fori_loop(
        0, steps, step, tuple((zero, zero, jnp.ones((STEPS, 128), F32)) for _ in chains), unroll=4
    )
    for (r, t), (num, den, alive) in zip(chains, done):
        gains = alive * jnp.exp(-float(steps) * rate_ref[0:1, t])
        piece_ref[0, r, :, t] = num
        piece_ref[1, r, :, t] = den
        piece_ref[2, r, :, t] = gains
        tail_ref[0, r : r + 1, t] = join_pieces(num, gains, range(STEPS)[::-1])
        tail_ref[1, r : r + 1, t] = join_pieces(den, gains, range(STEPS)[::-1])


def backward_states_kernel(
    gnum_ref, gden_ref, k_ref, v_ref, num_ref, den_ref, keep_ref, rate_ref, bonus_ref, piece_ref,
    enter_ref, gkey_ref, gvalue_ref, sums_ref, snum_ref, sden_ref,
):
    rows, length, width = k_ref.shape
    steps = length // STEPS
    tiles = lane_tiles(width)
    chains = [(r, t) for r in range(rows) for t in tiles]
    decay = [jnp.exp(-rate_ref[0:1, t]) for t in tiles]
    carry = []
    for r, t in chains:
        gains = piece_ref[2, r, :, t]
        start = []
        for q in range(2):
            tails, held, parts = piece_ref[q, r, :, t], enter_ref[q, r : r + 1, t], []
            for c in range(STEPS)[::-1]:
                parts.append(held)
                held = gains[c : c + 1] * held + tails[c : c + 1]
            start.append(jnp.concatenate(parts[::-1], axis=0))
        carry.append(tuple(start))

    def step(i_step, carry):
        j = steps - 1 - i_step
        out = []
        flags = [keep_ref[r, pl.ds(j, STEPS, stride=steps), :] for r in range(rows)]
        for i, (r, t) in enumerate(chains):
            num, den = carry[i]
            snum_ref[r, pl.ds(j, STEPS, stride=steps), t] = num
            sden_ref[r, pl.ds(j, STEPS, stride=steps), t] = den
            d = decay[i % len(tiles)]
            out.append(
                (
                    flags[r] * (at_step(gnum_ref, r, j, length, t) + d * num),
                    flags[r] * (at_step(gden_ref, r, j, length, t) + d * den),
                )
            )
        return tuple(out)

    lax.fori_loop(0, steps, step, tuple(carry), unroll=4)
    bonus = bonus_ref[0:1, :]

    def finish(b, sums):
        slope, fade = sums
        for r in range(rows):
            at = pl.ds(pl.multiple_of(b * 16, 16), 16)
            key, value = k_ref[r, at, :], v_ref[r, at, :]
            e, first = jnp.exp(key), jnp.exp(bonus + key)
            up, low = gnum_ref[r, at, :], gden_ref[r, at, :]
            later_num, later_den = snum_ref[r, at, :], sden_ref[r, at, :]
            present = first * (up * value + low)
            gvalue_ref[r, at, :] = (up * first + later_num * e).astype(BF16)
            gkey_ref[r, at, :] = (present + e * (later_num * value + later_den)).astype(BF16)
            slope = slope + present[:8] + present[8:]
            both = num_ref[r, at, :] * later_num + den_ref[r, at, :] * later_den
            fade = fade + both[:8] + both[8:]
        return slope, fade

    zero = jnp.zeros((8, width), F32)
    slope, fade = lax.fori_loop(0, length // 16, finish, (zero, zero))
    sums_ref[0:8, :] = slope
    sums_ref[8:16, :] = fade


def scan_call(kernel, inputs, outputs, scratch=(), width=128):
    features = inputs[0].shape[-1]

    def spec(shape):
        lead = len(shape) - 1
        if shape[-1] == 128 and features != 128:
            return pl.BlockSpec(shape, lambda i: (0,) * (lead + 1))
        return pl.BlockSpec((*shape[:-1], width), lambda i: (0,) * lead + (i,))

    out_shape = [jax.ShapeDtypeStruct(s, d) for s, d in outputs]
    moved = sum(x.size * x.dtype.itemsize for x in [*inputs, *out_shape])
    return pl.pallas_call(
        kernel,
        out_shape=out_shape,
        grid=(features // width,),
        in_specs=[spec(x.shape) for x in inputs],
        out_specs=[spec(s) for s, _ in outputs],
        scratch_shapes=[pltpu.VMEM((*s[:-1], width), F32) for s in scratch],
        compiler_params=scan_params(),
        cost_estimate=pl.CostEstimate(
            flops=20 * inputs[0].size, bytes_accessed=moved, transcendentals=inputs[0].size
        ),
    )(*inputs)


def norm_rows(value_rows, gain_vec, bias_vec):
    row_mean = jnp.mean(value_rows, axis=-1, keepdims=True)
    centred = value_rows - row_mean
    inv_std = lax.rsqrt(jnp.mean(centred * centred, axis=-1, keepdims=True) + 1e-05)
    normed = centred * inv_std
    return (normed * gain_vec + bias_vec, normed, inv_std)


def norm_back(grad_in, normed, inv_std, gain_vec):
    scaled = grad_in * gain_vec
    return inv_std * (
        scaled
        - jnp.mean(scaled, axis=-1, keepdims=True)
        - normed * jnp.mean(scaled * normed, axis=-1, keepdims=True)
    )


def project(left_side, right_side):
    return jnp.einsum("rcd,de->rce", left_side, right_side, preferred_element_type=F32)


def project_back(grad_in, right_side):
    return jnp.einsum("rce,de->rcd", grad_in, right_side, preferred_element_type=F32)


def with_previous(value_rows, edge_row, keep):
    earlier = jnp.concatenate([edge_row[:, None, :], value_rows[:, :-1, :]], axis=1)
    return earlier * keep[:, :, None]


def flat(value):
    return value.reshape(-1, value.shape[-1])


def shards(
    incoming_symbols,
    article_sizes,
    mixer_norm_scale,
    mixer_norm_offset,
    temporal_lookup_share,
    temporal_payload_share,
    temporal_gate_share,
    fading_log_rates,
    present_reward_vector,
    lookup_matrix,
    payload_matrix,
    gate_matrix,
    emission_matrix,
    channel_norm_scale,
    channel_norm_offset,
    channel_lookup_share,
    channel_gate_share,
    channel_lookup_matrix,
    channel_payload_matrix,
    channel_gate_matrix,
    final_cotangent,
):
    rows_here, group_len, features = incoming_symbols.shape
    full = (rows_here, group_len, features)
    begins = jnp.cumsum(article_sizes, axis=1) - article_sizes
    position = lax.axis_index("seq") * group_len + jnp.arange(group_len, dtype=jnp.int32)
    starts = jnp.any(position[None, :, None] == begins[:, None, :], axis=2)
    keep = jnp.where(starts, 0.0, 1.0).astype(F32)
    keep_wide = jnp.broadcast_to(keep[:, :, None], (rows_here, group_len, 128))
    decay_rate = jnp.exp(fading_log_rates)
    rate_row = jnp.broadcast_to(decay_rate[None, :], (8, features))
    bonus_row = jnp.broadcast_to(present_reward_vector[None, :], (8, features))
    enter = functools.partial(entering, begins=begins, decay_rate=decay_rate, group_len=group_len)

    symbols = incoming_symbols.astype(F32)
    att_last = norm_rows(symbols[:, -1, :], mixer_norm_scale, mixer_norm_offset)[0]
    att_edge = shifted(att_last, "seq", 1)
    att_normed, att_unit, att_inv = norm_rows(symbols, mixer_norm_scale, mixer_norm_offset)
    att_prev = with_previous(att_normed, att_edge, keep)
    mix = lambda share: (att_normed * share + att_prev * (1.0 - share)).astype(BF16)
    key_mixed = mix(temporal_lookup_share)
    value_mixed = mix(temporal_payload_share)
    recep_mixed = mix(temporal_gate_share)
    key_proj = project(key_mixed, lookup_matrix)
    value_proj = project(value_mixed, payload_matrix)
    recep_proj = project(recep_mixed, gate_matrix)
    pieces = ((3, rows_here, STEPS, features), F32)
    tails = ((2, rows_here, features), F32)
    piece, tail = scan_call(
        forward_tails_kernel, [key_proj, value_proj, keep_wide, rate_row], [pieces, tails]
    )
    num_state, den_state, gated = scan_call(
        forward_states_kernel,
        [key_proj, value_proj, recep_proj, keep_wide, rate_row, bonus_row, piece, enter(tail, backward=False)],
        [(full, F32), (full, F32), (full, BF16)],
    )
    after_att = symbols + project(gated, emission_matrix)

    ffn_normed, ffn_unit, ffn_inv = norm_rows(after_att, channel_norm_scale, channel_norm_offset)
    ffn_edge = shifted(ffn_normed[:, -1, :], "seq", 1)
    ffn_prev = with_previous(ffn_normed, ffn_edge, keep)
    ffn_key_mixed = (
        ffn_normed * channel_lookup_share + ffn_prev * (1.0 - channel_lookup_share)
    ).astype(BF16)
    ffn_recep_mixed = (
        ffn_normed * channel_gate_share + ffn_prev * (1.0 - channel_gate_share)
    ).astype(BF16)
    hidden_pre = project(ffn_key_mixed, channel_lookup_matrix)
    above = jnp.maximum(hidden_pre, 0.0)
    squared = jnp.square(above).astype(BF16)
    ffn_gate = jax.nn.sigmoid(project(ffn_recep_mixed, channel_gate_matrix))
    ffn_value = project(squared, channel_payload_matrix)
    layer_out = (after_att + ffn_gate * ffn_value).astype(BF16)

    grad_top = final_cotangent.astype(F32)
    grad_fvalue = (grad_top * ffn_gate).astype(BF16)
    grad_frecep = (grad_top * ffn_value * (ffn_gate * (1.0 - ffn_gate))).astype(BF16)
    hidden = hidden_pre.shape[-1]
    value_parts = [
        weight_grad(flat(squared), flat(grad_fvalue)[:, i * features // 2 : (i + 1) * features // 2])
        for i in range(2)
    ]
    grad_squared = project_back(grad_fvalue, channel_payload_matrix)
    grad_hidden = (grad_squared * (2.0 * above)).astype(BF16)
    key_parts = [
        weight_grad(flat(ffn_key_mixed), flat(grad_hidden)[:, i * hidden // 2 : (i + 1) * hidden // 2])
        for i in range(2)
    ]
    frecep_part = weight_grad(flat(ffn_recep_mixed), flat(grad_frecep))
    grad_fkey_in = project_back(grad_hidden, channel_lookup_matrix)
    grad_frecep_in = project_back(grad_frecep, channel_gate_matrix)
    ffn_delta = ffn_normed - ffn_prev
    grad_ffn_mix_key = jnp.sum(grad_fkey_in * ffn_delta, axis=(0, 1))
    grad_ffn_mix_recep = jnp.sum(grad_frecep_in * ffn_delta, axis=(0, 1))
    grad_ffn_prev = (
        grad_fkey_in * (1.0 - channel_lookup_share) + grad_frecep_in * (1.0 - channel_gate_share)
    ) * keep[:, :, None]
    ffn_back_edge = shifted(grad_ffn_prev[:, 0, :], "seq", -1)
    grad_ffn_normed = (
        grad_fkey_in * channel_lookup_share
        + grad_frecep_in * channel_gate_share
        + jnp.concatenate([grad_ffn_prev[:, 1:, :], ffn_back_edge[:, None, :]], axis=1)
    )
    grad_ffn_ln_gain = jnp.sum(grad_ffn_normed * ffn_unit, axis=(0, 1))
    grad_ffn_ln_bias = jnp.sum(grad_ffn_normed, axis=(0, 1))
    grad_after = grad_top + norm_back(grad_ffn_normed, ffn_unit, ffn_inv, channel_norm_scale)

    grad_att_out = grad_after.astype(BF16)
    output_part = weight_grad(flat(gated), flat(grad_att_out))
    grad_gated = project_back(grad_att_out, emission_matrix)
    grad_num, grad_den, grad_recep, piece, tail = scan_call(
        backward_tails_kernel,
        [grad_gated, key_proj, value_proj, recep_proj, num_state, den_state, keep_wide, rate_row, bonus_row],
        [(full, F32), (full, F32), (full, BF16), pieces, tails],
    )
    grad_key, grad_value, sums = scan_call(
        backward_states_kernel,
        [grad_num, grad_den, key_proj, value_proj, num_state, den_state, keep_wide, rate_row, bonus_row, piece, enter(tail, backward=True)],
        [(full, BF16), (full, BF16), ((16, features), F32)],
        scratch=(full, full),
    )
    reward_slope = jnp.sum(sums[:8], axis=0)
    grad_time_decay = -decay_rate * jnp.exp(-decay_rate) * jnp.sum(sums[8:], axis=0)
    att_parts = [
        weight_grad(flat(recep_mixed), flat(grad_recep)),
        weight_grad(flat(key_mixed), flat(grad_key)),
        weight_grad(flat(value_mixed), flat(grad_value)),
    ]
    grad_key_in = project_back(grad_key, lookup_matrix)
    grad_value_in = project_back(grad_value, payload_matrix)
    grad_recep_in = project_back(grad_recep, gate_matrix)
    att_delta = att_normed - att_prev
    grad_mix_key = jnp.sum(grad_key_in * att_delta, axis=(0, 1))
    grad_mix_value = jnp.sum(grad_value_in * att_delta, axis=(0, 1))
    grad_mix_recep = jnp.sum(grad_recep_in * att_delta, axis=(0, 1))
    grad_att_prev = (
        grad_key_in * (1.0 - temporal_lookup_share)
        + grad_value_in * (1.0 - temporal_payload_share)
        + grad_recep_in * (1.0 - temporal_gate_share)
    ) * keep[:, :, None]
    att_back_edge = shifted(grad_att_prev[:, 0, :], "seq", -1)
    grad_att_normed = (
        grad_key_in * temporal_lookup_share
        + grad_value_in * temporal_payload_share
        + grad_recep_in * temporal_gate_share
        + jnp.concatenate([grad_att_prev[:, 1:, :], att_back_edge[:, None, :]], axis=1)
    )
    grad_att_ln_gain = jnp.sum(grad_att_normed * att_unit, axis=(0, 1))
    grad_att_ln_bias = jnp.sum(grad_att_normed, axis=(0, 1))
    grad_tokens = (
        grad_after + norm_back(grad_att_normed, att_unit, att_inv, mixer_norm_scale)
    ).astype(BF16)

    seq_bits, batch_bits = axis_bits("seq"), axis_bits("batch")[1:]
    plane_a = batch_bits + seq_bits
    plane_b = seq_bits[:1] + batch_bits + seq_bits[1:]
    far = seq_bits[1:] + batch_bits + seq_bits[:1]
    jobs = [
        (value_parts[0], plane_a),
        (value_parts[1], plane_b),
        (key_parts[0], plane_a),
        (key_parts[1], plane_b),
        (frecep_part, far),
        (output_part, far),
        (att_parts[0], plane_a),
        (att_parts[1], plane_b),
        (att_parts[2], plane_a),
    ]
    for part, order in jobs:
        for bit in order:
            part.halve(bit)
    done = [part.gather() for part, _ in jobs]
    vectors = jnp.stack(
        [
            grad_att_ln_gain,
            grad_att_ln_bias,
            grad_mix_key,
            grad_mix_value,
            grad_mix_recep,
            grad_time_decay,
            reward_slope,
            grad_ffn_ln_gain,
            grad_ffn_ln_bias,
            grad_ffn_mix_key,
            grad_ffn_mix_recep,
        ]
    )
    small = reduce_vectors(vectors)
    return (
        layer_out,
        grad_tokens,
        *[small[i] for i in range(7)],
        done[7],
        done[8],
        done[6],
        done[5],
        *[small[i] for i in range(7, 11)],
        jnp.concatenate(done[2:4], axis=1),
        jnp.concatenate(done[0:2], axis=1),
        done[4],
    )


def solution(mesh):
    tokens = P("batch", "seq", None)
    vector, matrix = P("seq"), P("seq", None)
    return jax.shard_map(
        shards,
        mesh=mesh,
        in_specs=(tokens, P("batch", None), *([P()] * 18), tokens),
        out_specs=(tokens, tokens, *([vector] * 7), *([matrix] * 4), *([vector] * 4), *([matrix] * 3)),
        check_vma=False,
    )
```

```python
import functools
import math

import jax
import jax.numpy as jnp
from jax import lax
from jax.experimental import pallas as pl
from jax.experimental.pallas import tpu as pltpu
from jax.sharding import PartitionSpec as P

F32, BF16 = jnp.float32, jnp.bfloat16
CHUNK = 64
STEPS = 8


def shifted(value, axis, distance):
    devices = range(lax.axis_size(axis))
    route = [(i - distance, i) for i in devices if i - distance in devices]
    return lax.ppermute(value, axis, route)


def bit_value(bit):
    axis, place = bit
    return (lax.axis_index(axis) >> place) & 1


def exchange(value, bit):
    axis, place = bit
    return lax.ppermute(value, axis, [(i, i ^ (1 << place)) for i in range(lax.axis_size(axis))])


def pick(value, index, dim):
    return lax.dynamic_index_in_dim(value, index, dim, keepdims=False)


def total_of(terms):
    return functools.reduce(lambda a, b: a + b, terms)


def axis_bits(axis):
    return [(axis, k) for k in range(int(math.log2(lax.axis_size(axis))))]


def at_once(ready, step, *values):
    blank = lambda *v: jax.tree.map(
        lambda x: jnp.zeros(x.shape, x.dtype), jax.eval_shape(step, *v)
    )
    return lax.cond(ready, step, blank, *values)


class Line:
    def __init__(self):
        self.token = None

    def gate(self, value):
        if self.token is None:
            return value
        return lax.optimization_barrier((value, self.token))[0]

    def mark(self, value, *others):
        self.token = (value, *others)
        return value


CORE = ("batch", 0)


def send_half(value):
    half = value.shape[1] // 2
    theirs = lax.dynamic_slice_in_dim(value, (1 - bit_value(CORE)) * half, half, 1)
    return exchange(theirs.astype(F32), CORE)


def send_half_of(values):
    half = values[0].shape[1] // 2
    at = (1 - bit_value(CORE)) * half
    theirs = [lax.dynamic_slice_in_dim(v, at, half, 1).astype(F32) for v in values]
    got = exchange(jnp.concatenate(theirs, axis=0), CORE)
    return jnp.split(got, len(values), axis=0)


def send_whole(value):
    return exchange(value.astype(F32), CORE)


CROSS = ("batch", 1)


def send_across(value):
    value = value.astype(F32)
    return exchange(value, CORE), exchange(value, CROSS)


def hidden_kernel(
    at_ref, *refs, unit,
):
    del at_ref
    lefts, grads, (up_a, up_b, down_a, down_b, value_ref, key_ref, left_all, grad_all) = (
        refs[:4], refs[4:8], refs[8:]
    )
    tokens = lefts[0].shape[0]

    @pl.when(pl.program_id(0) == 0)
    def _():
        for k in range(4):
            at = pl.ds(k * tokens, tokens)
            left_all[at, :] = lefts[k][...].astype(BF16)
            grad_all[at, :] = grads[k][...].astype(BF16)

    up = jnp.concatenate([up_a[...], up_b[...]], axis=1)
    down = jnp.concatenate([down_a[...], down_b[...]], axis=0)
    first = lambda a, b: lax.dot_general(a, b, (((0,), (0,)), ((), ())), preferred_element_type=F32)

    def products(k):
        at = pl.ds(pl.multiple_of(k * tokens, tokens), tokens)
        left, grad = left_all[at, :], grad_all[at, :]
        above = jnp.maximum(jnp.dot(left, up, preferred_element_type=F32), 0.0)
        back = lax.dot_general(grad, down, (((1,), (1,)), ((), ())), preferred_element_type=F32)
        return first((above * above).astype(BF16), grad), first((back * (2.0 * above)).astype(BF16), left)

    def put(value, key, add):
        for half in range(2):
            part = value[half * unit : (half + 1) * unit]
            value_ref[half] = value_ref[half] + part if add else part
        rows = key.shape[1] // key_ref.shape[0]
        for s in range(key_ref.shape[0]):
            part = key[:, s * rows : (s + 1) * rows]
            key_ref[s] = key_ref[s] + part if add else part

    put(*products(0), False)

    def more(k, _):
        put(*products(k), True)
        return 0

    lax.fori_loop(1, 4, more, 0)


def hidden_products(left, far_lefts, grad, far_grads, up, down):
    seq, tokens, features = lax.axis_size("seq"), left.shape[0], left.shape[1]
    unit = up.shape[1] // seq // 4
    quarter = 2 * bit_value(CORE) + bit_value(CROSS)
    out_shapes = (seq, unit, features), (seq, seq * unit, features // seq)
    if unit % 128 or features // seq % 128:
        up = pick(up.reshape(features, seq, 4, unit), quarter, 2).reshape(features, -1)
        down = pick(down.reshape(seq, 4, unit, features), quarter, 1).reshape(-1, features)
        lefts = jnp.concatenate([left, *[f.astype(BF16) for f in far_lefts]])
        grads = jnp.concatenate([grad, *[f.astype(BF16) for f in far_grads]])
        above = jnp.maximum(jnp.dot(lefts, up, preferred_element_type=F32), 0.0)
        back = lax.dot_general(grads, down, (((1,), (1,)), ((), ())), preferred_element_type=F32)
        first = lambda a, b: lax.dot_general(a, b, (((0,), (0,)), ((), ())), preferred_element_type=F32)
        value = first((above * above).astype(BF16), grads).reshape(out_shapes[0])
        key = first((back * (2.0 * above)).astype(BF16), lefts)
        return value, jnp.swapaxes(key.reshape(-1, seq, features // seq), 0, 1)
    whole = lambda: pl.BlockSpec((tokens, features), lambda i, at: (0, 0), pipeline_mode=pl.Buffered(1))
    ups = [pl.BlockSpec((features, unit), lambda i, at, h=h: (0, 4 * (2 * i + h) + at[0])) for h in (0, 1)]
    downs = [pl.BlockSpec((unit, features), lambda i, at, h=h: (4 * (2 * i + h) + at[0], 0)) for h in (0, 1)]
    return pl.pallas_call(
        functools.partial(hidden_kernel, unit=unit),
        grid_spec=pltpu.PrefetchScalarGridSpec(
            num_scalar_prefetch=1,
            grid=(seq // 2,),
            in_specs=[whole() for _ in range(8)] + ups + downs,
            out_specs=[
                pl.BlockSpec((2, unit, features), lambda i, at: (i, 0, 0)),
                pl.BlockSpec((seq, 2 * unit, features // seq), lambda i, at: (0, i, 0)),
            ],
            scratch_shapes=[pltpu.VMEM((4 * tokens, features), BF16)] * 2,
        ),
        out_shape=[jax.ShapeDtypeStruct(shape, F32) for shape in out_shapes],
        compiler_params=pltpu.CompilerParams(vmem_limit_bytes=56 * 1024 * 1024),
        cost_estimate=pl.CostEstimate(
            flops=32 * tokens * features * seq * unit,
            bytes_accessed=40 * tokens * features,
            transcendentals=0,
        ),
    )(quarter[None].astype(jnp.int32), left, *far_lefts, grad, *far_grads, up, up, down, down)


ORDERS = dict(BV="zywx", BK="yzwx", FR="xzwy", OU="zxwy", AR="yxzw", AK="xyzw", AV="xyzw")
SEQUENCE = ("OVK", "", "PBPPPPPPPA", "PPPPPPFPR")


def order_of(name):
    seq = axis_bits("seq")
    places = dict(x=axis_bits("batch")[1:], y=seq[:1], z=seq[1:2], w=seq[2:])
    return [bit for letter in ORDERS[name] for bit in places[letter]]


class Blocks:
    def __init__(self, name, value):
        self.bits, self.dims = order_of(name), axis_bits("seq")[::-1]
        self.terms = [value.reshape(*((2,) * len(self.dims)), *value.shape[1:])]

    begun = False

    def multiply(self, line):
        return self

    def start(self, line):
        send, kept = self.split(self.terms)
        self.move(line.mark(send), kept)

    def started(self, got):
        self.dims.remove(self.bits.pop(0))
        self.begun, self.terms = True, [self.kept, got]

    def split(self, terms):
        if self.bits[0] not in self.dims:
            total = total_of(terms)
            return total, [total]
        dim, mine = self.dims.index(self.bits[0]), bit_value(self.bits[0])
        send = total_of([pick(t, 1 - mine, dim) for t in terms])
        return send, [pick(t, mine, dim) for t in terms]

    def move(self, send, kept):
        bit = self.bits.pop(0)
        if bit in self.dims:
            self.dims.remove(bit)
        self.begun = True
        self.terms = kept + [exchange(send, bit)]


class Queue:
    def __init__(self, line):
        self.line, self.jobs = line, []

    def run(self, steps, **jobs):
        for step in steps:
            if step == "P":
                self.pop()
                continue
            job = jobs[step]
            if job.begun:
                self.forward(job)
            else:
                job.multiply(self.line)
                job.start(self.line)
            self.jobs.append(job)

    def forward(self, job):
        send, kept = job.split(job.terms[:-1] + [self.line.gate(job.terms[-1])])
        job.move(self.line.mark(send), kept)

    def pop(self):
        job = self.jobs.pop(0)
        if job.bits:
            self.forward(job)
            self.jobs.append(job)


def product_kernel(
    at_ref, left_ref, far_left_ref, right_ref, far_right_ref, send_ref, keep_ref,
    *, rows, cols, group, place,
):
    first = at_ref[0]

    def lefts(blocks):
        cut = lambda ref, js: jnp.concatenate(
            [ref[:, pl.ds(pl.multiple_of(j * rows, 128), rows)] for j in js], axis=1
        )
        return jnp.concatenate([cut(left_ref, blocks), cut(far_left_ref, blocks).astype(BF16)], axis=0)

    def rights(x):
        at = pl.ds(pl.multiple_of(x * cols, 128), cols)
        return jnp.concatenate([right_ref[:, at], far_right_ref[:, at].astype(BF16)], axis=0)

    dot = lambda a, b: lax.dot_general(
        a, b, (((0,), (0,)), ((), ())), preferred_element_type=F32
    )
    for out, value in ((send_ref, 1 - first), (keep_ref, first)):
        if place is None:
            out[0] = dot(lefts(list(range(group))), rights(value))
        else:
            low = 1 << place
            blocks = [(q // low) * 2 * low + q % low + value * low for q in range(group // 2)]
            left = lefts(blocks)
            for x in range(2):
                out[x, 0] = dot(left, rights(x))


class Partial(Blocks):
    def __init__(self, name, left, right):
        self.left, self.right = left, right
        self.bits = order_of(name)
        self.dims = axis_bits("batch")[1:] + axis_bits("seq")[::-1]
        self.blocks = lax.axis_size("seq")
        self.rows = left[0].shape[1] // self.blocks
        self.cols = right[0].shape[1] // 4

    def plain(self):
        half = self.right[0].shape[1] // 2
        own = lax.dynamic_slice_in_dim(self.right[0], bit_value(CORE) * half, half, 1)
        dot = lambda a, b: lax.dot_general(
            a.astype(BF16), b.astype(BF16), (((0,), (0,)), ((), ())), preferred_element_type=F32
        )
        whole = dot(self.left[0], own) + dot(self.left[1], self.right[1])
        lead = (2,) * len(axis_bits("seq"))
        whole = jnp.moveaxis(whole.reshape(*lead, self.rows, 2, self.cols), -2, 0)
        dim, bit = self.dims.index(self.bits[0]), bit_value(self.bits[0])
        return pick(whole, 1 - bit, dim), pick(whole, bit, dim)

    def kernel(self):
        rows, cols, tokens = self.rows, self.cols, self.left[0].shape[0]
        first = self.bits[0]
        place = first[1] if first[0] == "seq" else None
        group = 4
        steps = self.blocks // group
        if place is None:
            block, shape = (1, group * rows, cols), (steps, group * rows, cols)
            out_index = lambda i, at: (i, 0, 0)
        else:
            block, shape = (2, 1, group // 2 * rows, cols), (2, steps, group // 2 * rows, cols)
            out_index = lambda i, at: (0, i, 0, 0)
        out = jax.ShapeDtypeStruct(shape, F32)
        at = jnp.stack([bit_value(first), bit_value(CORE)]).astype(jnp.int32)
        send, kept = pl.pallas_call(
            functools.partial(
                product_kernel, rows=rows, cols=cols, group=group, place=place
            ),
            grid_spec=pltpu.PrefetchScalarGridSpec(
                num_scalar_prefetch=1,
                grid=(steps,),
                in_specs=[
                    pl.BlockSpec((tokens, group * rows), lambda i, at: (0, i)),
                    pl.BlockSpec((tokens, group * rows), lambda i, at: (0, i)),
                    pl.BlockSpec((tokens, 2 * cols), lambda i, at: (0, at[1])),
                    pl.BlockSpec((tokens, 2 * cols), lambda i, at: (0, 0)),
                ],
                out_specs=[pl.BlockSpec(block, out_index)] * 2,
            ),
            out_shape=[out, out],
            compiler_params=scan_params(),
            cost_estimate=pl.CostEstimate(
                flops=8 * tokens * self.blocks * rows * cols,
                bytes_accessed=8 * self.blocks * rows * cols,
                transcendentals=0,
            ),
        )(at, self.left[0], self.left[1], self.right[0], self.right[1])
        lead = (2,) * (len(self.dims) - 1)
        return send.reshape(*lead, rows, cols), kept.reshape(*lead, rows, cols)

    def multiply(self, line):
        self.left = (line.gate(self.left[0]), self.left[1])
        aligned = self.rows % 128 == 0 and self.blocks % 4 == 0 and len(axis_bits("batch")) == 2
        self.send, self.kept = self.kernel() if aligned else self.plain()
        line.mark(self.send)
        return self

    def start(self, line):
        self.move(line.gate(self.send), [self.kept])


class Vectors(Blocks):
    def __init__(self, vectors):
        count, seq = vectors.shape[0], lax.axis_size("seq")
        self.dims = axis_bits("seq")[::-1]
        self.bits = axis_bits("batch") + axis_bits("seq")
        value = jnp.swapaxes(vectors.reshape(count, seq, -1), 0, 1)
        self.terms = [value.reshape(*((2,) * len(self.dims)), count, -1)]

def in_order(own, other, bit, axis):
    first = bit_value(bit) == 0
    return jnp.concatenate(
        [jnp.where(first, own, other), jnp.where(first, other, own)], axis=axis
    )


def gather(line, value_part, key_part, parts):
    own = line.mark(jnp.stack([total_of(p.terms[:-1] + [line.gate(p.terms[-1])]) for p in parts]))
    other = exchange(own, CROSS)
    value = in_order(*value_part.terms, CROSS, 0)
    value = in_order(value, exchange(value, CORE), CORE, 0)
    seq = lax.axis_size("seq")
    halves = [t.reshape(seq, 1, -1, t.shape[-1]) for t in key_part.terms]
    key = in_order(*halves, CROSS, 1)
    key = in_order(key, exchange(key, CORE), CORE, 1)
    own = in_order(own, other, CROSS, 2)
    own = in_order(own, exchange(own, CORE), CORE, 2)
    return value, jnp.transpose(key.reshape(-1, key.shape[-1])), *[own[i] for i in range(len(parts))]


def entering(tails, begins, decay_rate, group_len, backward):
    count, mine = lax.axis_size("seq"), lax.axis_index("seq")
    sign = -1 if backward else 1

    def gain(lo, hi):
        a, b = (mine + lo, mine + hi) if backward else (mine - hi + 1, mine - lo + 1)
        hit = jnp.any((begins >= a * group_len) & (begins < b * group_len), axis=1, keepdims=True)
        return jnp.where(hit, 0.0, 1.0) * jnp.exp(-float((hi - lo) * group_len) * decay_rate)[None, :]

    reach, window, before = 1, tails, None
    while reach < count:
        got = [
            (j, shifted(window, "seq", sign * j * reach)) for j in range(1, 4) if j * reach < count
        ]
        if before is None:
            before = total_of([v if j == 1 else gain(1, j) * v for j, v in got])
            seen = 1 + len(got)
            window = tails + gain(0, 1) * before if seen < count else None
        else:
            before_more = total_of([gain(1, j * reach) * v for j, v in got])
            seen = reach * (1 + len(got))
            if seen < count:
                window = window + total_of([gain(0, j * reach) * v for j, v in got])
            before = before + before_more
        reach *= 4
    return before


def scan_params():
    return pltpu.CompilerParams(vmem_limit_bytes=48 * 1024 * 1024)


def at_step(ref, row, step, length, lanes):
    return ref[row, pl.ds(step, STEPS, stride=length // STEPS), lanes]


def lane_tiles(width):
    return [slice(i, i + 128) for i in range(0, width, 128)]


def join_pieces(tails, gains, order):
    total = None
    for c in order:
        part = tails[c : c + 1]
        total = part if total is None else gains[c : c + 1] * total + part
    return total


def forward_tails_kernel(k_ref, v_ref, keep_ref, rate_ref, piece_ref, tail_ref):
    rows, length, width = k_ref.shape
    steps = length // STEPS
    tiles = lane_tiles(width)
    chains = [(r, t) for r in range(rows) for t in tiles]
    decay = [jnp.exp(-rate_ref[0:1, t]) for t in tiles]

    def step(j, carry):
        out = []
        flags = [keep_ref[r, pl.ds(j, STEPS, stride=steps), :] for r in range(rows)]
        for i, (r, t) in enumerate(chains):
            num, den, alive = carry[i]
            e = jnp.exp(at_step(k_ref, r, j, length, t))
            v = at_step(v_ref, r, j, length, t)
            f = flags[r] * decay[i % len(tiles)]
            out.append((f * num + e * v, f * den + e, alive * flags[r]))
        return tuple(out)

    zero = jnp.zeros((STEPS, 128), F32)
    done = lax.fori_loop(
        0, steps, step, tuple((zero, zero, jnp.ones((STEPS, 128), F32)) for _ in chains), unroll=4
    )
    for (r, t), (num, den, alive) in zip(chains, done):
        gains = alive * jnp.exp(-float(steps) * rate_ref[0:1, t])
        piece_ref[0, r, :, t] = num
        piece_ref[1, r, :, t] = den
        piece_ref[2, r, :, t] = gains
        tail_ref[0, r : r + 1, t] = join_pieces(num, gains, range(STEPS))
        tail_ref[1, r : r + 1, t] = join_pieces(den, gains, range(STEPS))


def forward_states_kernel(
    k_ref, v_ref, recep_ref, keep_ref, rate_ref, bonus_ref, piece_ref, enter_ref,
    num_ref, den_ref, gated_ref,
):
    rows, length, width = k_ref.shape
    steps = length // STEPS
    tiles = lane_tiles(width)
    chains = [(r, t) for r in range(rows) for t in tiles]
    decay = [jnp.exp(-rate_ref[0:1, t]) for t in tiles]
    carry = []
    for r, t in chains:
        gains = piece_ref[2, r, :, t]
        start = []
        for q in range(2):
            tails, held, parts = piece_ref[q, r, :, t], enter_ref[q, r : r + 1, t], []
            for c in range(STEPS):
                parts.append(held)
                held = gains[c : c + 1] * held + tails[c : c + 1]
            start.append(jnp.concatenate(parts, axis=0))
        carry.append(tuple(start))

    def step(j, carry):
        out = []
        flags = [keep_ref[r, pl.ds(j, STEPS, stride=steps), :] for r in range(rows)]
        for i, (r, t) in enumerate(chains):
            num, den = carry[i]
            num, den = num * flags[r], den * flags[r]
            num_ref[r, pl.ds(j, STEPS, stride=steps), t] = num
            den_ref[r, pl.ds(j, STEPS, stride=steps), t] = den
            e = jnp.exp(at_step(k_ref, r, j, length, t))
            v = at_step(v_ref, r, j, length, t)
            d = decay[i % len(tiles)]
            out.append((d * num + e * v, d * den + e))
        return tuple(out)

    lax.fori_loop(0, steps, step, tuple(carry), unroll=4)
    bonus = bonus_ref[0:1, :]

    def finish(b, _):
        for r in range(rows):
            at = pl.ds(pl.multiple_of(b * CHUNK, CHUNK), CHUNK)
            first = jnp.exp(bonus + k_ref[r, at, :])
            wkv = (num_ref[r, at, :] + first * v_ref[r, at, :]) / (den_ref[r, at, :] + first)
            gated_ref[r, at, :] = (jax.nn.sigmoid(recep_ref[r, at, :]) * wkv).astype(BF16)
        return 0

    lax.fori_loop(0, length // CHUNK, finish, 0)


def backward_tails_kernel(
    grad_ref, k_ref, v_ref, recep_ref, num_ref, den_ref, keep_ref, rate_ref, bonus_ref,
    gnum_ref, gden_ref, grecep_ref, piece_ref, tail_ref,
):
    rows, length, width = k_ref.shape
    steps = length // STEPS
    tiles = lane_tiles(width)
    bonus = bonus_ref[0:1, :]

    def begin(b, _):
        for r in range(rows):
            at = pl.ds(pl.multiple_of(b * CHUNK, CHUNK), CHUNK)
            first = jnp.exp(bonus + k_ref[r, at, :])
            below = den_ref[r, at, :] + first
            wkv = (num_ref[r, at, :] + first * v_ref[r, at, :]) / below
            gate = jax.nn.sigmoid(recep_ref[r, at, :])
            grad = grad_ref[r, at, :]
            grecep_ref[r, at, :] = (grad * wkv * (gate * (1.0 - gate))).astype(BF16)
            up = grad * gate / below
            gnum_ref[r, at, :] = up
            gden_ref[r, at, :] = -up * wkv
        return 0

    lax.fori_loop(0, length // CHUNK, begin, 0)
    chains = [(r, t) for r in range(rows) for t in tiles]
    decay = [jnp.exp(-rate_ref[0:1, t]) for t in tiles]

    def step(i_step, carry):
        j = steps - 1 - i_step
        out = []
        flags = [keep_ref[r, pl.ds(j, STEPS, stride=steps), :] for r in range(rows)]
        for i, (r, t) in enumerate(chains):
            num, den, alive = carry[i]
            d = decay[i % len(tiles)]
            out.append(
                (
                    flags[r] * (at_step(gnum_ref, r, j, length, t) + d * num),
                    flags[r] * (at_step(gden_ref, r, j, length, t) + d * den),
                    alive * flags[r],
                )
            )
        return tuple(out)

    zero = jnp.zeros((STEPS, 128), F32)
    done = lax.fori_loop(
        0, steps, step, tuple((zero, zero, jnp.ones((STEPS, 128), F32)) for _ in chains), unroll=4
    )
    for (r, t), (num, den, alive) in zip(chains, done):
        gains = alive * jnp.exp(-float(steps) * rate_ref[0:1, t])
        piece_ref[0, r, :, t] = num
        piece_ref[1, r, :, t] = den
        piece_ref[2, r, :, t] = gains
        tail_ref[0, r : r + 1, t] = join_pieces(num, gains, range(STEPS)[::-1])
        tail_ref[1, r : r + 1, t] = join_pieces(den, gains, range(STEPS)[::-1])


def backward_states_kernel(
    gnum_ref, gden_ref, k_ref, v_ref, num_ref, den_ref, keep_ref, rate_ref, bonus_ref, piece_ref,
    enter_ref, gkey_ref, gvalue_ref, sums_ref, snum_ref, sden_ref,
):
    rows, length, width = k_ref.shape
    steps = length // STEPS
    tiles = lane_tiles(width)
    chains = [(r, t) for r in range(rows) for t in tiles]
    decay = [jnp.exp(-rate_ref[0:1, t]) for t in tiles]
    carry = []
    for r, t in chains:
        gains = piece_ref[2, r, :, t]
        start = []
        for q in range(2):
            tails, held, parts = piece_ref[q, r, :, t], enter_ref[q, r : r + 1, t], []
            for c in range(STEPS)[::-1]:
                parts.append(held)
                held = gains[c : c + 1] * held + tails[c : c + 1]
            start.append(jnp.concatenate(parts[::-1], axis=0))
        carry.append(tuple(start))

    def step(i_step, carry):
        j = steps - 1 - i_step
        out = []
        flags = [keep_ref[r, pl.ds(j, STEPS, stride=steps), :] for r in range(rows)]
        for i, (r, t) in enumerate(chains):
            num, den = carry[i]
            snum_ref[r, pl.ds(j, STEPS, stride=steps), t] = num
            sden_ref[r, pl.ds(j, STEPS, stride=steps), t] = den
            d = decay[i % len(tiles)]
            out.append(
                (
                    flags[r] * (at_step(gnum_ref, r, j, length, t) + d * num),
                    flags[r] * (at_step(gden_ref, r, j, length, t) + d * den),
                )
            )
        return tuple(out)

    lax.fori_loop(0, steps, step, tuple(carry), unroll=4)
    bonus = bonus_ref[0:1, :]

    def finish(b, sums):
        slope, fade = sums
        for r in range(rows):
            at = pl.ds(pl.multiple_of(b * CHUNK, CHUNK), CHUNK)
            key, value = k_ref[r, at, :], v_ref[r, at, :]
            e, first = jnp.exp(key), jnp.exp(bonus + key)
            up, low = gnum_ref[r, at, :], gden_ref[r, at, :]
            later_num, later_den = snum_ref[r, at, :], sden_ref[r, at, :]
            present = first * (up * value + low)
            gvalue_ref[r, at, :] = (up * first + later_num * e).astype(BF16)
            gkey_ref[r, at, :] = (present + e * (later_num * value + later_den)).astype(BF16)
            slope = slope + jnp.sum(present.reshape(-1, 8, width), axis=0)
            both = num_ref[r, at, :] * later_num + den_ref[r, at, :] * later_den
            fade = fade + jnp.sum(both.reshape(-1, 8, width), axis=0)
        return slope, fade

    zero = jnp.zeros((8, width), F32)
    slope, fade = lax.fori_loop(0, length // CHUNK, finish, (zero, zero))
    sums_ref[0:8, :] = slope
    sums_ref[8:16, :] = fade


def scan_call(kernel, inputs, outputs, scratch=(), width=128):
    features = inputs[0].shape[-1]

    def spec(shape):
        lead = len(shape) - 1
        if shape[-1] == 128 and features != 128:
            return pl.BlockSpec(shape, lambda i: (0,) * (lead + 1))
        return pl.BlockSpec((*shape[:-1], width), lambda i: (0,) * lead + (i,))

    out_shape = [jax.ShapeDtypeStruct(s, d) for s, d in outputs]
    moved = sum(x.size * x.dtype.itemsize for x in [*inputs, *out_shape])
    return pl.pallas_call(
        kernel,
        out_shape=out_shape,
        grid=(features // width,),
        in_specs=[spec(x.shape) for x in inputs],
        out_specs=[spec(s) for s, _ in outputs],
        scratch_shapes=[pltpu.VMEM((*s[:-1], width), F32) for s in scratch],
        compiler_params=scan_params(),
        cost_estimate=pl.CostEstimate(
            flops=20 * inputs[0].size, bytes_accessed=moved, transcendentals=inputs[0].size
        ),
    )(*inputs)


def norm_rows(value_rows, gain_vec, bias_vec):
    row_mean = jnp.mean(value_rows, axis=-1, keepdims=True)
    centred = value_rows - row_mean
    inv_std = lax.rsqrt(jnp.mean(centred * centred, axis=-1, keepdims=True) + 1e-05)
    normed = centred * inv_std
    return (normed * gain_vec + bias_vec, normed, inv_std)


def norm_back(grad_in, normed, inv_std, gain_vec):
    scaled = grad_in * gain_vec
    return inv_std * (
        scaled
        - jnp.mean(scaled, axis=-1, keepdims=True)
        - normed * jnp.mean(scaled * normed, axis=-1, keepdims=True)
    )


def project(left_side, right_side):
    return jnp.einsum("rcd,de->rce", left_side, right_side, preferred_element_type=F32)


def project_back(grad_in, right_side):
    return jnp.einsum("rce,de->rcd", grad_in, right_side, preferred_element_type=F32)


def with_previous(value_rows, edge_row, keep):
    earlier = jnp.concatenate([edge_row[:, None, :], value_rows[:, :-1, :]], axis=1)
    return earlier * keep[:, :, None]


def flat(value):
    return value.reshape(-1, value.shape[-1])


def shards(
    incoming_symbols,
    article_sizes,
    mixer_norm_scale,
    mixer_norm_offset,
    temporal_lookup_share,
    temporal_payload_share,
    temporal_gate_share,
    fading_log_rates,
    present_reward_vector,
    lookup_matrix,
    payload_matrix,
    gate_matrix,
    emission_matrix,
    channel_norm_scale,
    channel_norm_offset,
    channel_lookup_share,
    channel_gate_share,
    channel_lookup_matrix,
    channel_payload_matrix,
    channel_gate_matrix,
    final_cotangent,
):
    rows_here, group_len, features = incoming_symbols.shape
    full = (rows_here, group_len, features)
    begins = jnp.cumsum(article_sizes, axis=1) - article_sizes
    position = lax.axis_index("seq") * group_len + jnp.arange(group_len, dtype=jnp.int32)
    starts = jnp.any(position[None, :, None] == begins[:, None, :], axis=2)
    keep = jnp.where(starts, 0.0, 1.0).astype(F32)
    keep_wide = jnp.broadcast_to(keep[:, :, None], (rows_here, group_len, 128))
    decay_rate = jnp.exp(fading_log_rates)
    rate_row = jnp.broadcast_to(decay_rate[None, :], (8, features))
    bonus_row = jnp.broadcast_to(present_reward_vector[None, :], (8, features))
    ready = article_sizes[0, 0] > 0
    enter = functools.partial(entering, begins=begins, decay_rate=decay_rate, group_len=group_len)

    symbols = incoming_symbols.astype(F32)
    att_last = norm_rows(symbols[:, -1, :], mixer_norm_scale, mixer_norm_offset)[0]
    att_edge = shifted(att_last, "seq", 1)
    att_normed, att_unit, att_inv = norm_rows(symbols, mixer_norm_scale, mixer_norm_offset)
    att_prev = with_previous(att_normed, att_edge, keep)
    mix = lambda share: (att_normed * share + att_prev * (1.0 - share)).astype(BF16)
    key_mixed = mix(temporal_lookup_share)
    value_mixed = mix(temporal_payload_share)
    recep_mixed = mix(temporal_gate_share)
    key_proj = project(key_mixed, lookup_matrix)
    value_proj = project(value_mixed, payload_matrix)
    recep_proj = project(recep_mixed, gate_matrix)
    pieces = ((3, rows_here, STEPS, features), F32)
    tails = ((2, rows_here, features), F32)
    piece, tail = scan_call(
        forward_tails_kernel, [key_proj, value_proj, keep_wide, rate_row], [pieces, tails]
    )
    key_mixed, value_mixed, recep_mixed = map(flat, (key_mixed, value_mixed, recep_mixed))
    state, key_far, value_far, recep_far = at_once(
        ready,
        lambda: (enter(tail, backward=False), *map(send_whole, (key_mixed, value_mixed, recep_mixed))),
    )
    key_side, value_side, recep_side = (
        (key_mixed, key_far), (value_mixed, value_far), (recep_mixed, recep_far)
    )
    num_state, den_state, gated = scan_call(
        forward_states_kernel,
        [key_proj, value_proj, recep_proj, keep_wide, rate_row, bonus_row, piece, state],
        [(full, F32), (full, F32), (full, BF16)],
    )
    after_att = symbols + project(gated, emission_matrix)

    ffn_normed, ffn_unit, ffn_inv = norm_rows(after_att, channel_norm_scale, channel_norm_offset)
    gated = flat(gated)
    last_rows = ffn_normed[:, -1, :]
    ffn_edge, gated_far = at_once(
        ready, lambda: (shifted(last_rows, "seq", 1), send_whole(gated))
    )
    gated_side = (gated, gated_far)
    ffn_prev = with_previous(ffn_normed, ffn_edge, keep)
    ffn_key_mixed = (
        ffn_normed * channel_lookup_share + ffn_prev * (1.0 - channel_lookup_share)
    ).astype(BF16)
    ffn_recep_mixed = (
        ffn_normed * channel_gate_share + ffn_prev * (1.0 - channel_gate_share)
    ).astype(BF16)
    line = Line()
    gate, mark = line.gate, line.mark
    fkey_far = send_across(flat(ffn_key_mixed))
    hidden_pre = project(ffn_key_mixed, channel_lookup_matrix)
    above = jnp.maximum(hidden_pre, 0.0)
    squared = jnp.square(above).astype(BF16)
    ffn_gate = jax.nn.sigmoid(project(ffn_recep_mixed, channel_gate_matrix))
    ffn_value = project(squared, channel_payload_matrix)
    layer_out = (after_att + ffn_gate * ffn_value).astype(BF16)

    grad_top = final_cotangent.astype(F32)
    grad_fvalue = mark((grad_top * ffn_gate).astype(BF16))
    grad_frecep = (grad_top * ffn_value * (ffn_gate * (1.0 - ffn_gate))).astype(BF16)
    fvalue_far = send_across(flat(grad_fvalue))
    grad_squared = project_back(grad_fvalue, channel_payload_matrix)
    grad_hidden = (grad_squared * (2.0 * above)).astype(BF16)
    grad_fkey_in = project_back(grad_hidden, channel_lookup_matrix)
    grad_frecep_in = project_back(grad_frecep, channel_gate_matrix)
    ffn_delta = ffn_normed - ffn_prev
    grad_ffn_mix_key = jnp.sum(grad_fkey_in * ffn_delta, axis=(0, 1))
    grad_ffn_mix_recep = jnp.sum(grad_frecep_in * ffn_delta, axis=(0, 1))
    grad_ffn_prev = mark(
        (grad_fkey_in * (1.0 - channel_lookup_share) + grad_frecep_in * (1.0 - channel_gate_share))
        * keep[:, :, None]
    )
    first_row = gate(grad_ffn_prev[:, 0, :])
    ffn_back_edge, frecep_far, grad_frecep_far, fkey_cross = at_once(
        ready,
        lambda: (
            shifted(first_row, "seq", -1),
            send_whole(flat(ffn_recep_mixed)),
            send_half(flat(grad_frecep)),
            exchange(fkey_far[1], CORE),
        ),
    )
    mark(ffn_back_edge)
    grad_ffn_normed = (
        grad_fkey_in * channel_lookup_share
        + grad_frecep_in * channel_gate_share
        + jnp.concatenate([grad_ffn_prev[:, 1:, :], ffn_back_edge[:, None, :]], axis=1)
    )
    grad_ffn_ln_gain = jnp.sum(grad_ffn_normed * ffn_unit, axis=(0, 1))
    grad_ffn_ln_bias = jnp.sum(grad_ffn_normed, axis=(0, 1))
    grad_after = grad_top + norm_back(grad_ffn_normed, ffn_unit, ffn_inv, channel_norm_scale)

    grad_att_out = mark(grad_after.astype(BF16))
    grad_gated = project_back(gate(grad_att_out), emission_matrix)
    grad_num, grad_den, grad_recep, piece, tail = scan_call(
        backward_tails_kernel,
        [grad_gated, key_proj, value_proj, recep_proj, num_state, den_state, keep_wide, rate_row, bonus_row],
        [(full, F32), (full, F32), (full, BF16), pieces, tails],
    )
    gated_tail = gate(mark(tail))
    state, recep_out_far = at_once(
        ready,
        lambda: (
            enter(gated_tail, backward=True),
            send_half_of((flat(grad_recep), flat(grad_att_out))),
        ),
    )
    recep_far, out_far = recep_out_far
    mark(state)

    fr = Partial("FR", (flat(ffn_recep_mixed), frecep_far), (flat(grad_frecep), grad_frecep_far))
    ou = Partial("OU", (gated, gated_far), (flat(grad_att_out), out_far))
    ar = Partial("AR", recep_side, (flat(grad_recep), recep_far))
    queue = Queue(line)
    fvalue_cross = exchange(gate(fvalue_far[1]), CORE)
    fr.multiply(line)
    ar.multiply(line)
    ou.multiply(line)
    mark(fvalue_cross, ou.send)
    early = (fr, ou, ar)
    gated_left = gate(flat(ffn_key_mixed))

    def hidden_step():
        got = [exchange(job.send, job.bits[0]) for job in early]
        made = hidden_products(
            gated_left,
            (*fkey_far, fkey_cross),
            flat(grad_fvalue),
            (*fvalue_far, fvalue_cross),
            channel_lookup_matrix,
            channel_payload_matrix,
        )
        return *made, got

    value_blocks, key_blocks, arrived = at_once(ready, hidden_step)
    for job, got in zip(early, arrived):
        job.started(got)
    mark(key_blocks)
    big_value, big_key = Blocks("BV", value_blocks), Blocks("BK", key_blocks)
    queue.run(SEQUENCE[0], V=big_value, K=big_key, F=fr, O=ou, R=ar)
    grad_key, grad_value, sums = scan_call(
        backward_states_kernel,
        [grad_num, grad_den, key_proj, value_proj, num_state, den_state, keep_wide, rate_row, bonus_row, piece, gate(state)],
        [(full, BF16), (full, BF16), ((16, features), F32)],
        scratch=(full, full),
    )
    mark(sums)
    reward_slope = jnp.sum(sums[:8], axis=0)
    grad_time_decay = -decay_rate * jnp.exp(-decay_rate) * jnp.sum(sums[8:], axis=0)
    queue.run(SEQUENCE[1], F=fr, O=ou, R=ar)

    gated_key = gate(grad_key)

    def back_att():
        return (
            send_half_of((flat(gated_key), flat(grad_value))),
            project_back(gated_key, lookup_matrix),
            project_back(grad_value, payload_matrix),
            project_back(grad_recep, gate_matrix),
        )

    (key_far, value_far), grad_key_in, grad_value_in, grad_recep_in = at_once(ready, back_att)
    mark(key_far)
    ak = Partial("AK", key_side, (flat(grad_key), key_far))
    av = Partial("AV", value_side, (flat(grad_value), value_far))
    queue.run(SEQUENCE[2], F=fr, O=ou, R=ar, A=ak, B=av)
    att_delta = att_normed - att_prev
    grad_mix_key = jnp.sum(grad_key_in * att_delta, axis=(0, 1))
    grad_mix_value = jnp.sum(grad_value_in * att_delta, axis=(0, 1))
    grad_mix_recep = jnp.sum(grad_recep_in * att_delta, axis=(0, 1))
    direct = (
        grad_key_in * temporal_lookup_share
        + grad_value_in * temporal_payload_share
        + grad_recep_in * temporal_gate_share
    )
    grad_att_prev = mark(
        (
            grad_key_in * (1.0 - temporal_lookup_share)
            + grad_value_in * (1.0 - temporal_payload_share)
            + grad_recep_in * (1.0 - temporal_gate_share)
        )
        * keep[:, :, None]
    )
    last_row = gate(grad_att_prev[:, 0, :])
    att_back_edge = mark(at_once(ready, lambda: shifted(last_row, "seq", -1)))
    grad_att_normed = direct + jnp.concatenate(
        [grad_att_prev[:, 1:, :], att_back_edge[:, None, :]], axis=1
    )
    grad_att_ln_gain = mark(jnp.sum(grad_att_normed * att_unit, axis=(0, 1)))
    grad_att_ln_bias = jnp.sum(grad_att_normed, axis=(0, 1))
    grad_tokens = (
        grad_after + norm_back(grad_att_normed, att_unit, att_inv, mixer_norm_scale)
    ).astype(BF16)
    vectors = Vectors(
        jnp.stack(
            [
                grad_att_ln_gain,
                grad_att_ln_bias,
                grad_mix_key,
                grad_mix_value,
                grad_mix_recep,
                grad_time_decay,
                reward_slope,
                grad_ffn_ln_gain,
                grad_ffn_ln_bias,
                grad_ffn_mix_key,
                grad_ffn_mix_recep,
            ]
        )
    )
    queue.run(SEQUENCE[3] + "X", F=fr, O=ou, R=ar, A=ak, B=av, X=vectors)
    while queue.jobs:
        queue.pop()
    value_sum, key_sum, fr_sum, ou_sum, ar_sum, ak_sum, av_sum = gather(
        line, big_value, big_key, [fr, ou, ar, ak, av]
    )
    small = total_of(vectors.terms)
    return (
        layer_out,
        grad_tokens,
        *[small[i] for i in range(7)],
        ak_sum,
        av_sum,
        ar_sum,
        ou_sum,
        *[small[i] for i in range(7, 11)],
        key_sum,
        value_sum,
        fr_sum,
    )


def solution(mesh):
    tokens = P("batch", "seq", None)
    vector, matrix = P("seq"), P("seq", None)
    return jax.shard_map(
        shards,
        mesh=mesh,
        in_specs=(tokens, P("batch", None), *([P()] * 18), tokens),
        out_specs=(tokens, tokens, *([vector] * 7), *([matrix] * 4), *([vector] * 4), *([matrix] * 3)),
        check_vma=False,
    )
```

```python
import functools
import math

import jax
import jax.numpy as jnp
from jax import lax
from jax.experimental import pallas as pl
from jax.experimental.pallas import tpu as pltpu
from jax.sharding import PartitionSpec as P

F32, BF16 = jnp.float32, jnp.bfloat16


def shifted(value, axis, distance):
    devices = range(lax.axis_size(axis))
    route = [(i - distance, i) for i in devices if i - distance in devices]
    return lax.ppermute(value, axis, route)


def bit_value(bit):
    axis, place = bit
    return (lax.axis_index(axis) >> place) & 1


def exchange(value, bit):
    axis, place = bit
    return lax.ppermute(value, axis, [(i, i ^ (1 << place)) for i in range(lax.axis_size(axis))])


def pick(value, index, dim):
    return lax.dynamic_index_in_dim(value, index, dim, keepdims=False)


def total_of(terms):
    return functools.reduce(lambda a, b: a + b, terms)


def axis_bits(axis):
    return [(axis, k) for k in range(int(math.log2(lax.axis_size(axis))))]


def at_once(ready, step, *values):
    blank = lambda *v: jax.tree.map(
        lambda x: jnp.zeros(x.shape, x.dtype), jax.eval_shape(step, *v)
    )
    return lax.cond(ready, step, blank, *values)


class Line:
    def __init__(self):
        self.token = None

    def gate(self, value):
        if self.token is None:
            return value
        return lax.optimization_barrier((value, self.token))[0]

    def mark(self, value, *others):
        self.token = (value, *others)
        return value


CORE = ("batch", 0)


def send_half(value):
    half = value.shape[1] // 2
    theirs = lax.dynamic_slice_in_dim(value, (1 - bit_value(CORE)) * half, half, 1)
    return exchange(theirs.astype(F32), CORE)


def send_half_of(values):
    half = values[0].shape[1] // 2
    at = (1 - bit_value(CORE)) * half
    theirs = [lax.dynamic_slice_in_dim(v, at, half, 1).astype(F32) for v in values]
    got = exchange(jnp.concatenate(theirs, axis=0), CORE)
    return jnp.split(got, len(values), axis=0)


def send_whole(value):
    return exchange(value.astype(F32), CORE)


CROSS = ("batch", 1)


def send_across(value):
    value = value.astype(F32)
    return exchange(value, CORE), exchange(value, CROSS)


def hidden_kernel(
    at_ref, *refs, unit,
):
    del at_ref
    lefts, grads, (up_a, up_b, down_a, down_b, value_ref, key_ref, left_all, grad_all) = (
        refs[:4], refs[4:8], refs[8:]
    )
    tokens = lefts[0].shape[0]

    @pl.when(pl.program_id(0) == 0)
    def _():
        for k in range(4):
            at = pl.ds(k * tokens, tokens)
            left_all[at, :] = lefts[k][...].astype(BF16)
            grad_all[at, :] = grads[k][...].astype(BF16)

    up = jnp.concatenate([up_a[...], up_b[...]], axis=1)
    down = jnp.concatenate([down_a[...], down_b[...]], axis=0)
    first = lambda a, b: lax.dot_general(a, b, (((0,), (0,)), ((), ())), preferred_element_type=F32)

    def products(k):
        at = pl.ds(k * 2 * tokens, 2 * tokens)
        left, grad = left_all[at, :], grad_all[at, :]
        above = jnp.maximum(jnp.dot(left, up, preferred_element_type=F32), 0.0)
        back = lax.dot_general(grad, down, (((1,), (1,)), ((), ())), preferred_element_type=F32)
        return first((above * above).astype(BF16), grad), first((back * (2.0 * above)).astype(BF16), left)

    def put(value, key, add):
        for half in range(2):
            part = value[half * unit : (half + 1) * unit]
            value_ref[half] = value_ref[half] + part if add else part
        rows = key.shape[1] // key_ref.shape[0]
        for s in range(key_ref.shape[0]):
            part = key[:, s * rows : (s + 1) * rows]
            key_ref[s] = key_ref[s] + part if add else part

    put(*products(0), False)
    put(*products(1), True)


def hidden_products(left, far_lefts, grad, far_grads, up, down):
    seq, tokens, features = lax.axis_size("seq"), left.shape[0], left.shape[1]
    unit = up.shape[1] // seq // 4
    quarter = 2 * bit_value(CORE) + bit_value(CROSS)
    out_shapes = (seq, unit, features), (seq, seq * unit, features // seq)
    if unit % 128 or features // seq % 128:
        up = pick(up.reshape(features, seq, 4, unit), quarter, 2).reshape(features, -1)
        down = pick(down.reshape(seq, 4, unit, features), quarter, 1).reshape(-1, features)
        lefts = jnp.concatenate([left, *[f.astype(BF16) for f in far_lefts]])
        grads = jnp.concatenate([grad, *[f.astype(BF16) for f in far_grads]])
        above = jnp.maximum(jnp.dot(lefts, up, preferred_element_type=F32), 0.0)
        back = lax.dot_general(grads, down, (((1,), (1,)), ((), ())), preferred_element_type=F32)
        first = lambda a, b: lax.dot_general(a, b, (((0,), (0,)), ((), ())), preferred_element_type=F32)
        value = first((above * above).astype(BF16), grads).reshape(out_shapes[0])
        key = first((back * (2.0 * above)).astype(BF16), lefts)
        return value, jnp.swapaxes(key.reshape(-1, seq, features // seq), 0, 1)
    whole = lambda: pl.BlockSpec((tokens, features), lambda i, at: (0, 0), pipeline_mode=pl.Buffered(1))
    ups = [pl.BlockSpec((features, unit), lambda i, at, h=h: (0, 4 * (2 * i + h) + at[0])) for h in (0, 1)]
    downs = [pl.BlockSpec((unit, features), lambda i, at, h=h: (4 * (2 * i + h) + at[0], 0)) for h in (0, 1)]
    return pl.pallas_call(
        functools.partial(hidden_kernel, unit=unit),
        grid_spec=pltpu.PrefetchScalarGridSpec(
            num_scalar_prefetch=1,
            grid=(seq // 2,),
            in_specs=[whole() for _ in range(8)] + ups + downs,
            out_specs=[
                pl.BlockSpec((2, unit, features), lambda i, at: (i, 0, 0)),
                pl.BlockSpec((seq, 2 * unit, features // seq), lambda i, at: (0, i, 0)),
            ],
            scratch_shapes=[pltpu.VMEM((4 * tokens, features), BF16)] * 2,
        ),
        out_shape=[jax.ShapeDtypeStruct(shape, F32) for shape in out_shapes],
        compiler_params=pltpu.CompilerParams(vmem_limit_bytes=56 * 1024 * 1024),
        cost_estimate=pl.CostEstimate(
            flops=32 * tokens * features * seq * unit,
            bytes_accessed=40 * tokens * features,
            transcendentals=0,
        ),
    )(quarter[None].astype(jnp.int32), left, *far_lefts, grad, *far_grads, up, up, down, down)


ORDERS = dict(BV="zywx", BK="yzwx", FR="xzwy", OU="zxwy", AR="yxzw", AK="xyzw", AV="xyzw")
SEQUENCE = ("OVK", "", "PBPPPPPPPA", "PPPPPPFPR")


def order_of(name):
    seq = axis_bits("seq")
    places = dict(x=axis_bits("batch")[1:], y=seq[:1], z=seq[1:2], w=seq[2:])
    return [bit for letter in ORDERS[name] for bit in places[letter]]


class Blocks:
    def __init__(self, name, value):
        self.bits, self.dims = order_of(name), axis_bits("seq")[::-1]
        self.terms = [value.reshape(*((2,) * len(self.dims)), *value.shape[1:])]

    begun = False

    def multiply(self, line):
        return self

    def start(self, line):
        send, kept = self.split(self.terms)
        self.move(line.mark(send), kept)

    def started(self, got):
        self.dims.remove(self.bits.pop(0))
        self.begun, self.terms = True, [self.kept, got]

    def split(self, terms):
        if self.bits[0] not in self.dims:
            total = total_of(terms)
            return total, [total]
        dim, mine = self.dims.index(self.bits[0]), bit_value(self.bits[0])
        send = total_of([pick(t, 1 - mine, dim) for t in terms])
        return send, [pick(t, mine, dim) for t in terms]

    def move(self, send, kept):
        bit = self.bits.pop(0)
        if bit in self.dims:
            self.dims.remove(bit)
        self.begun = True
        self.terms = kept + [exchange(send, bit)]


class Queue:
    def __init__(self, line):
        self.line, self.jobs = line, []

    def run(self, steps, **jobs):
        for step in steps:
            if step == "P":
                self.pop()
                continue
            job = jobs[step]
            if job.begun:
                self.forward(job)
            else:
                job.multiply(self.line)
                job.start(self.line)
            self.jobs.append(job)

    def forward(self, job):
        send, kept = job.split(job.terms[:-1] + [self.line.gate(job.terms[-1])])
        job.move(self.line.mark(send), kept)

    def pop(self):
        job = self.jobs.pop(0)
        if job.bits:
            self.forward(job)
            self.jobs.append(job)


def product_kernel(
    at_ref, left_ref, far_left_ref, right_ref, far_right_ref, send_ref, keep_ref,
    *, rows, cols, group, place,
):
    first = at_ref[0]

    def lefts(blocks):
        cut = lambda ref, js: jnp.concatenate(
            [ref[:, pl.ds(pl.multiple_of(j * rows, 128), rows)] for j in js], axis=1
        )
        return jnp.concatenate([cut(left_ref, blocks), cut(far_left_ref, blocks).astype(BF16)], axis=0)

    def rights(x):
        at = pl.ds(pl.multiple_of(x * cols, 128), cols)
        return jnp.concatenate([right_ref[:, at], far_right_ref[:, at].astype(BF16)], axis=0)

    dot = lambda a, b: lax.dot_general(
        a, b, (((0,), (0,)), ((), ())), preferred_element_type=F32
    )
    for out, value in ((send_ref, 1 - first), (keep_ref, first)):
        if place is None:
            out[0] = dot(lefts(list(range(group))), rights(value))
        else:
            low = 1 << place
            blocks = [(q // low) * 2 * low + q % low + value * low for q in range(group // 2)]
            left = lefts(blocks)
            for x in range(2):
                out[x, 0] = dot(left, rights(x))


class Partial(Blocks):
    def __init__(self, name, left, right):
        self.left, self.right = left, right
        self.bits = order_of(name)
        self.dims = axis_bits("batch")[1:] + axis_bits("seq")[::-1]
        self.blocks = lax.axis_size("seq")
        self.rows = left[0].shape[1] // self.blocks
        self.cols = right[0].shape[1] // 4

    def plain(self):
        half = self.right[0].shape[1] // 2
        own = lax.dynamic_slice_in_dim(self.right[0], bit_value(CORE) * half, half, 1)
        dot = lambda a, b: lax.dot_general(
            a.astype(BF16), b.astype(BF16), (((0,), (0,)), ((), ())), preferred_element_type=F32
        )
        whole = dot(self.left[0], own) + dot(self.left[1], self.right[1])
        lead = (2,) * len(axis_bits("seq"))
        whole = jnp.moveaxis(whole.reshape(*lead, self.rows, 2, self.cols), -2, 0)
        dim, bit = self.dims.index(self.bits[0]), bit_value(self.bits[0])
        return pick(whole, 1 - bit, dim), pick(whole, bit, dim)

    def kernel(self):
        rows, cols, tokens = self.rows, self.cols, self.left[0].shape[0]
        first = self.bits[0]
        place = first[1] if first[0] == "seq" else None
        group = 4
        steps = self.blocks // group
        if place is None:
            block, shape = (1, group * rows, cols), (steps, group * rows, cols)
            out_index = lambda i, at: (i, 0, 0)
        else:
            block, shape = (2, 1, group // 2 * rows, cols), (2, steps, group // 2 * rows, cols)
            out_index = lambda i, at: (0, i, 0, 0)
        out = jax.ShapeDtypeStruct(shape, F32)
        at = jnp.stack([bit_value(first), bit_value(CORE)]).astype(jnp.int32)
        send, kept = pl.pallas_call(
            functools.partial(
                product_kernel, rows=rows, cols=cols, group=group, place=place
            ),
            grid_spec=pltpu.PrefetchScalarGridSpec(
                num_scalar_prefetch=1,
                grid=(steps,),
                in_specs=[
                    pl.BlockSpec((tokens, group * rows), lambda i, at: (0, i)),
                    pl.BlockSpec((tokens, group * rows), lambda i, at: (0, i)),
                    pl.BlockSpec((tokens, 2 * cols), lambda i, at: (0, at[1])),
                    pl.BlockSpec((tokens, 2 * cols), lambda i, at: (0, 0)),
                ],
                out_specs=[pl.BlockSpec(block, out_index)] * 2,
            ),
            out_shape=[out, out],
            compiler_params=scan_params(),
            cost_estimate=pl.CostEstimate(
                flops=8 * tokens * self.blocks * rows * cols,
                bytes_accessed=8 * self.blocks * rows * cols,
                transcendentals=0,
            ),
        )(at, self.left[0], self.left[1], self.right[0], self.right[1])
        lead = (2,) * (len(self.dims) - 1)
        return send.reshape(*lead, rows, cols), kept.reshape(*lead, rows, cols)

    def multiply(self, line):
        self.left = (line.gate(self.left[0]), self.left[1])
        aligned = self.rows % 128 == 0 and self.blocks % 4 == 0 and len(axis_bits("batch")) == 2
        self.send, self.kept = self.kernel() if aligned else self.plain()
        line.mark(self.send)
        return self

    def start(self, line):
        self.move(line.gate(self.send), [self.kept])


class Vectors(Blocks):
    def __init__(self, vectors):
        count, seq = vectors.shape[0], lax.axis_size("seq")
        self.dims = axis_bits("seq")[::-1]
        self.bits = axis_bits("batch") + axis_bits("seq")
        value = jnp.swapaxes(vectors.reshape(count, seq, -1), 0, 1)
        self.terms = [value.reshape(*((2,) * len(self.dims)), count, -1)]

def in_order(own, other, bit, axis):
    first = bit_value(bit) == 0
    return jnp.concatenate(
        [jnp.where(first, own, other), jnp.where(first, other, own)], axis=axis
    )


def gather(line, value_part, key_part, parts):
    own = line.mark(jnp.stack([total_of(p.terms[:-1] + [line.gate(p.terms[-1])]) for p in parts]))
    other = exchange(own, CROSS)
    value = in_order(*value_part.terms, CROSS, 0)
    value = in_order(value, exchange(value, CORE), CORE, 0)
    seq = lax.axis_size("seq")
    halves = [t.reshape(seq, 1, -1, t.shape[-1]) for t in key_part.terms]
    key = in_order(*halves, CROSS, 1)
    key = in_order(key, exchange(key, CORE), CORE, 1)
    own = in_order(own, other, CROSS, 2)
    own = in_order(own, exchange(own, CORE), CORE, 2)
    return value, jnp.transpose(key.reshape(-1, key.shape[-1])), *[own[i] for i in range(len(parts))]


def entering(tails, begins, decay_rate, group_len, backward):
    count, mine = lax.axis_size("seq"), lax.axis_index("seq")
    sign = -1 if backward else 1

    def gain(lo, hi):
        a, b = (mine + lo, mine + hi) if backward else (mine - hi + 1, mine - lo + 1)
        hit = jnp.any((begins >= a * group_len) & (begins < b * group_len), axis=1, keepdims=True)
        return jnp.where(hit, 0.0, 1.0) * jnp.exp(-float((hi - lo) * group_len) * decay_rate)[None, :]

    reach, window, before = 1, tails, None
    while reach < count:
        got = [
            (j, shifted(window, "seq", sign * j * reach)) for j in range(1, 4) if j * reach < count
        ]
        if before is None:
            before = total_of([v if j == 1 else gain(1, j) * v for j, v in got])
            seen = 1 + len(got)
            window = tails + gain(0, 1) * before if seen < count else None
        else:
            before_more = total_of([gain(1, j * reach) * v for j, v in got])
            seen = reach * (1 + len(got))
            if seen < count:
                window = window + total_of([gain(0, j * reach) * v for j, v in got])
            before = before + before_more
        reach *= 4
    return before


def scan_params():
    return pltpu.CompilerParams(vmem_limit_bytes=48 * 1024 * 1024)


def lane_tiles(width):
    return [slice(i, i + 128) for i in range(0, width, 128)]


WINDOW = {name: k for k, name in enumerate(("keep", "one", "two", "four", "group", "eight", "end"))}


def keep_windows(starts, width):
    rows, length = starts.shape
    count = jnp.cumsum(starts.astype(jnp.int32), axis=1)
    before = jnp.concatenate([jnp.zeros((rows, 1), jnp.int32), count], axis=1)
    place = jnp.arange(length, dtype=jnp.int32)
    inner = place % 8
    ended = lambda t: jnp.pad(before, ((0, 0), (8, 8)), mode="edge")[:, 8 + t : 8 + t + length]
    here, after = ended(0), ended(1)
    groups = before[:, : length + 1 : 8]
    first = jnp.repeat(groups[:, :-1], 8, axis=1)
    last = jnp.repeat(groups[:, 1:], 8, axis=1)
    ahead = [
        after == here,
        *[(after == ended(1 - n)) & (inner >= n) for n in (1, 2, 4)],
        after == first,
        (after == ended(-7)) & (place >= 8),
        after == before[:, -1:],
    ]
    back = [
        after == here,
        *[(ended(n) == here) & (inner <= 7 - n) for n in (1, 2, 4)],
        last == here,
        (ended(8) == here) & (place < length - 8),
        here == 0,
    ]
    wide = lambda w: jnp.broadcast_to(jnp.stack(w).astype(F32)[..., None], (7, rows, length, width))
    return wide(ahead), wide(back)


def powers(rate_ref, tiles):
    return lambda n: [jnp.exp(-n * rate_ref[0:1, t]) for t in tiles]


def inner_place(shape=(8, 128)):
    return lax.broadcasted_iota(jnp.int32, shape, 0)


def spread(row):
    return jnp.broadcast_to(row, (8, 128))


def in_group(value, factors, back):
    for n, factor in zip((1, 2, 4), factors):
        value = value + factor * pltpu.roll(value, 8 - n if back else n, 0)
    return value


def halves_of(ref, row, at, tile):
    value = ref[row, at, tile]
    return value[:8], value[8:]


def windows_at(win_ref, row, at):
    names = ("keep", "one", "two", "four", "group")
    return [dict(zip(names, v)) for v in zip(*[halves_of(win_ref.at[WINDOW[n]], row, at, slice(None)) for n in names])]


def pair_at(p):
    return pl.ds(pl.multiple_of(p * 16, 16), 16)


def forward_tails_kernel(k_ref, v_ref, win_ref, rate_ref, tail_ref):
    rows, length, width = k_ref.shape
    tiles = lane_tiles(width)
    chains = [(r, i, t) for r in range(rows) for i, t in enumerate(tiles)]
    eight = powers(rate_ref, tiles)(8.0)

    def step(p, carry):
        at, out = pair_at(p), []
        windows = [halves_of(win_ref.at[WINDOW["eight"]], r, at, slice(None)) for r in range(rows)]
        for (r, i, t), (num, den) in zip(chains, carry):
            for h, (key, value) in enumerate(zip(halves_of(k_ref, r, at, t), halves_of(v_ref, r, at, t))):
                factor, e = windows[r][h] * eight[i], jnp.exp(key)
                num, den = factor * num + e * value, factor * den + e
            out.append((num, den))
        return tuple(out)

    zero = jnp.zeros((8, 128), F32)
    done = lax.fori_loop(0, length // 16, step, tuple((zero, zero) for _ in chains), unroll=2)
    left = powers(rate_ref, tiles)((7 - inner_place()).astype(F32))
    for (r, i, t), pair in zip(chains, done):
        factor = win_ref[WINDOW["end"], r, pl.ds(length - 8, 8), :] * left[i]
        for q in range(2):
            tail_ref[q, r : r + 1, t] = jnp.sum(factor * pair[q], axis=0, keepdims=True)


def forward_states_kernel(
    k_ref, v_ref, recep_ref, win_ref, rate_ref, bonus_ref, enter_ref, num_ref, den_ref, gated_ref
):
    rows, length, width = k_ref.shape
    tiles = lane_tiles(width)
    chains = [(r, i, t) for r in range(rows) for i, t in enumerate(tiles)]
    power = powers(rate_ref, tiles)
    ones, twos, fours = power(1.0), power(2.0), power(4.0)
    groups = power((1 + inner_place()).astype(F32))
    head = inner_place() == 0

    def step(p, carry):
        at, out = pair_at(p), []
        windows = [windows_at(win_ref, r, at) for r in range(rows)]
        for (r, i, t), states in zip(chains, carry):
            keys, values = halves_of(k_ref, r, at, t), halves_of(v_ref, r, at, t)
            receps, bonus, results = halves_of(recep_ref, r, at, t), bonus_ref[0:1, t], []
            for h in range(2):
                w = windows[r][h]
                factors = (w["one"] * ones[i], w["two"] * twos[i], w["four"] * fours[i])
                group = w["group"] * groups[i]
                e, held, here = jnp.exp(keys[h]), [], []
                for state, item in zip(states, (e * values[h], e)):
                    full = in_group(item, factors, False) + group * state
                    here.append(w["keep"] * jnp.where(head, state, pltpu.roll(full, 1, 0)))
                    held.append(spread(full[7:8]))
                states = held
                first = jnp.exp(bonus + keys[h])
                wkv = (here[0] + first * values[h]) / (here[1] + first)
                results.append((*here, jax.nn.sigmoid(receps[h]) * wkv))
            for ref, two in zip((num_ref, den_ref, gated_ref), zip(*results)):
                ref[r, at, t] = jnp.concatenate(two, axis=0).astype(ref.dtype)
            out.append(tuple(states))
        return tuple(out)

    start = tuple(tuple(spread(enter_ref[q, r : r + 1, t]) for q in range(2)) for r, _, t in chains)
    lax.fori_loop(0, length // 16, step, start)


def backward_tails_kernel(
    grad_ref, k_ref, v_ref, recep_ref, num_ref, den_ref, win_ref, rate_ref, bonus_ref,
    gnum_ref, gden_ref, grecep_ref, tail_ref,
):
    rows, length, width = k_ref.shape
    tiles = lane_tiles(width)
    chains = [(r, i, t) for r in range(rows) for i, t in enumerate(tiles)]
    eight = powers(rate_ref, tiles)(8.0)
    pairs = length // 16

    def step(p, carry):
        at, out = pair_at(pairs - 1 - p), []
        keeps = [halves_of(win_ref.at[WINDOW["keep"]], r, at, slice(None)) for r in range(rows)]
        windows = [halves_of(win_ref.at[WINDOW["eight"]], r, at, slice(None)) for r in range(rows)]
        for (r, i, t), (late_num, late_den) in zip(chains, carry):
            key, value = k_ref[r, at, t], v_ref[r, at, t]
            first = jnp.exp(bonus_ref[0:1, t] + key)
            below = den_ref[r, at, t] + first
            wkv = (num_ref[r, at, t] + first * value) / below
            gate, grad = jax.nn.sigmoid(recep_ref[r, at, t]), grad_ref[r, at, t]
            grecep_ref[r, at, t] = (grad * wkv * (gate * (1.0 - gate))).astype(BF16)
            up = grad * gate / below
            low = -up * wkv
            gnum_ref[r, at, t] = up
            gden_ref[r, at, t] = low
            for h in (1, 0):
                rows_of = slice(8 * h, 8 * h + 8)
                factor, keep = windows[r][h] * eight[i], keeps[r][h]
                late_num = factor * late_num + keep * up[rows_of]
                late_den = factor * late_den + keep * low[rows_of]
            out.append((late_num, late_den))
        return tuple(out)

    zero = jnp.zeros((8, 128), F32)
    done = lax.fori_loop(0, pairs, step, tuple((zero, zero) for _ in chains))
    left = powers(rate_ref, tiles)(inner_place().astype(F32))
    for (r, i, t), pair in zip(chains, done):
        factor = win_ref[WINDOW["end"], r, pl.ds(0, 8), :] * left[i]
        for q in range(2):
            tail_ref[q, r : r + 1, t] = jnp.sum(factor * pair[q], axis=0, keepdims=True)


def backward_states_kernel(
    gnum_ref, gden_ref, k_ref, v_ref, num_ref, den_ref, win_ref, rate_ref, bonus_ref, enter_ref,
    gkey_ref, gvalue_ref, sums_ref,
):
    rows, length, width = k_ref.shape
    tiles = lane_tiles(width)
    chains = [(r, i, t) for r in range(rows) for i, t in enumerate(tiles)]
    power = powers(rate_ref, tiles)
    ones, twos, fours = power(1.0), power(2.0), power(4.0)
    groups = power((8 - inner_place()).astype(F32))
    tail = inner_place() == 7
    pairs = length // 16

    def step(p, carry):
        at, out = pair_at(pairs - 1 - p), []
        windows = [windows_at(win_ref, r, at) for r in range(rows)]
        for (r, i, t), (num_state, den_state, slope, fade) in zip(chains, carry):
            states, parts = (num_state, den_state), []
            keys, values = halves_of(k_ref, r, at, t), halves_of(v_ref, r, at, t)
            ups, lows = halves_of(gnum_ref, r, at, t), halves_of(gden_ref, r, at, t)
            nums, dens = halves_of(num_ref, r, at, t), halves_of(den_ref, r, at, t)
            for h in (1, 0):
                w = windows[r][h]
                factors = (w["one"] * ones[i], w["two"] * twos[i], w["four"] * fours[i])
                group, held, here = w["group"] * groups[i], [], []
                for state, item in zip(states, (ups[h], lows[h])):
                    full = in_group(w["keep"] * item, factors, True) + group * state
                    here.append(jnp.where(tail, state, pltpu.roll(full, 7, 0)))
                    held.append(spread(full[0:1]))
                states = held
                e, first = jnp.exp(keys[h]), jnp.exp(bonus_ref[0:1, t] + keys[h])
                present = first * (ups[h] * values[h] + lows[h])
                slope = slope + present
                fade = fade + nums[h] * here[0] + dens[h] * here[1]
                parts.append(
                    (
                        present + e * (here[0] * values[h] + here[1]),
                        ups[h] * first + here[0] * e,
                    )
                )
            for ref, two in zip((gkey_ref, gvalue_ref), zip(*parts[::-1])):
                ref[r, at, t] = jnp.concatenate(two, axis=0).astype(BF16)
            out.append((*states, slope, fade))
        return tuple(out)

    zero = jnp.zeros((8, 128), F32)
    start = tuple(
        (*[spread(enter_ref[q, r : r + 1, t]) for q in range(2)], zero, zero) for r, _, t in chains
    )
    done = lax.fori_loop(0, pairs, step, start)
    for i, t in enumerate(tiles):
        for q in range(2):
            sums_ref[8 * q : 8 * q + 8, t] = total_of(
                [c[2 + q] for (_, j, _), c in zip(chains, done) if j == i]
            )


def scan_call(kernel, inputs, outputs, width=512):
    features = inputs[0].shape[-1]

    def spec(shape):
        lead = len(shape) - 1
        if shape[-1] == 128 and features != 128:
            return pl.BlockSpec(shape, lambda i: (0,) * (lead + 1))
        return pl.BlockSpec((*shape[:-1], width), lambda i: (0,) * lead + (i,))

    out_shape = [jax.ShapeDtypeStruct(s, d) for s, d in outputs]
    moved = sum(x.size * x.dtype.itemsize for x in [*inputs, *out_shape])
    return pl.pallas_call(
        kernel,
        out_shape=out_shape,
        grid=(features // width,),
        in_specs=[spec(x.shape) for x in inputs],
        out_specs=[spec(s) for s, _ in outputs],
        compiler_params=scan_params(),
        cost_estimate=pl.CostEstimate(
            flops=20 * inputs[0].size, bytes_accessed=moved, transcendentals=inputs[0].size
        ),
    )(*inputs)


def ahead_kernel(
    left_ref, recep_ref, up_ref, down_ref, gate_ref, after_ref, top_ref,
    above_ref, out_ref, fvalue_ref, frecep_ref, total_ref,
):
    above = jnp.maximum(jnp.dot(left_ref[...], up_ref[...], preferred_element_type=F32), 0.0)
    above_ref[...] = above
    part = jnp.dot((above * above).astype(BF16), down_ref[...], preferred_element_type=F32)
    step, last = pl.program_id(0), pl.num_programs(0) - 1

    @pl.when(step == 0)
    def _():
        total_ref[...] = part

    @pl.when((step > 0) & (step < last))
    def _():
        total_ref[...] += part

    @pl.when(step == last)
    def _():
        value = total_ref[...] + part
        gate = jax.nn.sigmoid(
            jnp.dot(recep_ref[...], gate_ref[...], preferred_element_type=F32)
        )
        top = top_ref[...].astype(F32)
        out_ref[...] = (after_ref[...] + gate * value).astype(BF16)
        fvalue_ref[...] = (top * gate).astype(BF16)
        frecep_ref[...] = (top * value * (gate * (1.0 - gate))).astype(BF16)


def back_kernel(fvalue_ref, frecep_ref, up_ref, down_ref, gate_ref, above_ref, fkey_ref, recep_ref):
    across = (((1,), (1,)), ((), ()))
    back = lax.dot_general(fvalue_ref[...], down_ref[...], across, preferred_element_type=F32)
    hidden = (back * (2.0 * above_ref[...])).astype(BF16)
    part = lax.dot_general(hidden, up_ref[...], across, preferred_element_type=F32)

    @pl.when(pl.program_id(0) == 0)
    def _():
        fkey_ref[...] = part
        recep_ref[...] = lax.dot_general(
            frecep_ref[...], gate_ref[...], across, preferred_element_type=F32
        )

    @pl.when(pl.program_id(0) > 0)
    def _():
        fkey_ref[...] += part


def channel_call(kernel, inputs, by_hidden, outputs, out_by_hidden, scratch, hidden):
    block = min(512, hidden)

    def spec(shape, dim):
        if dim is None:
            return pl.BlockSpec(shape, lambda i: (0, 0))
        return pl.BlockSpec(
            tuple(block if d == dim else n for d, n in enumerate(shape)),
            lambda i: tuple(i if d == dim else 0 for d in range(2)),
        )

    out_shape = [jax.ShapeDtypeStruct(s, d) for s, d in outputs]
    tokens, features = inputs[0].shape
    return pl.pallas_call(
        kernel,
        out_shape=out_shape,
        grid=(hidden // block,),
        in_specs=[spec(x.shape, dim) for x, dim in zip(inputs, by_hidden)],
        out_specs=[spec(x.shape, dim) for x, dim in zip(out_shape, out_by_hidden)],
        scratch_shapes=scratch,
        compiler_params=scan_params(),
        cost_estimate=pl.CostEstimate(
            flops=4 * tokens * features * (hidden + features // 2),
            bytes_accessed=sum(x.size * x.dtype.itemsize for x in [*inputs, *out_shape]),
            transcendentals=tokens * features,
        ),
    )(*inputs)


def norm_rows(value_rows, gain_vec, bias_vec):
    row_mean = jnp.mean(value_rows, axis=-1, keepdims=True)
    centred = value_rows - row_mean
    inv_std = lax.rsqrt(jnp.mean(centred * centred, axis=-1, keepdims=True) + 1e-05)
    normed = centred * inv_std
    return (normed * gain_vec + bias_vec, normed, inv_std)


def norm_back(grad_in, normed, inv_std, gain_vec):
    scaled = grad_in * gain_vec
    return inv_std * (
        scaled
        - jnp.mean(scaled, axis=-1, keepdims=True)
        - normed * jnp.mean(scaled * normed, axis=-1, keepdims=True)
    )


def project(left_side, right_side):
    return jnp.einsum("rcd,de->rce", left_side, right_side, preferred_element_type=F32)


def project_back(grad_in, right_side):
    return jnp.einsum("rce,de->rcd", grad_in, right_side, preferred_element_type=F32)


def with_previous(value_rows, edge_row, keep):
    earlier = jnp.concatenate([edge_row[:, None, :], value_rows[:, :-1, :]], axis=1)
    return earlier * keep[:, :, None]


def flat(value):
    return value.reshape(-1, value.shape[-1])


def shards(
    incoming_symbols,
    article_sizes,
    mixer_norm_scale,
    mixer_norm_offset,
    temporal_lookup_share,
    temporal_payload_share,
    temporal_gate_share,
    fading_log_rates,
    present_reward_vector,
    lookup_matrix,
    payload_matrix,
    gate_matrix,
    emission_matrix,
    channel_norm_scale,
    channel_norm_offset,
    channel_lookup_share,
    channel_gate_share,
    channel_lookup_matrix,
    channel_payload_matrix,
    channel_gate_matrix,
    final_cotangent,
):
    rows_here, group_len, features = incoming_symbols.shape
    full = (rows_here, group_len, features)
    begins = jnp.cumsum(article_sizes, axis=1) - article_sizes
    position = lax.axis_index("seq") * group_len + jnp.arange(group_len, dtype=jnp.int32)
    starts = jnp.any(position[None, :, None] == begins[:, None, :], axis=2)
    keep = jnp.where(starts, 0.0, 1.0).astype(F32)
    ahead_windows, back_windows = keep_windows(starts, 128)
    decay_rate = jnp.exp(fading_log_rates)
    rate_row = jnp.broadcast_to(decay_rate[None, :], (8, features))
    bonus_row = jnp.broadcast_to(present_reward_vector[None, :], (8, features))
    ready = article_sizes[0, 0] > 0
    enter = functools.partial(entering, begins=begins, decay_rate=decay_rate, group_len=group_len)

    symbols = incoming_symbols.astype(F32)
    att_last = norm_rows(symbols[:, -1, :], mixer_norm_scale, mixer_norm_offset)[0]
    att_edge = shifted(att_last, "seq", 1)
    att_normed, att_unit, att_inv = norm_rows(symbols, mixer_norm_scale, mixer_norm_offset)
    att_prev = with_previous(att_normed, att_edge, keep)
    mix = lambda share: (att_normed * share + att_prev * (1.0 - share)).astype(BF16)
    key_mixed = mix(temporal_lookup_share)
    value_mixed = mix(temporal_payload_share)
    recep_mixed = mix(temporal_gate_share)
    key_proj = project(key_mixed, lookup_matrix)
    value_proj = project(value_mixed, payload_matrix)
    recep_proj = project(recep_mixed, gate_matrix)
    tails = ((2, rows_here, features), F32)
    (tail,) = scan_call(
        forward_tails_kernel, [key_proj, value_proj, ahead_windows, rate_row], [tails]
    )
    key_mixed, value_mixed, recep_mixed = map(flat, (key_mixed, value_mixed, recep_mixed))
    state, key_far, value_far, recep_far = at_once(
        ready,
        lambda: (enter(tail, backward=False), *map(send_whole, (key_mixed, value_mixed, recep_mixed))),
    )
    key_side, value_side, recep_side = (
        (key_mixed, key_far), (value_mixed, value_far), (recep_mixed, recep_far)
    )
    num_state, den_state, gated = scan_call(
        forward_states_kernel,
        [key_proj, value_proj, recep_proj, ahead_windows, rate_row, bonus_row, state],
        [(full, F32), (full, F32), (full, BF16)],
    )
    after_att = symbols + project(gated, emission_matrix)

    ffn_normed, ffn_unit, ffn_inv = norm_rows(after_att, channel_norm_scale, channel_norm_offset)
    gated = flat(gated)
    last_rows = ffn_normed[:, -1, :]
    ffn_edge, gated_far = at_once(
        ready, lambda: (shifted(last_rows, "seq", 1), send_whole(gated))
    )
    gated_side = (gated, gated_far)
    ffn_prev = with_previous(ffn_normed, ffn_edge, keep)
    ffn_key_mixed = (
        ffn_normed * channel_lookup_share + ffn_prev * (1.0 - channel_lookup_share)
    ).astype(BF16)
    ffn_recep_mixed = (
        ffn_normed * channel_gate_share + ffn_prev * (1.0 - channel_gate_share)
    ).astype(BF16)
    line = Line()
    gate, mark = line.gate, line.mark
    fkey_far = send_across(flat(ffn_key_mixed))
    tokens, hidden = rows_here * group_len, channel_lookup_matrix.shape[1]
    flat_shape = (tokens, features)
    above, layer_out, grad_fvalue, grad_frecep = channel_call(
        ahead_kernel,
        [
            flat(ffn_key_mixed), flat(ffn_recep_mixed), channel_lookup_matrix,
            channel_payload_matrix, channel_gate_matrix, flat(after_att), flat(final_cotangent),
        ],
        (None, None, 1, 0, None, None, None),
        [((tokens, hidden), F32), (flat_shape, BF16), (flat_shape, BF16), (flat_shape, BF16)],
        (1, None, None, None),
        [pltpu.VMEM(flat_shape, F32)],
        hidden,
    )
    layer_out = layer_out.reshape(full)

    grad_top = final_cotangent.astype(F32)
    mark(grad_fvalue)
    fvalue_far = send_across(flat(grad_fvalue))
    grad_fkey_in, grad_frecep_in = channel_call(
        back_kernel,
        [grad_fvalue, grad_frecep, channel_lookup_matrix, channel_payload_matrix, channel_gate_matrix, above],
        (None, None, 1, 0, None, 1),
        [(flat_shape, F32), (flat_shape, F32)],
        (None, None),
        [],
        hidden,
    )
    grad_fkey_in, grad_frecep_in = grad_fkey_in.reshape(full), grad_frecep_in.reshape(full)
    ffn_delta = ffn_normed - ffn_prev
    grad_ffn_mix_key = jnp.sum(grad_fkey_in * ffn_delta, axis=(0, 1))
    grad_ffn_mix_recep = jnp.sum(grad_frecep_in * ffn_delta, axis=(0, 1))
    grad_ffn_prev = mark(
        (grad_fkey_in * (1.0 - channel_lookup_share) + grad_frecep_in * (1.0 - channel_gate_share))
        * keep[:, :, None]
    )
    first_row = gate(grad_ffn_prev[:, 0, :])
    ffn_back_edge, frecep_far, grad_frecep_far, fkey_cross = at_once(
        ready,
        lambda: (
            shifted(first_row, "seq", -1),
            send_whole(flat(ffn_recep_mixed)),
            send_half(flat(grad_frecep)),
            exchange(fkey_far[1], CORE),
        ),
    )
    mark(ffn_back_edge)
    grad_ffn_normed = (
        grad_fkey_in * channel_lookup_share
        + grad_frecep_in * channel_gate_share
        + jnp.concatenate([grad_ffn_prev[:, 1:, :], ffn_back_edge[:, None, :]], axis=1)
    )
    grad_ffn_ln_gain = jnp.sum(grad_ffn_normed * ffn_unit, axis=(0, 1))
    grad_ffn_ln_bias = jnp.sum(grad_ffn_normed, axis=(0, 1))
    grad_after = grad_top + norm_back(grad_ffn_normed, ffn_unit, ffn_inv, channel_norm_scale)

    grad_att_out = mark(grad_after.astype(BF16))
    grad_gated = project_back(gate(grad_att_out), emission_matrix)
    grad_num, grad_den, grad_recep, tail = scan_call(
        backward_tails_kernel,
        [grad_gated, key_proj, value_proj, recep_proj, num_state, den_state, back_windows, rate_row, bonus_row],
        [(full, F32), (full, F32), (full, BF16), tails],
    )
    gated_tail = gate(mark(tail))
    state, recep_out_far = at_once(
        ready,
        lambda: (
            enter(gated_tail, backward=True),
            send_half_of((flat(grad_recep), flat(grad_att_out))),
        ),
    )
    recep_far, out_far = recep_out_far
    mark(state)

    fr = Partial("FR", (flat(ffn_recep_mixed), frecep_far), (flat(grad_frecep), grad_frecep_far))
    ou = Partial("OU", (gated, gated_far), (flat(grad_att_out), out_far))
    ar = Partial("AR", recep_side, (flat(grad_recep), recep_far))
    queue = Queue(line)
    fvalue_cross = exchange(gate(fvalue_far[1]), CORE)
    fr.multiply(line)
    ar.multiply(line)
    ou.multiply(line)
    mark(fvalue_cross, ou.send)
    early = (fr, ou, ar)
    gated_left = gate(flat(ffn_key_mixed))

    def hidden_step():
        got = [exchange(job.send, job.bits[0]) for job in early]
        made = hidden_products(
            gated_left,
            (*fkey_far, fkey_cross),
            flat(grad_fvalue),
            (*fvalue_far, fvalue_cross),
            channel_lookup_matrix,
            channel_payload_matrix,
        )
        return *made, got

    value_blocks, key_blocks, arrived = at_once(ready, hidden_step)
    for job, got in zip(early, arrived):
        job.started(got)
    mark(key_blocks)
    big_value, big_key = Blocks("BV", value_blocks), Blocks("BK", key_blocks)
    queue.run(SEQUENCE[0], V=big_value, K=big_key, F=fr, O=ou, R=ar)
    grad_key, grad_value, sums = scan_call(
        backward_states_kernel,
        [grad_num, grad_den, key_proj, value_proj, num_state, den_state, back_windows, rate_row, bonus_row, gate(state)],
        [(full, BF16), (full, BF16), ((16, features), F32)],
    )
    mark(sums)
    reward_slope = jnp.sum(sums[:8], axis=0)
    grad_time_decay = -decay_rate * jnp.exp(-decay_rate) * jnp.sum(sums[8:], axis=0)
    queue.run(SEQUENCE[1], F=fr, O=ou, R=ar)

    gated_key = gate(grad_key)

    def back_att():
        return (
            send_half_of((flat(gated_key), flat(grad_value))),
            project_back(gated_key, lookup_matrix),
            project_back(grad_value, payload_matrix),
            project_back(grad_recep, gate_matrix),
        )

    (key_far, value_far), grad_key_in, grad_value_in, grad_recep_in = at_once(ready, back_att)
    mark(key_far)
    ak = Partial("AK", key_side, (flat(grad_key), key_far))
    av = Partial("AV", value_side, (flat(grad_value), value_far))
    queue.run(SEQUENCE[2], F=fr, O=ou, R=ar, A=ak, B=av)
    att_delta = att_normed - att_prev
    grad_mix_key = jnp.sum(grad_key_in * att_delta, axis=(0, 1))
    grad_mix_value = jnp.sum(grad_value_in * att_delta, axis=(0, 1))
    grad_mix_recep = jnp.sum(grad_recep_in * att_delta, axis=(0, 1))
    direct = (
        grad_key_in * temporal_lookup_share
        + grad_value_in * temporal_payload_share
        + grad_recep_in * temporal_gate_share
    )
    grad_att_prev = mark(
        (
            grad_key_in * (1.0 - temporal_lookup_share)
            + grad_value_in * (1.0 - temporal_payload_share)
            + grad_recep_in * (1.0 - temporal_gate_share)
        )
        * keep[:, :, None]
    )
    last_row = gate(grad_att_prev[:, 0, :])
    att_back_edge = mark(at_once(ready, lambda: shifted(last_row, "seq", -1)))
    grad_att_normed = direct + jnp.concatenate(
        [grad_att_prev[:, 1:, :], att_back_edge[:, None, :]], axis=1
    )
    grad_att_ln_gain = mark(jnp.sum(grad_att_normed * att_unit, axis=(0, 1)))
    grad_att_ln_bias = jnp.sum(grad_att_normed, axis=(0, 1))
    grad_tokens = (
        grad_after + norm_back(grad_att_normed, att_unit, att_inv, mixer_norm_scale)
    ).astype(BF16)
    vectors = Vectors(
        jnp.stack(
            [
                grad_att_ln_gain,
                grad_att_ln_bias,
                grad_mix_key,
                grad_mix_value,
                grad_mix_recep,
                grad_time_decay,
                reward_slope,
                grad_ffn_ln_gain,
                grad_ffn_ln_bias,
                grad_ffn_mix_key,
                grad_ffn_mix_recep,
            ]
        )
    )
    queue.run(SEQUENCE[3] + "X", F=fr, O=ou, R=ar, A=ak, B=av, X=vectors)
    while queue.jobs:
        queue.pop()
    value_sum, key_sum, fr_sum, ou_sum, ar_sum, ak_sum, av_sum = gather(
        line, big_value, big_key, [fr, ou, ar, ak, av]
    )
    small = total_of(vectors.terms)
    return (
        layer_out,
        grad_tokens,
        *[small[i] for i in range(7)],
        ak_sum,
        av_sum,
        ar_sum,
        ou_sum,
        *[small[i] for i in range(7, 11)],
        key_sum,
        value_sum,
        fr_sum,
    )


def solution(mesh):
    tokens = P("batch", "seq", None)
    vector, matrix = P("seq"), P("seq", None)
    return jax.shard_map(
        shards,
        mesh=mesh,
        in_specs=(tokens, P("batch", None), *([P()] * 18), tokens),
        out_specs=(tokens, tokens, *([vector] * 7), *([matrix] * 4), *([vector] * 4), *([matrix] * 3)),
        check_vma=False,
    )
```

```python
import functools
import math

import jax
import jax.numpy as jnp
from jax import lax
from jax.experimental import pallas as pl
from jax.experimental.pallas import tpu as pltpu
from jax.sharding import PartitionSpec as P

F32, BF16 = jnp.float32, jnp.bfloat16


def shifted(value, axis, distance):
    devices = range(lax.axis_size(axis))
    route = [(i - distance, i) for i in devices if i - distance in devices]
    return lax.ppermute(value, axis, route)


def bit_value(bit):
    axis, place = bit
    return (lax.axis_index(axis) >> place) & 1


def exchange(value, bit):
    axis, place = bit
    return lax.ppermute(value, axis, [(i, i ^ (1 << place)) for i in range(lax.axis_size(axis))])


def pick(value, index, dim):
    return lax.dynamic_index_in_dim(value, index, dim, keepdims=False)


def total_of(terms):
    return functools.reduce(lambda a, b: a + b, terms)


def axis_bits(axis):
    return [(axis, k) for k in range(int(math.log2(lax.axis_size(axis))))]


def at_once(ready, step, *values):
    blank = lambda *v: jax.tree.map(
        lambda x: jnp.zeros(x.shape, x.dtype), jax.eval_shape(step, *v)
    )
    return lax.cond(ready, step, blank, *values)


class Line:
    def __init__(self):
        self.token = None

    def gate(self, value):
        if self.token is None:
            return value
        return lax.optimization_barrier((value, self.token))[0]

    def mark(self, value, *others):
        self.token = (value, *others)
        return value


CORE = ("batch", 0)


def send_half(value):
    half = value.shape[1] // 2
    theirs = lax.dynamic_slice_in_dim(value, (1 - bit_value(CORE)) * half, half, 1)
    return exchange(theirs.astype(F32), CORE)


def send_half_of(values):
    half = values[0].shape[1] // 2
    at = (1 - bit_value(CORE)) * half
    theirs = [lax.dynamic_slice_in_dim(v, at, half, 1).astype(F32) for v in values]
    got = exchange(jnp.concatenate(theirs, axis=0), CORE)
    return jnp.split(got, len(values), axis=0)


def send_whole(value):
    return exchange(value.astype(F32), CORE)


CROSS = ("batch", 1)


def send_across(value):
    value = value.astype(F32)
    return exchange(value, CORE), exchange(value, CROSS)


def hidden_kernel(
    at_ref, *refs, unit,
):
    del at_ref
    lefts, grads, (up_a, up_b, down_a, down_b, value_ref, key_ref, left_all, grad_all) = (
        refs[:4], refs[4:8], refs[8:]
    )
    tokens = lefts[0].shape[0]

    @pl.when(pl.program_id(0) == 0)
    def _():
        for k in range(4):
            at = pl.ds(k * tokens, tokens)
            left_all[at, :] = lefts[k][...].astype(BF16)
            grad_all[at, :] = grads[k][...].astype(BF16)

    up = jnp.concatenate([up_a[...], up_b[...]], axis=1)
    down = jnp.concatenate([down_a[...], down_b[...]], axis=0)
    first = lambda a, b: lax.dot_general(a, b, (((0,), (0,)), ((), ())), preferred_element_type=F32)

    def products(k):
        at = pl.ds(k * 2 * tokens, 2 * tokens)
        left, grad = left_all[at, :], grad_all[at, :]
        above = jnp.maximum(jnp.dot(left, up, preferred_element_type=F32), 0.0)
        back = lax.dot_general(grad, down, (((1,), (1,)), ((), ())), preferred_element_type=F32)
        return first((above * above).astype(BF16), grad), first((back * (2.0 * above)).astype(BF16), left)

    def put(value, key, add):
        for half in range(2):
            part = value[half * unit : (half + 1) * unit]
            value_ref[half] = value_ref[half] + part if add else part
        rows = key.shape[1] // key_ref.shape[0]
        for s in range(key_ref.shape[0]):
            part = key[:, s * rows : (s + 1) * rows]
            key_ref[s] = key_ref[s] + part if add else part

    put(*products(0), False)
    put(*products(1), True)


def hidden_products(left, far_lefts, grad, far_grads, up, down):
    seq, tokens, features = lax.axis_size("seq"), left.shape[0], left.shape[1]
    unit = up.shape[1] // seq // 4
    quarter = 2 * bit_value(CORE) + bit_value(CROSS)
    out_shapes = (seq, unit, features), (seq, seq * unit, features // seq)
    if unit % 128 or features // seq % 128:
        up = pick(up.reshape(features, seq, 4, unit), quarter, 2).reshape(features, -1)
        down = pick(down.reshape(seq, 4, unit, features), quarter, 1).reshape(-1, features)
        lefts = jnp.concatenate([left, *[f.astype(BF16) for f in far_lefts]])
        grads = jnp.concatenate([grad, *[f.astype(BF16) for f in far_grads]])
        above = jnp.maximum(jnp.dot(lefts, up, preferred_element_type=F32), 0.0)
        back = lax.dot_general(grads, down, (((1,), (1,)), ((), ())), preferred_element_type=F32)
        first = lambda a, b: lax.dot_general(a, b, (((0,), (0,)), ((), ())), preferred_element_type=F32)
        value = first((above * above).astype(BF16), grads).reshape(out_shapes[0])
        key = first((back * (2.0 * above)).astype(BF16), lefts)
        return value, jnp.swapaxes(key.reshape(-1, seq, features // seq), 0, 1)
    whole = lambda: pl.BlockSpec((tokens, features), lambda i, at: (0, 0), pipeline_mode=pl.Buffered(1))
    ups = [pl.BlockSpec((features, unit), lambda i, at, h=h: (0, 4 * (2 * i + h) + at[0])) for h in (0, 1)]
    downs = [pl.BlockSpec((unit, features), lambda i, at, h=h: (4 * (2 * i + h) + at[0], 0)) for h in (0, 1)]
    return pl.pallas_call(
        functools.partial(hidden_kernel, unit=unit),
        grid_spec=pltpu.PrefetchScalarGridSpec(
            num_scalar_prefetch=1,
            grid=(seq // 2,),
            in_specs=[whole() for _ in range(8)] + ups + downs,
            out_specs=[
                pl.BlockSpec((2, unit, features), lambda i, at: (i, 0, 0)),
                pl.BlockSpec((seq, 2 * unit, features // seq), lambda i, at: (0, i, 0)),
            ],
            scratch_shapes=[pltpu.VMEM((4 * tokens, features), BF16)] * 2,
        ),
        out_shape=[jax.ShapeDtypeStruct(shape, F32) for shape in out_shapes],
        compiler_params=pltpu.CompilerParams(vmem_limit_bytes=56 * 1024 * 1024),
        cost_estimate=pl.CostEstimate(
            flops=32 * tokens * features * seq * unit,
            bytes_accessed=40 * tokens * features,
            transcendentals=0,
        ),
    )(quarter[None].astype(jnp.int32), left, *far_lefts, grad, *far_grads, up, up, down, down)


ORDERS = dict(BV="zywx", BK="yzwx", FR="xyzw", OU="zxyw", AR="yxzw", AK="xyzw", AV="xyzw")


def order_of(name):
    seq = axis_bits("seq")
    places = dict(x=axis_bits("batch")[1:], y=seq[:1], z=seq[1:2], w=seq[2:])
    return [places[letter] for letter in ORDERS[name]]


def halve(terms, dims, bit):
    if bit not in dims:
        total = total_of(terms)
        return total, [total]
    dim, mine = dims.index(bit), bit_value(bit)
    send = total_of([pick(t, 1 - mine, dim) for t in terms])
    return send, [pick(t, mine, dim) for t in terms]


class Blocks:
    halves = None

    def __init__(self, name, value, halves=None):
        self.hops, self.dims = order_of(name), axis_bits("seq")[::-1]
        self.halves, self.terms = halves, None
        if halves is None:
            self.terms = [value.reshape(*((2,) * len(self.dims)), *value.shape[1:])]

    def first(self):
        send, kept = self.split(self.terms)
        return send, kept[0]

    def split(self, terms):
        if self.halves:
            return self.halves[0], [self.halves[1]]
        return halve(terms, self.dims, self.hops[0][0])

    def go(self, sends):
        bits, dims = self.hops[0], list(self.dims)
        got = exchange(sends, bits[0])
        if len(bits) == 1:
            return got
        terms = self.split(self.terms)[1] + [got]
        dims = [d for d in dims if d != bits[0]]
        for bit in bits[1:]:
            send, kept = halve(terms, dims, bit)
            terms = kept + [exchange(send, bit)]
            dims = [d for d in dims if d != bit]
        return total_of(terms)

    def hop(self):
        return self.go(self.split(self.terms)[0])

    def landed(self, got):
        bits = self.hops[0]
        self.terms = self.split(self.terms)[1] + [got] if len(bits) == 1 else [got]
        self.halves = None
        self.dims = [d for d in self.dims if d not in bits]
        self.hops.pop(0)

    def arrived(self, line):
        return self.terms[:-1] + [line.gate(self.terms[-1])]

    def forward(self, line):
        if self.halves:
            send = line.gate(self.halves[0])
        else:
            send = self.split(self.arrived(line))[0]
        self.landed(self.go(line.mark(send)))


def phase(line, ready, jobs, beside=None):
    def step():
        return [job.hop() for job in jobs], beside() if beside else ()

    got, more = at_once(line.gate(ready), step)
    for job, value in zip(jobs, got):
        job.landed(value)
    line.mark(*jax.tree.leaves((got, more)))
    return more


def product_kernel(
    at_ref, left_ref, far_left_ref, right_ref, far_right_ref, send_ref, keep_ref,
    *, rows, cols, group, place,
):
    first = at_ref[0]

    def lefts(blocks):
        cut = lambda ref, js: jnp.concatenate(
            [ref[:, pl.ds(pl.multiple_of(j * rows, 128), rows)] for j in js], axis=1
        )
        return jnp.concatenate([cut(left_ref, blocks), cut(far_left_ref, blocks).astype(BF16)], axis=0)

    def rights(x):
        at = pl.ds(pl.multiple_of(x * cols, 128), cols)
        return jnp.concatenate([right_ref[:, at], far_right_ref[:, at].astype(BF16)], axis=0)

    dot = lambda a, b: lax.dot_general(
        a, b, (((0,), (0,)), ((), ())), preferred_element_type=F32
    )
    for out, value in ((send_ref, 1 - first), (keep_ref, first)):
        if place is None:
            out[0] = dot(lefts(list(range(group))), rights(value))
        else:
            low = 1 << place
            blocks = [(q // low) * 2 * low + q % low + value * low for q in range(group // 2)]
            left = lefts(blocks)
            for x in range(2):
                out[x, 0] = dot(left, rights(x))


class Partial(Blocks):
    def __init__(self, name, left, right):
        self.left, self.right = left, right
        self.hops, self.terms = order_of(name), None
        self.dims = axis_bits("batch")[1:] + axis_bits("seq")[::-1]
        self.blocks = lax.axis_size("seq")
        self.rows = left[0].shape[1] // self.blocks
        self.cols = right[0].shape[1] // 4

    def plain(self):
        half = self.right[0].shape[1] // 2
        own = lax.dynamic_slice_in_dim(self.right[0], bit_value(CORE) * half, half, 1)
        dot = lambda a, b: lax.dot_general(
            a.astype(BF16), b.astype(BF16), (((0,), (0,)), ((), ())), preferred_element_type=F32
        )
        whole = dot(self.left[0], own) + dot(self.left[1], self.right[1])
        lead = (2,) * len(axis_bits("seq"))
        whole = jnp.moveaxis(whole.reshape(*lead, self.rows, 2, self.cols), -2, 0)
        send, kept = halve([whole], self.dims, self.hops[0][0])
        return send, kept[0]

    def kernel(self):
        rows, cols, tokens = self.rows, self.cols, self.left[0].shape[0]
        first = self.hops[0][0]
        place = first[1] if first[0] == "seq" else None
        group = 4
        steps = self.blocks // group
        if place is None:
            block, shape = (1, group * rows, cols), (steps, group * rows, cols)
            out_index = lambda i, at: (i, 0, 0)
        else:
            block, shape = (2, 1, group // 2 * rows, cols), (2, steps, group // 2 * rows, cols)
            out_index = lambda i, at: (0, i, 0, 0)
        out = jax.ShapeDtypeStruct(shape, F32)
        at = jnp.stack([bit_value(first), bit_value(CORE)]).astype(jnp.int32)
        send, kept = pl.pallas_call(
            functools.partial(
                product_kernel, rows=rows, cols=cols, group=group, place=place
            ),
            grid_spec=pltpu.PrefetchScalarGridSpec(
                num_scalar_prefetch=1,
                grid=(steps,),
                in_specs=[
                    pl.BlockSpec((tokens, group * rows), lambda i, at: (0, i)),
                    pl.BlockSpec((tokens, group * rows), lambda i, at: (0, i)),
                    pl.BlockSpec((tokens, 2 * cols), lambda i, at: (0, at[1])),
                    pl.BlockSpec((tokens, 2 * cols), lambda i, at: (0, 0)),
                ],
                out_specs=[pl.BlockSpec(block, out_index)] * 2,
            ),
            out_shape=[out, out],
            compiler_params=scan_params(),
            cost_estimate=pl.CostEstimate(
                flops=8 * tokens * self.blocks * rows * cols,
                bytes_accessed=8 * self.blocks * rows * cols,
                transcendentals=0,
            ),
        )(at, self.left[0], self.left[1], self.right[0], self.right[1])
        lead = (2,) * (len(self.dims) - 1)
        return send.reshape(*lead, rows, cols), kept.reshape(*lead, rows, cols)

    def products(self):
        aligned = self.rows % 128 == 0 and self.blocks % 4 == 0 and len(axis_bits("batch")) == 2
        return self.kernel() if aligned else self.plain()

    def multiply(self, line):
        self.left = (line.gate(self.left[0]), self.left[1])
        self.halves = self.products()
        line.mark(self.halves[0])


class Stacked(Blocks):
    def __init__(self, line, jobs):
        self.hops, self.dims = list(jobs[0].hops), jobs[0].dims
        sums = [total_of(j.arrived(line)) for j in jobs]
        sums = [v if isinstance(j, Stacked) else v[..., None, :, :] for j, v in zip(jobs, sums)]
        self.terms = [jnp.concatenate(sums, axis=-3)]


class Vectors(Blocks):
    def __init__(self, vectors):
        vectors = jnp.pad(vectors, ((0, -vectors.shape[0] % 8), (0, 0)))
        count, seq = vectors.shape[0], lax.axis_size("seq")
        self.dims = axis_bits("seq")[::-1]
        bits = axis_bits("seq")
        self.hops = [[b] for b in axis_bits("batch") + bits[:1]] + [bits[1:]]
        value = jnp.swapaxes(vectors.reshape(count, seq, -1), 0, 1)
        self.terms = [value.reshape(*((2,) * len(self.dims)), count, -1)]

def in_order(own, other, bit, axis):
    first = bit_value(bit) == 0
    return jnp.concatenate(
        [jnp.where(first, own, other), jnp.where(first, other, own)], axis=axis
    )


def gather(own, beside=None):
    other, more = exchange(own, CROSS), None
    if beside:
        other, more = lax.optimization_barrier((other, beside()))
    own = in_order(own, other, CROSS, 2)
    own = in_order(own, exchange(own, CORE), CORE, 2)
    joined = [own[i] for i in range(own.shape[0])]
    return (joined, more) if beside else joined


def join_hidden(values, keys):
    seq = lax.axis_size("seq")
    value = in_order(*values, CROSS, 0)
    key = in_order(*[t.reshape(seq, 1, -1, t.shape[-1]) for t in keys], CROSS, 1)
    value = in_order(value, exchange(value, CORE), CORE, 0)
    key = in_order(key, exchange(key, CORE), CORE, 1)
    return value, jnp.transpose(key.reshape(-1, key.shape[-1]))


def entering(tails, begins, decay_rate, group_len, backward):
    count, mine = lax.axis_size("seq"), lax.axis_index("seq")
    sign = -1 if backward else 1

    def gain(lo, hi):
        a, b = (mine + lo, mine + hi) if backward else (mine - hi + 1, mine - lo + 1)
        hit = jnp.any((begins >= a * group_len) & (begins < b * group_len), axis=1, keepdims=True)
        return jnp.where(hit, 0.0, 1.0) * jnp.exp(-float((hi - lo) * group_len) * decay_rate)[None, :]

    reach, window, before = 1, tails, None
    while reach < count:
        got = [
            (j, shifted(window, "seq", sign * j * reach)) for j in range(1, 4) if j * reach < count
        ]
        if before is None:
            before = total_of([v if j == 1 else gain(1, j) * v for j, v in got])
            seen = 1 + len(got)
            window = tails + gain(0, 1) * before if seen < count else None
        else:
            before_more = total_of([gain(1, j * reach) * v for j, v in got])
            seen = reach * (1 + len(got))
            if seen < count:
                window = window + total_of([gain(0, j * reach) * v for j, v in got])
            before = before + before_more
        reach *= 4
    return before


def scan_params():
    return pltpu.CompilerParams(vmem_limit_bytes=48 * 1024 * 1024)


def lane_tiles(width):
    return [slice(i, i + 128) for i in range(0, width, 128)]


WINDOW = {name: k for k, name in enumerate(("keep", "one", "two", "four", "group", "eight", "end"))}


def windows_kernel(sizes_ref, block_ref, ahead_ref, back_ref):
    rows, length, width = ahead_ref.shape[1:]
    t = lax.broadcasted_iota(jnp.int32, (length, width), 0)
    inner = t & 7

    def put(ref, name, equal, inside=None):
        kept = equal if inside is None else equal & inside
        ref[WINDOW[name], row] = jnp.where(kept, 1.0, 0.0)

    for row in range(rows):
        begins, at = [], -block_ref[0]
        for j in range(sizes_ref.shape[1]):
            begins.append(at)
            at = at + sizes_ref[row, j]

        def begun(by):
            return total_of([jnp.where(by >= b, 1, 0) for b in begins])

        here, ahead_of = begun(t), begun(t - 1)
        keep = here == ahead_of
        put(ahead_ref, "keep", keep)
        put(back_ref, "keep", keep)
        for name, n in (("one", 1), ("two", 2), ("four", 4)):
            put(ahead_ref, name, here == begun(t - n), inner >= n)
            put(back_ref, name, begun(t + (n - 1)) == ahead_of, inner <= 7 - n)
        put(ahead_ref, "group", here == begun(t - inner - 1))
        put(back_ref, "group", begun(t - inner + 7) == ahead_of)
        put(ahead_ref, "eight", here == begun(t - 8), t >= 8)
        put(back_ref, "eight", begun(t + 7) == ahead_of, t < length - 8)
        put(ahead_ref, "end", here == begun(jnp.full_like(t, length - 1)))
        put(back_ref, "end", ahead_of == begun(jnp.full_like(t, -1)))


def keep_windows(sizes, length, width):
    block = (lax.axis_index("seq") * length)[None].astype(jnp.int32)
    out = jax.ShapeDtypeStruct((len(WINDOW), sizes.shape[0], length, width), F32)
    return pl.pallas_call(
        windows_kernel,
        out_shape=[out, out],
        in_specs=[pl.BlockSpec(memory_space=pltpu.SMEM)] * 2,
        compiler_params=scan_params(),
        cost_estimate=pl.CostEstimate(flops=100 * out.size, bytes_accessed=8 * out.size, transcendentals=0),
    )(sizes, block)


def powers(rate_ref, tiles):
    return lambda n: [jnp.exp(-n * rate_ref[0:1, t]) for t in tiles]


def inner_place(shape=(8, 128)):
    return lax.broadcasted_iota(jnp.int32, shape, 0)


def spread(row):
    return jnp.broadcast_to(row, (8, 128))


def in_group(value, factors, back):
    for n, factor in zip((1, 2, 4), factors):
        value = value + factor * pltpu.roll(value, 8 - n if back else n, 0)
    return value


def halves_of(ref, row, at, tile):
    value = ref[row, at, tile]
    return value[:8], value[8:]


def windows_at(win_ref, row, at):
    names = ("keep", "one", "two", "four", "group")
    return [dict(zip(names, v)) for v in zip(*[halves_of(win_ref.at[WINDOW[n]], row, at, slice(None)) for n in names])]


def pair_at(p):
    return pl.ds(pl.multiple_of(p * 16, 16), 16)


def forward_tails_kernel(k_ref, v_ref, win_ref, rate_ref, tail_ref):
    rows, length, width = k_ref.shape
    tiles = lane_tiles(width)
    chains = [(r, i, t) for r in range(rows) for i, t in enumerate(tiles)]
    eight = powers(rate_ref, tiles)(8.0)

    def step(p, carry):
        at, out = pair_at(p), []
        windows = [halves_of(win_ref.at[WINDOW["eight"]], r, at, slice(None)) for r in range(rows)]
        for (r, i, t), (num, den) in zip(chains, carry):
            for h, (key, value) in enumerate(zip(halves_of(k_ref, r, at, t), halves_of(v_ref, r, at, t))):
                factor, e = windows[r][h] * eight[i], jnp.exp(key)
                num, den = factor * num + e * value, factor * den + e
            out.append((num, den))
        return tuple(out)

    zero = jnp.zeros((8, 128), F32)
    done = lax.fori_loop(0, length // 16, step, tuple((zero, zero) for _ in chains), unroll=2)
    left = powers(rate_ref, tiles)((7 - inner_place()).astype(F32))
    for (r, i, t), pair in zip(chains, done):
        factor = win_ref[WINDOW["end"], r, pl.ds(length - 8, 8), :] * left[i]
        for q in range(2):
            tail_ref[q, r : r + 1, t] = jnp.sum(factor * pair[q], axis=0, keepdims=True)


def forward_states_kernel(
    k_ref, v_ref, recep_ref, win_ref, rate_ref, bonus_ref, enter_ref, num_ref, den_ref, gated_ref
):
    rows, length, width = k_ref.shape
    tiles = lane_tiles(width)
    chains = [(r, i, t) for r in range(rows) for i, t in enumerate(tiles)]
    power = powers(rate_ref, tiles)
    ones, twos, fours = power(1.0), power(2.0), power(4.0)
    groups = power((1 + inner_place()).astype(F32))
    head = inner_place() == 0

    def step(p, carry):
        at, out = pair_at(p), []
        windows = [windows_at(win_ref, r, at) for r in range(rows)]
        for (r, i, t), states in zip(chains, carry):
            keys, values = halves_of(k_ref, r, at, t), halves_of(v_ref, r, at, t)
            receps, bonus, results = halves_of(recep_ref, r, at, t), bonus_ref[0:1, t], []
            for h in range(2):
                w = windows[r][h]
                factors = (w["one"] * ones[i], w["two"] * twos[i], w["four"] * fours[i])
                group = w["group"] * groups[i]
                e, held, here = jnp.exp(keys[h]), [], []
                for state, item in zip(states, (e * values[h], e)):
                    full = in_group(item, factors, False) + group * state
                    here.append(w["keep"] * jnp.where(head, state, pltpu.roll(full, 1, 0)))
                    held.append(spread(full[7:8]))
                states = held
                first = jnp.exp(bonus + keys[h])
                wkv = (here[0] + first * values[h]) / (here[1] + first)
                results.append((*here, jax.nn.sigmoid(receps[h]) * wkv))
            for ref, two in zip((num_ref, den_ref, gated_ref), zip(*results)):
                ref[r, at, t] = jnp.concatenate(two, axis=0).astype(ref.dtype)
            out.append(tuple(states))
        return tuple(out)

    start = tuple(tuple(spread(enter_ref[q, r : r + 1, t]) for q in range(2)) for r, _, t in chains)
    lax.fori_loop(0, length // 16, step, start)


def backward_tails_kernel(
    grad_ref, k_ref, v_ref, recep_ref, num_ref, den_ref, win_ref, rate_ref, bonus_ref,
    gnum_ref, gden_ref, grecep_ref, tail_ref,
):
    rows, length, width = k_ref.shape
    tiles = lane_tiles(width)
    chains = [(r, i, t) for r in range(rows) for i, t in enumerate(tiles)]
    eight = powers(rate_ref, tiles)(8.0)
    pairs = length // 16

    def step(p, carry):
        at, out = pair_at(pairs - 1 - p), []
        keeps = [halves_of(win_ref.at[WINDOW["keep"]], r, at, slice(None)) for r in range(rows)]
        windows = [halves_of(win_ref.at[WINDOW["eight"]], r, at, slice(None)) for r in range(rows)]
        for (r, i, t), (late_num, late_den) in zip(chains, carry):
            key, value = k_ref[r, at, t], v_ref[r, at, t]
            first = jnp.exp(bonus_ref[0:1, t] + key)
            below = den_ref[r, at, t] + first
            wkv = (num_ref[r, at, t] + first * value) / below
            gate, grad = jax.nn.sigmoid(recep_ref[r, at, t]), grad_ref[r, at, t]
            grecep_ref[r, at, t] = (grad * wkv * (gate * (1.0 - gate))).astype(BF16)
            up = grad * gate / below
            low = -up * wkv
            gnum_ref[r, at, t] = up
            gden_ref[r, at, t] = low
            for h in (1, 0):
                rows_of = slice(8 * h, 8 * h + 8)
                factor, keep = windows[r][h] * eight[i], keeps[r][h]
                late_num = factor * late_num + keep * up[rows_of]
                late_den = factor * late_den + keep * low[rows_of]
            out.append((late_num, late_den))
        return tuple(out)

    zero = jnp.zeros((8, 128), F32)
    done = lax.fori_loop(0, pairs, step, tuple((zero, zero) for _ in chains))
    left = powers(rate_ref, tiles)(inner_place().astype(F32))
    for (r, i, t), pair in zip(chains, done):
        factor = win_ref[WINDOW["end"], r, pl.ds(0, 8), :] * left[i]
        for q in range(2):
            tail_ref[q, r : r + 1, t] = jnp.sum(factor * pair[q], axis=0, keepdims=True)


def backward_states_kernel(
    gnum_ref, gden_ref, k_ref, v_ref, num_ref, den_ref, win_ref, rate_ref, bonus_ref, enter_ref,
    gkey_ref, gvalue_ref, sums_ref,
):
    rows, length, width = k_ref.shape
    tiles = lane_tiles(width)
    chains = [(r, i, t) for r in range(rows) for i, t in enumerate(tiles)]
    power = powers(rate_ref, tiles)
    ones, twos, fours = power(1.0), power(2.0), power(4.0)
    groups = power((8 - inner_place()).astype(F32))
    tail = inner_place() == 7
    pairs = length // 16

    def step(p, carry):
        at, out = pair_at(pairs - 1 - p), []
        windows = [windows_at(win_ref, r, at) for r in range(rows)]
        for (r, i, t), (num_state, den_state, slope, fade) in zip(chains, carry):
            states, parts = (num_state, den_state), []
            keys, values = halves_of(k_ref, r, at, t), halves_of(v_ref, r, at, t)
            ups, lows = halves_of(gnum_ref, r, at, t), halves_of(gden_ref, r, at, t)
            nums, dens = halves_of(num_ref, r, at, t), halves_of(den_ref, r, at, t)
            for h in (1, 0):
                w = windows[r][h]
                factors = (w["one"] * ones[i], w["two"] * twos[i], w["four"] * fours[i])
                group, held, here = w["group"] * groups[i], [], []
                for state, item in zip(states, (ups[h], lows[h])):
                    full = in_group(w["keep"] * item, factors, True) + group * state
                    here.append(jnp.where(tail, state, pltpu.roll(full, 7, 0)))
                    held.append(spread(full[0:1]))
                states = held
                e, first = jnp.exp(keys[h]), jnp.exp(bonus_ref[0:1, t] + keys[h])
                present = first * (ups[h] * values[h] + lows[h])
                slope = slope + present
                fade = fade + nums[h] * here[0] + dens[h] * here[1]
                parts.append(
                    (
                        present + e * (here[0] * values[h] + here[1]),
                        ups[h] * first + here[0] * e,
                    )
                )
            for ref, two in zip((gkey_ref, gvalue_ref), zip(*parts[::-1])):
                ref[r, at, t] = jnp.concatenate(two, axis=0).astype(BF16)
            out.append((*states, slope, fade))
        return tuple(out)

    zero = jnp.zeros((8, 128), F32)
    start = tuple(
        (*[spread(enter_ref[q, r : r + 1, t]) for q in range(2)], zero, zero) for r, _, t in chains
    )
    done = lax.fori_loop(0, pairs, step, start)
    for i, t in enumerate(tiles):
        for q in range(2):
            sums_ref[8 * q : 8 * q + 8, t] = total_of(
                [c[2 + q] for (_, j, _), c in zip(chains, done) if j == i]
            )


def scan_call(kernel, inputs, outputs, width=512):
    features = inputs[0].shape[-1]

    def spec(shape):
        lead = len(shape) - 1
        if shape[-1] == 128 and features != 128:
            return pl.BlockSpec(shape, lambda i: (0,) * (lead + 1))
        return pl.BlockSpec((*shape[:-1], width), lambda i: (0,) * lead + (i,))

    out_shape = [jax.ShapeDtypeStruct(s, d) for s, d in outputs]
    moved = sum(x.size * x.dtype.itemsize for x in [*inputs, *out_shape])
    return pl.pallas_call(
        kernel,
        out_shape=out_shape,
        grid=(features // width,),
        in_specs=[spec(x.shape) for x in inputs],
        out_specs=[spec(s) for s, _ in outputs],
        compiler_params=scan_params(),
        cost_estimate=pl.CostEstimate(
            flops=20 * inputs[0].size, bytes_accessed=moved, transcendentals=inputs[0].size
        ),
    )(*inputs)


def ahead_kernel(
    left_ref, recep_ref, up_ref, down_ref, gate_ref, after_ref, top_ref,
    above_ref, out_ref, fvalue_ref, frecep_ref, total_ref,
):
    above = jnp.maximum(jnp.dot(left_ref[...], up_ref[...], preferred_element_type=F32), 0.0)
    above_ref[...] = above
    part = jnp.dot((above * above).astype(BF16), down_ref[...], preferred_element_type=F32)
    step, last = pl.program_id(0), pl.num_programs(0) - 1

    @pl.when(step == 0)
    def _():
        total_ref[...] = part

    @pl.when((step > 0) & (step < last))
    def _():
        total_ref[...] += part

    @pl.when(step == last)
    def _():
        value = total_ref[...] + part
        gate = jax.nn.sigmoid(
            jnp.dot(recep_ref[...], gate_ref[...], preferred_element_type=F32)
        )
        top = top_ref[...].astype(F32)
        out_ref[...] = (after_ref[...] + gate * value).astype(BF16)
        fvalue_ref[...] = (top * gate).astype(BF16)
        frecep_ref[...] = (top * value * (gate * (1.0 - gate))).astype(BF16)


def back_kernel(fvalue_ref, frecep_ref, up_ref, down_ref, gate_ref, above_ref, fkey_ref, recep_ref):
    across = (((1,), (1,)), ((), ()))
    back = lax.dot_general(fvalue_ref[...], down_ref[...], across, preferred_element_type=F32)
    hidden = (back * (2.0 * above_ref[...])).astype(BF16)
    part = lax.dot_general(hidden, up_ref[...], across, preferred_element_type=F32)

    @pl.when(pl.program_id(0) == 0)
    def _():
        fkey_ref[...] = part
        recep_ref[...] = lax.dot_general(
            frecep_ref[...], gate_ref[...], across, preferred_element_type=F32
        )

    @pl.when(pl.program_id(0) > 0)
    def _():
        fkey_ref[...] += part


def channel_call(kernel, inputs, by_hidden, outputs, out_by_hidden, scratch, hidden):
    block = min(512, hidden)

    def spec(shape, dim):
        if dim is None:
            return pl.BlockSpec(shape, lambda i: (0, 0))
        return pl.BlockSpec(
            tuple(block if d == dim else n for d, n in enumerate(shape)),
            lambda i: tuple(i if d == dim else 0 for d in range(2)),
        )

    out_shape = [jax.ShapeDtypeStruct(s, d) for s, d in outputs]
    tokens, features = inputs[0].shape
    return pl.pallas_call(
        kernel,
        out_shape=out_shape,
        grid=(hidden // block,),
        in_specs=[spec(x.shape, dim) for x, dim in zip(inputs, by_hidden)],
        out_specs=[spec(x.shape, dim) for x, dim in zip(out_shape, out_by_hidden)],
        scratch_shapes=scratch,
        compiler_params=scan_params(),
        cost_estimate=pl.CostEstimate(
            flops=4 * tokens * features * (hidden + features // 2),
            bytes_accessed=sum(x.size * x.dtype.itemsize for x in [*inputs, *out_shape]),
            transcendentals=tokens * features,
        ),
    )(*inputs)


def norm_rows(value_rows, gain_vec, bias_vec):
    row_mean = jnp.mean(value_rows, axis=-1, keepdims=True)
    centred = value_rows - row_mean
    inv_std = lax.rsqrt(jnp.mean(centred * centred, axis=-1, keepdims=True) + 1e-05)
    normed = centred * inv_std
    return (normed * gain_vec + bias_vec, normed, inv_std)


def norm_back(grad_in, normed, inv_std, gain_vec):
    scaled = grad_in * gain_vec
    return inv_std * (
        scaled
        - jnp.mean(scaled, axis=-1, keepdims=True)
        - normed * jnp.mean(scaled * normed, axis=-1, keepdims=True)
    )


def project(left_side, right_side):
    return jnp.einsum("rcd,de->rce", left_side, right_side, preferred_element_type=F32)


def project_back(grad_in, right_side):
    return jnp.einsum("rce,de->rcd", grad_in, right_side, preferred_element_type=F32)


def with_previous(value_rows, edge_row, keep):
    earlier = jnp.concatenate([edge_row[:, None, :], value_rows[:, :-1, :]], axis=1)
    return earlier * keep[:, :, None]


def flat(value):
    return value.reshape(-1, value.shape[-1])


def shards(
    incoming_symbols,
    article_sizes,
    mixer_norm_scale,
    mixer_norm_offset,
    temporal_lookup_share,
    temporal_payload_share,
    temporal_gate_share,
    fading_log_rates,
    present_reward_vector,
    lookup_matrix,
    payload_matrix,
    gate_matrix,
    emission_matrix,
    channel_norm_scale,
    channel_norm_offset,
    channel_lookup_share,
    channel_gate_share,
    channel_lookup_matrix,
    channel_payload_matrix,
    channel_gate_matrix,
    final_cotangent,
):
    rows_here, group_len, features = incoming_symbols.shape
    full = (rows_here, group_len, features)
    begins = jnp.cumsum(article_sizes, axis=1) - article_sizes
    position = lax.axis_index("seq") * group_len + jnp.arange(group_len, dtype=jnp.int32)
    starts = jnp.any(position[None, :, None] == begins[:, None, :], axis=2)
    keep = jnp.where(starts, 0.0, 1.0).astype(F32)
    ahead_windows, back_windows = keep_windows(article_sizes, group_len, 128)
    decay_rate = jnp.exp(fading_log_rates)
    rate_row = jnp.broadcast_to(decay_rate[None, :], (8, features))
    bonus_row = jnp.broadcast_to(present_reward_vector[None, :], (8, features))
    ready = article_sizes[0, 0] > 0
    enter = functools.partial(entering, begins=begins, decay_rate=decay_rate, group_len=group_len)

    symbols = incoming_symbols.astype(F32)
    att_last = norm_rows(symbols[:, -1, :], mixer_norm_scale, mixer_norm_offset)[0]
    att_edge = shifted(att_last, "seq", 1)
    att_normed, _, att_inv = norm_rows(symbols, mixer_norm_scale, mixer_norm_offset)
    att_mean = jnp.mean(symbols, axis=-1, keepdims=True)
    att_unit_again = lambda: (incoming_symbols.astype(F32) - att_mean) * att_inv
    att_prev = with_previous(att_normed, att_edge, keep)
    mix = lambda share: (att_normed * share + att_prev * (1.0 - share)).astype(BF16)
    key_mixed = mix(temporal_lookup_share)
    value_mixed = mix(temporal_payload_share)
    recep_mixed = mix(temporal_gate_share)
    key_proj = project(key_mixed, lookup_matrix)
    value_proj = project(value_mixed, payload_matrix)
    recep_proj = project(recep_mixed, gate_matrix)
    tails = ((2, rows_here, features), F32)
    (tail,) = scan_call(
        forward_tails_kernel, [key_proj, value_proj, ahead_windows, rate_row], [tails]
    )
    key_mixed, value_mixed, recep_mixed = map(flat, (key_mixed, value_mixed, recep_mixed))
    state, key_far, value_far, recep_far = at_once(
        ready,
        lambda: (enter(tail, backward=False), *map(send_whole, (key_mixed, value_mixed, recep_mixed))),
    )
    key_side, value_side, recep_side = (
        (key_mixed, key_far), (value_mixed, value_far), (recep_mixed, recep_far)
    )
    num_state, den_state, gated = scan_call(
        forward_states_kernel,
        [key_proj, value_proj, recep_proj, ahead_windows, rate_row, bonus_row, state],
        [(full, F32), (full, F32), (full, BF16)],
    )
    after_att = symbols + project(gated, emission_matrix)

    ffn_normed, ffn_unit, ffn_inv = norm_rows(after_att, channel_norm_scale, channel_norm_offset)
    gated = flat(gated)
    last_rows = ffn_normed[:, -1, :]
    ffn_edge, gated_far = at_once(
        ready, lambda: (shifted(last_rows, "seq", 1), send_whole(gated))
    )
    gated_side = (gated, gated_far)
    ffn_prev = with_previous(ffn_normed, ffn_edge, keep)
    ffn_key_mixed = (
        ffn_normed * channel_lookup_share + ffn_prev * (1.0 - channel_lookup_share)
    ).astype(BF16)
    ffn_recep_mixed = (
        ffn_normed * channel_gate_share + ffn_prev * (1.0 - channel_gate_share)
    ).astype(BF16)
    line = Line()
    gate, mark = line.gate, line.mark
    fkey_far = send_across(flat(ffn_key_mixed))
    tokens, hidden = rows_here * group_len, channel_lookup_matrix.shape[1]
    flat_shape = (tokens, features)
    above, layer_out, grad_fvalue, grad_frecep = channel_call(
        ahead_kernel,
        [
            flat(ffn_key_mixed), flat(ffn_recep_mixed), channel_lookup_matrix,
            channel_payload_matrix, channel_gate_matrix, flat(after_att), flat(final_cotangent),
        ],
        (None, None, 1, 0, None, None, None),
        [((tokens, hidden), F32), (flat_shape, BF16), (flat_shape, BF16), (flat_shape, BF16)],
        (1, None, None, None),
        [pltpu.VMEM(flat_shape, F32)],
        hidden,
    )
    layer_out = layer_out.reshape(full)

    grad_top = final_cotangent.astype(F32)
    mark(grad_fvalue)
    fvalue_far = send_across(flat(grad_fvalue))
    grad_fkey_in, grad_frecep_in = channel_call(
        back_kernel,
        [grad_fvalue, grad_frecep, channel_lookup_matrix, channel_payload_matrix, channel_gate_matrix, above],
        (None, None, 1, 0, None, 1),
        [(flat_shape, F32), (flat_shape, F32)],
        (None, None),
        [],
        hidden,
    )
    grad_fkey_in, grad_frecep_in = grad_fkey_in.reshape(full), grad_frecep_in.reshape(full)
    ffn_delta = ffn_normed - ffn_prev
    grad_ffn_mix_key = jnp.sum(grad_fkey_in * ffn_delta, axis=(0, 1))
    grad_ffn_mix_recep = jnp.sum(grad_frecep_in * ffn_delta, axis=(0, 1))
    grad_ffn_prev = mark(
        (grad_fkey_in * (1.0 - channel_lookup_share) + grad_frecep_in * (1.0 - channel_gate_share))
        * keep[:, :, None]
    )
    first_row = gate(grad_ffn_prev[:, 0, :])
    ffn_back_edge, frecep_far, grad_frecep_far, fkey_cross = at_once(
        ready,
        lambda: (
            shifted(first_row, "seq", -1),
            send_whole(flat(ffn_recep_mixed)),
            send_half(flat(grad_frecep)),
            exchange(fkey_far[1], CORE),
        ),
    )
    mark(ffn_back_edge)
    grad_ffn_normed = (
        grad_fkey_in * channel_lookup_share
        + grad_frecep_in * channel_gate_share
        + jnp.concatenate([grad_ffn_prev[:, 1:, :], ffn_back_edge[:, None, :]], axis=1)
    )
    grad_ffn_ln_gain = jnp.sum(grad_ffn_normed * ffn_unit, axis=(0, 1))
    grad_ffn_ln_bias = jnp.sum(grad_ffn_normed, axis=(0, 1))
    grad_after = grad_top + norm_back(grad_ffn_normed, ffn_unit, ffn_inv, channel_norm_scale)

    grad_att_out = mark(grad_after.astype(BF16))
    grad_gated = project_back(gate(grad_att_out), emission_matrix)
    grad_num, grad_den, grad_recep, tail = scan_call(
        backward_tails_kernel,
        [grad_gated, key_proj, value_proj, recep_proj, num_state, den_state, back_windows, rate_row, bonus_row],
        [(full, F32), (full, F32), (full, BF16), tails],
    )
    fr = Partial("FR", (flat(ffn_recep_mixed), frecep_far), (flat(grad_frecep), grad_frecep_far))
    gated_tail = gate(mark(tail))
    state, (recep_far, out_far), fr.halves = at_once(
        ready,
        lambda: (
            enter(gated_tail, backward=True),
            send_half_of((flat(grad_recep), flat(grad_att_out))),
            fr.products(),
        ),
    )
    mark(state)

    step = functools.partial(phase, line, ready)
    ou = Partial("OU", (gated, gated_far), (flat(grad_att_out), out_far))
    ar = Partial("AR", recep_side, (flat(grad_recep), recep_far))
    fvalue_cross = exchange(gate(fvalue_far[1]), CORE)
    ou.multiply(line)
    ar.multiply(line)
    mark(fvalue_cross, ar.halves[0])

    def hidden_halves():
        made = hidden_products(
            flat(ffn_key_mixed),
            (*fkey_far, fkey_cross),
            flat(grad_fvalue),
            (*fvalue_far, fvalue_cross),
            channel_lookup_matrix,
            channel_payload_matrix,
        )
        return [Blocks(name, value).first() for name, value in zip(("BV", "BK"), made)]

    halves = step([fr, ou, ar], hidden_halves)
    big_value, big_key = [Blocks(name, None, pair) for name, pair in zip(("BV", "BK"), halves)]
    big_key.forward(line)
    big_value.forward(line)
    grad_key, grad_value, sums = step(
        [ar, ou],
        lambda: scan_call(
            backward_states_kernel,
            [grad_num, grad_den, key_proj, value_proj, num_state, den_state, back_windows, rate_row, bonus_row, state],
            [(full, BF16), (full, BF16), ((16, features), F32)],
        ),
    )
    (key_far, value_far), grad_key_in, grad_value_in, grad_recep_in = step(
        [],
        lambda: (
            send_half_of((flat(grad_key), flat(grad_value))),
            project_back(grad_key, lookup_matrix),
            project_back(grad_value, payload_matrix),
            project_back(grad_recep, gate_matrix),
        ),
    )
    reward_slope = jnp.sum(sums[:8], axis=0)
    grad_time_decay = -decay_rate * jnp.exp(-decay_rate) * jnp.sum(sums[8:], axis=0)
    ak = Partial("AK", key_side, (flat(grad_key), key_far))
    av = Partial("AV", value_side, (flat(grad_value), value_far))
    ak.multiply(line)

    def mixes():
        normed = att_unit_again() * mixer_norm_scale + mixer_norm_offset
        att_delta = normed - with_previous(normed, att_edge, keep)
        att_back = (
            grad_key_in * (1.0 - temporal_lookup_share)
            + grad_value_in * (1.0 - temporal_payload_share)
            + grad_recep_in * (1.0 - temporal_gate_share)
        ) * keep[:, :, None]
        return (
            shifted(att_back[:, 0, :], "seq", -1),
            att_back,
            av.products(),
            jnp.sum(grad_key_in * att_delta, axis=(0, 1)),
            jnp.sum(grad_value_in * att_delta, axis=(0, 1)),
            jnp.sum(grad_recep_in * att_delta, axis=(0, 1)),
            grad_key_in * temporal_lookup_share
            + grad_value_in * temporal_payload_share
            + grad_recep_in * temporal_gate_share,
        )

    big_key.forward(line)
    big_value.forward(line)
    att_back_edge, grad_att_prev, av.halves, grad_mix_key, grad_mix_value, grad_mix_recep, direct = step(
        [ak], mixes
    )
    big_key.forward(line)
    big_value.forward(line)
    two = Stacked(line, [fr, ak])

    def norm_att():
        att_unit = att_unit_again()
        grad_att_normed = direct + jnp.concatenate(
            [grad_att_prev[:, 1:, :], att_back_edge[:, None, :]], axis=1
        )
        grad_tokens = (
            grad_after + norm_back(grad_att_normed, att_unit, att_inv, mixer_norm_scale)
        ).astype(BF16)
        return (
            grad_tokens,
            jnp.sum(grad_att_normed * att_unit, axis=(0, 1)),
            jnp.sum(grad_att_normed, axis=(0, 1)),
        )

    grad_tokens, grad_att_ln_gain, grad_att_ln_bias = step([two, av, ar], norm_att)
    vectors = Vectors(
        jnp.stack(
            [
                grad_att_ln_gain,
                grad_att_ln_bias,
                grad_mix_key,
                grad_mix_value,
                grad_mix_recep,
                grad_time_decay,
                reward_slope,
                grad_ffn_ln_gain,
                grad_ffn_ln_bias,
                grad_ffn_mix_key,
                grad_ffn_mix_recep,
            ]
        )
    )
    step([av, ou, vectors])
    big_key.forward(line)
    big_value.forward(line)
    three, pair = Stacked(line, [two, av]), Stacked(line, [ou, ar])
    step([three, pair, vectors])
    pairs = big_value.arrived(line), big_key.arrived(line)

    (ou_sum, ar_sum), (value_sum, key_sum) = step(
        [three, vectors],
        lambda: at_once(ready, lambda: (gather(total_of(pair.terms)), join_hidden(*pairs))),
    )
    (fr_sum, ak_sum, av_sum), got = step(
        [], lambda: gather(total_of(three.terms), lambda: at_once(ready, vectors.hop))
    )
    small = lax.optimization_barrier(got)
    return (
        layer_out,
        grad_tokens,
        *[small[i] for i in range(7)],
        ak_sum,
        av_sum,
        ar_sum,
        ou_sum,
        *[small[i] for i in range(7, 11)],
        key_sum,
        value_sum,
        fr_sum,
    )


def solution(mesh):
    tokens = P("batch", "seq", None)
    vector, matrix = P("seq"), P("seq", None)
    return jax.shard_map(
        shards,
        mesh=mesh,
        in_specs=(tokens, P("batch", None), *([P()] * 18), tokens),
        out_specs=(tokens, tokens, *([vector] * 7), *([matrix] * 4), *([vector] * 4), *([matrix] * 3)),
        check_vma=False,
    )
```

```python
import functools
import math

import jax
import jax.numpy as jnp
from jax import lax
from jax.experimental import pallas as pl
from jax.experimental.pallas import tpu as pltpu
from jax.sharding import PartitionSpec as P

F32, BF16 = jnp.float32, jnp.bfloat16


def shifted(value, axis, distance):
    devices = range(lax.axis_size(axis))
    route = [(i - distance, i) for i in devices if i - distance in devices]
    return lax.ppermute(value, axis, route)


def bit_value(bit):
    axis, place = bit
    return (lax.axis_index(axis) >> place) & 1


def exchange(value, bit):
    axis, place = bit
    return lax.ppermute(value, axis, [(i, i ^ (1 << place)) for i in range(lax.axis_size(axis))])


def pick(value, index, dim):
    return lax.dynamic_index_in_dim(value, index, dim, keepdims=False)


def total_of(terms):
    return functools.reduce(lambda a, b: a + b, terms)


def axis_bits(axis):
    return [(axis, k) for k in range(int(math.log2(lax.axis_size(axis))))]


def at_once(ready, step, *values):
    blank = lambda *v: jax.tree.map(
        lambda x: jnp.zeros(x.shape, x.dtype), jax.eval_shape(step, *v)
    )
    return lax.cond(ready, step, blank, *values)


class Line:
    def __init__(self):
        self.token = None

    def gate(self, value):
        if self.token is None:
            return value
        return lax.optimization_barrier((value, self.token))[0]

    def mark(self, value, *others):
        self.token = (value, *others)
        return value


CORE = ("batch", 0)


def send_half(value):
    half = value.shape[1] // 2
    theirs = lax.dynamic_slice_in_dim(value, (1 - bit_value(CORE)) * half, half, 1)
    return exchange(theirs.astype(F32), CORE)


def send_half_of(values):
    half = values[0].shape[1] // 2
    at = (1 - bit_value(CORE)) * half
    theirs = [lax.dynamic_slice_in_dim(v, at, half, 1).astype(F32) for v in values]
    got = exchange(jnp.concatenate(theirs, axis=0), CORE)
    return jnp.split(got, len(values), axis=0)


def send_whole(value):
    return exchange(value.astype(F32), CORE)


CROSS = ("batch", 1)


def send_across(value):
    value = value.astype(F32)
    return exchange(value, CORE), exchange(value, CROSS)


def hidden_kernel(
    at_ref, *refs, unit,
):
    del at_ref
    lefts, grads, (up_a, up_b, down_a, down_b, value_ref, key_ref, left_all, grad_all) = (
        refs[:4], refs[4:8], refs[8:]
    )
    tokens = lefts[0].shape[0]

    @pl.when(pl.program_id(0) == 0)
    def _():
        for k in range(4):
            at = pl.ds(k * tokens, tokens)
            left_all[at, :] = lefts[k][...].astype(BF16)
            grad_all[at, :] = grads[k][...].astype(BF16)

    up = jnp.concatenate([up_a[...], up_b[...]], axis=1)
    down = jnp.concatenate([down_a[...], down_b[...]], axis=0)
    first = lambda a, b: lax.dot_general(a, b, (((0,), (0,)), ((), ())), preferred_element_type=F32)

    def products(k):
        at = pl.ds(k * 2 * tokens, 2 * tokens)
        left, grad = left_all[at, :], grad_all[at, :]
        above = jnp.maximum(jnp.dot(left, up, preferred_element_type=F32), 0.0)
        back = lax.dot_general(grad, down, (((1,), (1,)), ((), ())), preferred_element_type=F32)
        return first((above * above).astype(BF16), grad), first((back * (2.0 * above)).astype(BF16), left)

    def put(value, key, add):
        for half in range(2):
            part = value[half * unit : (half + 1) * unit]
            value_ref[half] = value_ref[half] + part if add else part
        rows = key.shape[1] // key_ref.shape[0]
        for s in range(key_ref.shape[0]):
            part = key[:, s * rows : (s + 1) * rows]
            key_ref[s] = key_ref[s] + part if add else part

    put(*products(0), False)
    put(*products(1), True)


def hidden_products(left, far_lefts, grad, far_grads, up, down):
    seq, tokens, features = lax.axis_size("seq"), left.shape[0], left.shape[1]
    unit = up.shape[1] // seq // 4
    quarter = 2 * bit_value(CORE) + bit_value(CROSS)
    out_shapes = (seq, unit, features), (seq, seq * unit, features // seq)
    if unit % 128 or features // seq % 128:
        up = pick(up.reshape(features, seq, 4, unit), quarter, 2).reshape(features, -1)
        down = pick(down.reshape(seq, 4, unit, features), quarter, 1).reshape(-1, features)
        lefts = jnp.concatenate([left, *[f.astype(BF16) for f in far_lefts]])
        grads = jnp.concatenate([grad, *[f.astype(BF16) for f in far_grads]])
        above = jnp.maximum(jnp.dot(lefts, up, preferred_element_type=F32), 0.0)
        back = lax.dot_general(grads, down, (((1,), (1,)), ((), ())), preferred_element_type=F32)
        first = lambda a, b: lax.dot_general(a, b, (((0,), (0,)), ((), ())), preferred_element_type=F32)
        value = first((above * above).astype(BF16), grads).reshape(out_shapes[0])
        key = first((back * (2.0 * above)).astype(BF16), lefts)
        return value, jnp.swapaxes(key.reshape(-1, seq, features // seq), 0, 1)
    whole = lambda: pl.BlockSpec((tokens, features), lambda i, at: (0, 0), pipeline_mode=pl.Buffered(1))
    ups = [pl.BlockSpec((features, unit), lambda i, at, h=h: (0, 4 * (2 * i + h) + at[0])) for h in (0, 1)]
    downs = [pl.BlockSpec((unit, features), lambda i, at, h=h: (4 * (2 * i + h) + at[0], 0)) for h in (0, 1)]
    return pl.pallas_call(
        functools.partial(hidden_kernel, unit=unit),
        grid_spec=pltpu.PrefetchScalarGridSpec(
            num_scalar_prefetch=1,
            grid=(seq // 2,),
            in_specs=[whole() for _ in range(8)] + ups + downs,
            out_specs=[
                pl.BlockSpec((2, unit, features), lambda i, at: (i, 0, 0)),
                pl.BlockSpec((seq, 2 * unit, features // seq), lambda i, at: (0, i, 0)),
            ],
            scratch_shapes=[pltpu.VMEM((4 * tokens, features), BF16)] * 2,
        ),
        out_shape=[jax.ShapeDtypeStruct(shape, F32) for shape in out_shapes],
        compiler_params=pltpu.CompilerParams(vmem_limit_bytes=56 * 1024 * 1024),
        cost_estimate=pl.CostEstimate(
            flops=32 * tokens * features * seq * unit,
            bytes_accessed=40 * tokens * features,
            transcendentals=0,
        ),
    )(quarter[None].astype(jnp.int32), left, *far_lefts, grad, *far_grads, up, up, down, down)


ORDERS = dict(BV="zywx", BK="yzwx", FR="xyzw", OU="zxyw", AR="yxzw", AK="xyzw", AV="xyzw")


def order_of(name):
    seq = axis_bits("seq")
    places = dict(x=axis_bits("batch")[1:], y=seq[:1], z=seq[1:2], w=seq[2:])
    return [places[letter] for letter in ORDERS[name]]


def halve(terms, dims, bit):
    if bit not in dims:
        total = total_of(terms)
        return total, [total]
    dim, mine = dims.index(bit), bit_value(bit)
    send = total_of([pick(t, 1 - mine, dim) for t in terms])
    return send, [pick(t, mine, dim) for t in terms]


class Blocks:
    halves = None

    def __init__(self, name, value, halves=None):
        self.hops, self.dims = order_of(name), axis_bits("seq")[::-1]
        self.halves, self.terms = halves, None
        if halves is None:
            self.terms = [value.reshape(*((2,) * len(self.dims)), *value.shape[1:])]

    def first(self):
        send, kept = self.split(self.terms)
        return send, kept[0]

    def split(self, terms):
        if self.halves:
            return self.halves[0], [self.halves[1]]
        return halve(terms, self.dims, self.hops[0][0])

    def go(self, sends):
        bits, dims = self.hops[0], list(self.dims)
        got = exchange(sends, bits[0])
        if len(bits) == 1:
            return got
        terms = self.split(self.terms)[1] + [got]
        dims = [d for d in dims if d != bits[0]]
        for bit in bits[1:]:
            send, kept = halve(terms, dims, bit)
            terms = kept + [exchange(send, bit)]
            dims = [d for d in dims if d != bit]
        return total_of(terms)

    def hop(self):
        return self.go(self.split(self.terms)[0])

    def landed(self, got):
        bits = self.hops[0]
        self.terms = self.split(self.terms)[1] + [got] if len(bits) == 1 else [got]
        self.halves = None
        self.dims = [d for d in self.dims if d not in bits]
        self.hops.pop(0)

    def arrived(self, line):
        return self.terms[:-1] + [line.gate(self.terms[-1])]

    def forward(self, line):
        if self.halves:
            send = line.gate(self.halves[0])
        else:
            send = self.split(self.arrived(line))[0]
        self.landed(self.go(line.mark(send)))


def phase(line, ready, jobs, beside=None):
    def step():
        return [job.hop() for job in jobs], beside() if beside else ()

    got, more = at_once(line.gate(ready), step)
    for job, value in zip(jobs, got):
        job.landed(value)
    line.mark(*jax.tree.leaves((got, more)))
    return more


def product_kernel(
    at_ref, left_ref, far_left_ref, right_ref, far_right_ref, send_ref, keep_ref,
    *, rows, cols, group, place,
):
    first = at_ref[0]

    def lefts(blocks):
        cut = lambda ref, js: jnp.concatenate(
            [ref[:, pl.ds(pl.multiple_of(j * rows, 128), rows)] for j in js], axis=1
        )
        return jnp.concatenate([cut(left_ref, blocks), cut(far_left_ref, blocks).astype(BF16)], axis=0)

    def rights(x):
        at = pl.ds(pl.multiple_of(x * cols, 128), cols)
        return jnp.concatenate([right_ref[:, at], far_right_ref[:, at].astype(BF16)], axis=0)

    dot = lambda a, b: lax.dot_general(
        a, b, (((0,), (0,)), ((), ())), preferred_element_type=F32
    )
    for out, value in ((send_ref, 1 - first), (keep_ref, first)):
        if place is None:
            out[0] = dot(lefts(list(range(group))), rights(value))
        else:
            low = 1 << place
            blocks = [(q // low) * 2 * low + q % low + value * low for q in range(group // 2)]
            left = lefts(blocks)
            for x in range(2):
                out[x, 0] = dot(left, rights(x))


class Partial(Blocks):
    def __init__(self, name, left, right):
        self.left, self.right = left, right
        self.hops, self.terms = order_of(name), None
        self.dims = axis_bits("batch")[1:] + axis_bits("seq")[::-1]
        self.blocks = lax.axis_size("seq")
        self.rows = left[0].shape[1] // self.blocks
        self.cols = right[0].shape[1] // 4

    def plain(self):
        half = self.right[0].shape[1] // 2
        own = lax.dynamic_slice_in_dim(self.right[0], bit_value(CORE) * half, half, 1)
        dot = lambda a, b: lax.dot_general(
            a.astype(BF16), b.astype(BF16), (((0,), (0,)), ((), ())), preferred_element_type=F32
        )
        whole = dot(self.left[0], own) + dot(self.left[1], self.right[1])
        lead = (2,) * len(axis_bits("seq"))
        whole = jnp.moveaxis(whole.reshape(*lead, self.rows, 2, self.cols), -2, 0)
        send, kept = halve([whole], self.dims, self.hops[0][0])
        return send, kept[0]

    def kernel(self):
        rows, cols, tokens = self.rows, self.cols, self.left[0].shape[0]
        first = self.hops[0][0]
        place = first[1] if first[0] == "seq" else None
        group = 4
        steps = self.blocks // group
        if place is None:
            block, shape = (1, group * rows, cols), (steps, group * rows, cols)
            out_index = lambda i, at: (i, 0, 0)
        else:
            block, shape = (2, 1, group // 2 * rows, cols), (2, steps, group // 2 * rows, cols)
            out_index = lambda i, at: (0, i, 0, 0)
        out = jax.ShapeDtypeStruct(shape, F32)
        at = jnp.stack([bit_value(first), bit_value(CORE)]).astype(jnp.int32)
        send, kept = pl.pallas_call(
            functools.partial(
                product_kernel, rows=rows, cols=cols, group=group, place=place
            ),
            grid_spec=pltpu.PrefetchScalarGridSpec(
                num_scalar_prefetch=1,
                grid=(steps,),
                in_specs=[
                    pl.BlockSpec((tokens, group * rows), lambda i, at: (0, i)),
                    pl.BlockSpec((tokens, group * rows), lambda i, at: (0, i)),
                    pl.BlockSpec((tokens, 2 * cols), lambda i, at: (0, at[1])),
                    pl.BlockSpec((tokens, 2 * cols), lambda i, at: (0, 0)),
                ],
                out_specs=[pl.BlockSpec(block, out_index)] * 2,
            ),
            out_shape=[out, out],
            compiler_params=scan_params(),
            cost_estimate=pl.CostEstimate(
                flops=8 * tokens * self.blocks * rows * cols,
                bytes_accessed=8 * self.blocks * rows * cols,
                transcendentals=0,
            ),
        )(at, self.left[0], self.left[1], self.right[0], self.right[1])
        lead = (2,) * (len(self.dims) - 1)
        return send.reshape(*lead, rows, cols), kept.reshape(*lead, rows, cols)

    def products(self):
        aligned = self.rows % 128 == 0 and self.blocks % 4 == 0 and len(axis_bits("batch")) == 2
        return self.kernel() if aligned else self.plain()

    def multiply(self, line):
        self.left = (line.gate(self.left[0]), self.left[1])
        self.halves = self.products()
        line.mark(self.halves[0])


class Stacked(Blocks):
    def __init__(self, line, jobs):
        self.hops, self.dims = list(jobs[0].hops), jobs[0].dims
        sums = [total_of(j.arrived(line)) for j in jobs]
        sums = [v if isinstance(j, Stacked) else v[..., None, :, :] for j, v in zip(jobs, sums)]
        self.terms = [jnp.concatenate(sums, axis=-3)]


class Vectors(Blocks):
    def __init__(self, vectors):
        vectors = jnp.pad(vectors, ((0, -vectors.shape[0] % 8), (0, 0)))
        count, seq = vectors.shape[0], lax.axis_size("seq")
        self.dims = axis_bits("seq")[::-1]
        bits = axis_bits("seq")
        self.hops = [[b] for b in axis_bits("batch") + bits[:1]] + [bits[1:]]
        value = jnp.swapaxes(vectors.reshape(count, seq, -1), 0, 1)
        self.terms = [value.reshape(*((2,) * len(self.dims)), count, -1)]

def in_order(own, other, bit, axis):
    first = bit_value(bit) == 0
    return jnp.concatenate(
        [jnp.where(first, own, other), jnp.where(first, other, own)], axis=axis
    )


def gather(own, beside=None):
    other, more = exchange(own, CROSS), None
    if beside:
        other, more = lax.optimization_barrier((other, beside()))
    own = in_order(own, other, CROSS, 2)
    own = in_order(own, exchange(own, CORE), CORE, 2)
    joined = [own[i] for i in range(own.shape[0])]
    return (joined, more) if beside else joined


def join_hidden(values, keys):
    seq = lax.axis_size("seq")
    value = in_order(*values, CROSS, 0)
    key = in_order(*[t.reshape(seq, 1, -1, t.shape[-1]) for t in keys], CROSS, 1)
    return (value, exchange(value, CORE)), (key, exchange(key, CORE))


def whole_hidden(values, keys):
    key = in_order(*keys, CORE, 1)
    return in_order(*values, CORE, 0), jnp.transpose(key.reshape(-1, key.shape[-1]))


def entering(tails, begins, decay_rate, group_len, backward):
    count, mine = lax.axis_size("seq"), lax.axis_index("seq")
    sign = -1 if backward else 1

    def gain(lo, hi):
        a, b = (mine + lo, mine + hi) if backward else (mine - hi + 1, mine - lo + 1)
        hit = jnp.any((begins >= a * group_len) & (begins < b * group_len), axis=1, keepdims=True)
        return jnp.where(hit, 0.0, 1.0) * jnp.exp(-float((hi - lo) * group_len) * decay_rate)[None, :]

    reach, window, before = 1, tails, None
    while reach < count:
        got = [
            (j, shifted(window, "seq", sign * j * reach)) for j in range(1, 4) if j * reach < count
        ]
        if before is None:
            before = total_of([v if j == 1 else gain(1, j) * v for j, v in got])
            seen = 1 + len(got)
            window = tails + gain(0, 1) * before if seen < count else None
        else:
            before_more = total_of([gain(1, j * reach) * v for j, v in got])
            seen = reach * (1 + len(got))
            if seen < count:
                window = window + total_of([gain(0, j * reach) * v for j, v in got])
            before = before + before_more
        reach *= 4
    return before


def scan_params():
    return pltpu.CompilerParams(vmem_limit_bytes=48 * 1024 * 1024)


def lane_tiles(width):
    return [slice(i, i + 128) for i in range(0, width, 128)]


WINDOW = {name: k for k, name in enumerate(("keep", "one", "two", "four", "group", "eight", "end"))}


def windows_kernel(sizes_ref, block_ref, ahead_ref, back_ref):
    rows, length, width = ahead_ref.shape[1:]
    t = lax.broadcasted_iota(jnp.int32, (length, width), 0)
    inner = t & 7

    def put(ref, name, equal, inside=None):
        kept = equal if inside is None else equal & inside
        ref[WINDOW[name], row] = jnp.where(kept, 1.0, 0.0)

    for row in range(rows):
        begins, at = [], -block_ref[0]
        for j in range(sizes_ref.shape[1]):
            begins.append(at)
            at = at + sizes_ref[row, j]

        def begun(by):
            return total_of([jnp.where(by >= b, 1, 0) for b in begins])

        here, ahead_of = begun(t), begun(t - 1)
        keep = here == ahead_of
        put(ahead_ref, "keep", keep)
        put(back_ref, "keep", keep)
        for name, n in (("one", 1), ("two", 2), ("four", 4)):
            put(ahead_ref, name, here == begun(t - n), inner >= n)
            put(back_ref, name, begun(t + (n - 1)) == ahead_of, inner <= 7 - n)
        put(ahead_ref, "group", here == begun(t - inner - 1))
        put(back_ref, "group", begun(t - inner + 7) == ahead_of)
        put(ahead_ref, "eight", here == begun(t - 8), t >= 8)
        put(back_ref, "eight", begun(t + 7) == ahead_of, t < length - 8)
        put(ahead_ref, "end", here == begun(jnp.full_like(t, length - 1)))
        put(back_ref, "end", ahead_of == begun(jnp.full_like(t, -1)))


def keep_windows(sizes, length, width):
    block = (lax.axis_index("seq") * length)[None].astype(jnp.int32)
    out = jax.ShapeDtypeStruct((len(WINDOW), sizes.shape[0], length, width), F32)
    return pl.pallas_call(
        windows_kernel,
        out_shape=[out, out],
        in_specs=[pl.BlockSpec(memory_space=pltpu.SMEM)] * 2,
        compiler_params=scan_params(),
        cost_estimate=pl.CostEstimate(flops=100 * out.size, bytes_accessed=8 * out.size, transcendentals=0),
    )(sizes, block)


def powers(rate_ref, tiles):
    return lambda n: [jnp.exp(-n * rate_ref[0:1, t]) for t in tiles]


def inner_place(shape=(8, 128)):
    return lax.broadcasted_iota(jnp.int32, shape, 0)


def spread(row):
    return jnp.broadcast_to(row, (8, 128))


def in_group(value, factors, back):
    for n, factor in zip((1, 2, 4), factors):
        value = value + factor * pltpu.roll(value, 8 - n if back else n, 0)
    return value


def halves_of(ref, row, at, tile):
    value = ref[row, at, tile]
    return value[:8], value[8:]


def windows_at(win_ref, row, at):
    names = ("keep", "one", "two", "four", "group")
    return [dict(zip(names, v)) for v in zip(*[halves_of(win_ref.at[WINDOW[n]], row, at, slice(None)) for n in names])]


def pair_at(p):
    return pl.ds(pl.multiple_of(p * 16, 16), 16)


def forward_tails_kernel(k_ref, v_ref, win_ref, rate_ref, tail_ref):
    rows, length, width = k_ref.shape
    tiles = lane_tiles(width)
    chains = [(r, i, t) for r in range(rows) for i, t in enumerate(tiles)]
    eight = powers(rate_ref, tiles)(8.0)

    def step(p, carry):
        at, out = pair_at(p), []
        windows = [halves_of(win_ref.at[WINDOW["eight"]], r, at, slice(None)) for r in range(rows)]
        for (r, i, t), (num, den) in zip(chains, carry):
            for h, (key, value) in enumerate(zip(halves_of(k_ref, r, at, t), halves_of(v_ref, r, at, t))):
                factor, e = windows[r][h] * eight[i], jnp.exp(key)
                num, den = factor * num + e * value, factor * den + e
            out.append((num, den))
        return tuple(out)

    zero = jnp.zeros((8, 128), F32)
    done = lax.fori_loop(0, length // 16, step, tuple((zero, zero) for _ in chains), unroll=2)
    left = powers(rate_ref, tiles)((7 - inner_place()).astype(F32))
    for (r, i, t), pair in zip(chains, done):
        factor = win_ref[WINDOW["end"], r, pl.ds(length - 8, 8), :] * left[i]
        for q in range(2):
            tail_ref[q, r : r + 1, t] = jnp.sum(factor * pair[q], axis=0, keepdims=True)


def forward_states_kernel(
    k_ref, v_ref, recep_ref, win_ref, rate_ref, bonus_ref, enter_ref, num_ref, den_ref, gated_ref
):
    rows, length, width = k_ref.shape
    tiles = lane_tiles(width)
    chains = [(r, i, t) for r in range(rows) for i, t in enumerate(tiles)]
    power = powers(rate_ref, tiles)
    ones, twos, fours = power(1.0), power(2.0), power(4.0)
    groups = power((1 + inner_place()).astype(F32))
    head = inner_place() == 0

    def step(p, carry):
        at, out = pair_at(p), []
        windows = [windows_at(win_ref, r, at) for r in range(rows)]
        for (r, i, t), states in zip(chains, carry):
            keys, values = halves_of(k_ref, r, at, t), halves_of(v_ref, r, at, t)
            receps, bonus, results = halves_of(recep_ref, r, at, t), bonus_ref[0:1, t], []
            for h in range(2):
                w = windows[r][h]
                factors = (w["one"] * ones[i], w["two"] * twos[i], w["four"] * fours[i])
                group = w["group"] * groups[i]
                e, held, here = jnp.exp(keys[h]), [], []
                for state, item in zip(states, (e * values[h], e)):
                    full = in_group(item, factors, False) + group * state
                    here.append(w["keep"] * jnp.where(head, state, pltpu.roll(full, 1, 0)))
                    held.append(spread(full[7:8]))
                states = held
                first = jnp.exp(bonus + keys[h])
                wkv = (here[0] + first * values[h]) / (here[1] + first)
                results.append((*here, jax.nn.sigmoid(receps[h]) * wkv))
            for ref, two in zip((num_ref, den_ref, gated_ref), zip(*results)):
                ref[r, at, t] = jnp.concatenate(two, axis=0).astype(ref.dtype)
            out.append(tuple(states))
        return tuple(out)

    start = tuple(tuple(spread(enter_ref[q, r : r + 1, t]) for q in range(2)) for r, _, t in chains)
    lax.fori_loop(0, length // 16, step, start)


def backward_tails_kernel(
    grad_ref, k_ref, v_ref, recep_ref, num_ref, den_ref, win_ref, rate_ref, bonus_ref,
    gnum_ref, gden_ref, grecep_ref, tail_ref,
):
    rows, length, width = k_ref.shape
    tiles = lane_tiles(width)
    chains = [(r, i, t) for r in range(rows) for i, t in enumerate(tiles)]
    eight = powers(rate_ref, tiles)(8.0)
    pairs = length // 16

    def step(p, carry):
        at, out = pair_at(pairs - 1 - p), []
        keeps = [halves_of(win_ref.at[WINDOW["keep"]], r, at, slice(None)) for r in range(rows)]
        windows = [halves_of(win_ref.at[WINDOW["eight"]], r, at, slice(None)) for r in range(rows)]
        for (r, i, t), (late_num, late_den) in zip(chains, carry):
            key, value = k_ref[r, at, t], v_ref[r, at, t]
            first = jnp.exp(bonus_ref[0:1, t] + key)
            below = den_ref[r, at, t] + first
            wkv = (num_ref[r, at, t] + first * value) / below
            gate, grad = jax.nn.sigmoid(recep_ref[r, at, t]), grad_ref[r, at, t]
            grecep_ref[r, at, t] = (grad * wkv * (gate * (1.0 - gate))).astype(BF16)
            up = grad * gate / below
            low = -up * wkv
            gnum_ref[r, at, t] = up
            gden_ref[r, at, t] = low
            for h in (1, 0):
                rows_of = slice(8 * h, 8 * h + 8)
                factor, keep = windows[r][h] * eight[i], keeps[r][h]
                late_num = factor * late_num + keep * up[rows_of]
                late_den = factor * late_den + keep * low[rows_of]
            out.append((late_num, late_den))
        return tuple(out)

    zero = jnp.zeros((8, 128), F32)
    done = lax.fori_loop(0, pairs, step, tuple((zero, zero) for _ in chains))
    left = powers(rate_ref, tiles)(inner_place().astype(F32))
    for (r, i, t), pair in zip(chains, done):
        factor = win_ref[WINDOW["end"], r, pl.ds(0, 8), :] * left[i]
        for q in range(2):
            tail_ref[q, r : r + 1, t] = jnp.sum(factor * pair[q], axis=0, keepdims=True)


def backward_states_kernel(
    gnum_ref, gden_ref, k_ref, v_ref, num_ref, den_ref, win_ref, rate_ref, bonus_ref, enter_ref,
    gkey_ref, gvalue_ref, sums_ref,
):
    rows, length, width = k_ref.shape
    tiles = lane_tiles(width)
    chains = [(r, i, t) for r in range(rows) for i, t in enumerate(tiles)]
    power = powers(rate_ref, tiles)
    ones, twos, fours = power(1.0), power(2.0), power(4.0)
    groups = power((8 - inner_place()).astype(F32))
    tail = inner_place() == 7
    pairs = length // 16

    def step(p, carry):
        at, out = pair_at(pairs - 1 - p), []
        windows = [windows_at(win_ref, r, at) for r in range(rows)]
        for (r, i, t), (num_state, den_state, slope, fade) in zip(chains, carry):
            states, parts = (num_state, den_state), []
            keys, values = halves_of(k_ref, r, at, t), halves_of(v_ref, r, at, t)
            ups, lows = halves_of(gnum_ref, r, at, t), halves_of(gden_ref, r, at, t)
            nums, dens = halves_of(num_ref, r, at, t), halves_of(den_ref, r, at, t)
            for h in (1, 0):
                w = windows[r][h]
                factors = (w["one"] * ones[i], w["two"] * twos[i], w["four"] * fours[i])
                group, held, here = w["group"] * groups[i], [], []
                for state, item in zip(states, (ups[h], lows[h])):
                    full = in_group(w["keep"] * item, factors, True) + group * state
                    here.append(jnp.where(tail, state, pltpu.roll(full, 7, 0)))
                    held.append(spread(full[0:1]))
                states = held
                e, first = jnp.exp(keys[h]), jnp.exp(bonus_ref[0:1, t] + keys[h])
                present = first * (ups[h] * values[h] + lows[h])
                slope = slope + present
                fade = fade + nums[h] * here[0] + dens[h] * here[1]
                parts.append(
                    (
                        present + e * (here[0] * values[h] + here[1]),
                        ups[h] * first + here[0] * e,
                    )
                )
            for ref, two in zip((gkey_ref, gvalue_ref), zip(*parts[::-1])):
                ref[r, at, t] = jnp.concatenate(two, axis=0).astype(BF16)
            out.append((*states, slope, fade))
        return tuple(out)

    zero = jnp.zeros((8, 128), F32)
    start = tuple(
        (*[spread(enter_ref[q, r : r + 1, t]) for q in range(2)], zero, zero) for r, _, t in chains
    )
    done = lax.fori_loop(0, pairs, step, start)
    for i, t in enumerate(tiles):
        for q in range(2):
            sums_ref[8 * q : 8 * q + 8, t] = total_of(
                [c[2 + q] for (_, j, _), c in zip(chains, done) if j == i]
            )


def scan_call(kernel, inputs, outputs, width=512):
    features = inputs[0].shape[-1]

    def spec(shape):
        lead = len(shape) - 1
        if shape[-1] == 128 and features != 128:
            return pl.BlockSpec(shape, lambda i: (0,) * (lead + 1))
        return pl.BlockSpec((*shape[:-1], width), lambda i: (0,) * lead + (i,))

    out_shape = [jax.ShapeDtypeStruct(s, d) for s, d in outputs]
    moved = sum(x.size * x.dtype.itemsize for x in [*inputs, *out_shape])
    return pl.pallas_call(
        kernel,
        out_shape=out_shape,
        grid=(features // width,),
        in_specs=[spec(x.shape) for x in inputs],
        out_specs=[spec(s) for s, _ in outputs],
        compiler_params=scan_params(),
        cost_estimate=pl.CostEstimate(
            flops=20 * inputs[0].size, bytes_accessed=moved, transcendentals=inputs[0].size
        ),
    )(*inputs)


def channel_kernel(
    left_ref, recep_ref, up_ref, down_ref, gate_ref, after_ref, top_ref,
    out_ref, fvalue_ref, frecep_ref, fkey_ref, recep_in_ref, above_ref, total_ref,
):
    across = (((1,), (1,)), ((), ()))
    block = up_ref.shape[1]
    step, blocks = pl.program_id(0), pl.num_programs(0) // 2

    def at(i):
        return pl.ds(pl.multiple_of(i * block, block), block)

    def add(ref, first, part):
        @pl.when(step == first)
        def _():
            ref[...] = part

        @pl.when(step > first)
        def _():
            ref[...] += part

    @pl.when(step < blocks)
    def _():
        above = jnp.maximum(jnp.dot(left_ref[...], up_ref[...], preferred_element_type=F32), 0.0)
        above_ref[:, at(step)] = above
        add(total_ref, 0, jnp.dot((above * above).astype(BF16), down_ref[...], preferred_element_type=F32))

    @pl.when(step == blocks - 1)
    def _():
        value = total_ref[...]
        gate = jax.nn.sigmoid(
            jnp.dot(recep_ref[...], gate_ref[...], preferred_element_type=F32)
        )
        top = top_ref[...].astype(F32)
        out_ref[...] = (after_ref[...] + gate * value).astype(BF16)
        fvalue_ref[...] = (top * gate).astype(BF16)
        frecep = (top * value * (gate * (1.0 - gate))).astype(BF16)
        frecep_ref[...] = frecep
        recep_in_ref[...] = lax.dot_general(
            frecep, gate_ref[...], across, preferred_element_type=F32
        )

    @pl.when(step >= blocks)
    def _():
        back = lax.dot_general(fvalue_ref[...], down_ref[...], across, preferred_element_type=F32)
        hidden = (back * (2.0 * above_ref[:, at(step - blocks)])).astype(BF16)
        add(fkey_ref, blocks, lax.dot_general(hidden, up_ref[...], across, preferred_element_type=F32))


def channel_mix(left, recep, up, down, gate, after, top):
    (tokens, features), hidden = left.shape, up.shape[1]
    block = min(1024, hidden)
    blocks = hidden // block
    once = lambda x: pl.BlockSpec(x.shape, lambda i: (0, 0), pipeline_mode=pl.Buffered(1))
    shape = (tokens, features)
    return pl.pallas_call(
        channel_kernel,
        out_shape=[jax.ShapeDtypeStruct(shape, d) for d in (BF16, BF16, BF16, F32, F32)],
        grid=(2 * blocks,),
        in_specs=[
            once(left),
            once(recep),
            pl.BlockSpec((features, block), lambda i: (0, lax.rem(i, blocks))),
            pl.BlockSpec((block, features), lambda i: (lax.rem(i, blocks), 0)),
            once(gate),
            once(after),
            once(top),
        ],
        out_specs=[pl.BlockSpec(shape, lambda i: (0, 0))] * 5,
        scratch_shapes=[pltpu.VMEM((tokens, hidden), F32), pltpu.VMEM(shape, F32)],
        compiler_params=pltpu.CompilerParams(vmem_limit_bytes=56 * 1024 * 1024),
        cost_estimate=pl.CostEstimate(
            flops=8 * tokens * features * (hidden + features // 2),
            bytes_accessed=8 * features * hidden + 20 * tokens * features,
            transcendentals=tokens * features,
        ),
    )(left, recep, up, down, gate, after, top)


def norm_rows(value_rows, gain_vec, bias_vec):
    row_mean = jnp.mean(value_rows, axis=-1, keepdims=True)
    centred = value_rows - row_mean
    inv_std = lax.rsqrt(jnp.mean(centred * centred, axis=-1, keepdims=True) + 1e-05)
    normed = centred * inv_std
    return (normed * gain_vec + bias_vec, normed, inv_std)


def norm_back(grad_in, normed, inv_std, gain_vec):
    scaled = grad_in * gain_vec
    return inv_std * (
        scaled
        - jnp.mean(scaled, axis=-1, keepdims=True)
        - normed * jnp.mean(scaled * normed, axis=-1, keepdims=True)
    )


def project(left_side, right_side):
    return jnp.einsum("rcd,de->rce", left_side, right_side, preferred_element_type=F32)


def project_back(grad_in, right_side):
    return jnp.einsum("rce,de->rcd", grad_in, right_side, preferred_element_type=F32)


def with_previous(value_rows, edge_row, keep):
    earlier = jnp.concatenate([edge_row[:, None, :], value_rows[:, :-1, :]], axis=1)
    return earlier * keep[:, :, None]


def flat(value):
    return value.reshape(-1, value.shape[-1])


def shards(
    incoming_symbols,
    article_sizes,
    mixer_norm_scale,
    mixer_norm_offset,
    temporal_lookup_share,
    temporal_payload_share,
    temporal_gate_share,
    fading_log_rates,
    present_reward_vector,
    lookup_matrix,
    payload_matrix,
    gate_matrix,
    emission_matrix,
    channel_norm_scale,
    channel_norm_offset,
    channel_lookup_share,
    channel_gate_share,
    channel_lookup_matrix,
    channel_payload_matrix,
    channel_gate_matrix,
    final_cotangent,
):
    rows_here, group_len, features = incoming_symbols.shape
    full = (rows_here, group_len, features)
    begins = jnp.cumsum(article_sizes, axis=1) - article_sizes
    position = lax.axis_index("seq") * group_len + jnp.arange(group_len, dtype=jnp.int32)
    starts = jnp.any(position[None, :, None] == begins[:, None, :], axis=2)
    keep = jnp.where(starts, 0.0, 1.0).astype(F32)
    ahead_windows, back_windows = keep_windows(article_sizes, group_len, 128)
    decay_rate = jnp.exp(fading_log_rates)
    rate_row = jnp.broadcast_to(decay_rate[None, :], (8, features))
    bonus_row = jnp.broadcast_to(present_reward_vector[None, :], (8, features))
    ready = article_sizes[0, 0] > 0
    enter = functools.partial(entering, begins=begins, decay_rate=decay_rate, group_len=group_len)

    symbols = incoming_symbols.astype(F32)
    att_last = norm_rows(symbols[:, -1, :], mixer_norm_scale, mixer_norm_offset)[0]
    att_edge = shifted(att_last, "seq", 1)
    att_normed, _, att_inv = norm_rows(symbols, mixer_norm_scale, mixer_norm_offset)
    att_mean = jnp.mean(symbols, axis=-1, keepdims=True)
    att_unit_again = lambda: (incoming_symbols.astype(F32) - att_mean) * att_inv
    att_prev = with_previous(att_normed, att_edge, keep)
    mix = lambda share: (att_normed * share + att_prev * (1.0 - share)).astype(BF16)
    key_mixed = mix(temporal_lookup_share)
    value_mixed = mix(temporal_payload_share)
    recep_mixed = mix(temporal_gate_share)
    key_proj = project(key_mixed, lookup_matrix)
    value_proj = project(value_mixed, payload_matrix)
    recep_proj = project(recep_mixed, gate_matrix)
    tails = ((2, rows_here, features), F32)
    (tail,) = scan_call(
        forward_tails_kernel, [key_proj, value_proj, ahead_windows, rate_row], [tails]
    )
    key_mixed, value_mixed, recep_mixed = map(flat, (key_mixed, value_mixed, recep_mixed))
    state, key_far, value_far, recep_far = at_once(
        ready,
        lambda: (enter(tail, backward=False), *map(send_whole, (key_mixed, value_mixed, recep_mixed))),
    )
    key_side, value_side, recep_side = (
        (key_mixed, key_far), (value_mixed, value_far), (recep_mixed, recep_far)
    )
    num_state, den_state, gated = scan_call(
        forward_states_kernel,
        [key_proj, value_proj, recep_proj, ahead_windows, rate_row, bonus_row, state],
        [(full, F32), (full, F32), (full, BF16)],
    )
    after_att = symbols + project(gated, emission_matrix)

    ffn_normed, ffn_unit, ffn_inv = norm_rows(after_att, channel_norm_scale, channel_norm_offset)
    gated = flat(gated)
    last_rows = ffn_normed[:, -1, :]
    ffn_edge, gated_far = at_once(
        ready, lambda: (shifted(last_rows, "seq", 1), send_whole(gated))
    )
    gated_side = (gated, gated_far)
    ffn_prev = with_previous(ffn_normed, ffn_edge, keep)
    ffn_key_mixed = (
        ffn_normed * channel_lookup_share + ffn_prev * (1.0 - channel_lookup_share)
    ).astype(BF16)
    ffn_recep_mixed = (
        ffn_normed * channel_gate_share + ffn_prev * (1.0 - channel_gate_share)
    ).astype(BF16)
    line = Line()
    gate, mark = line.gate, line.mark
    fkey_far = send_across(flat(ffn_key_mixed))
    layer_out, grad_fvalue, grad_frecep, grad_fkey_in, grad_frecep_in = channel_mix(
        flat(ffn_key_mixed), flat(ffn_recep_mixed), channel_lookup_matrix, channel_payload_matrix,
        channel_gate_matrix, flat(after_att), flat(final_cotangent),
    )
    layer_out, grad_fkey_in, grad_frecep_in = [
        x.reshape(full) for x in (layer_out, grad_fkey_in, grad_frecep_in)
    ]

    grad_top = final_cotangent.astype(F32)
    mark(grad_fvalue)
    fvalue_far = send_across(flat(grad_fvalue))
    ffn_delta = ffn_normed - ffn_prev
    grad_ffn_mix_key = jnp.sum(grad_fkey_in * ffn_delta, axis=(0, 1))
    grad_ffn_mix_recep = jnp.sum(grad_frecep_in * ffn_delta, axis=(0, 1))
    grad_ffn_prev = mark(
        (grad_fkey_in * (1.0 - channel_lookup_share) + grad_frecep_in * (1.0 - channel_gate_share))
        * keep[:, :, None]
    )
    first_row = gate(grad_ffn_prev[:, 0, :])
    ffn_back_edge, frecep_far, grad_frecep_far = at_once(
        ready,
        lambda: (
            shifted(first_row, "seq", -1),
            send_whole(flat(ffn_recep_mixed)),
            send_half(flat(grad_frecep)),
        ),
    )
    mark(ffn_back_edge)
    grad_ffn_normed = (
        grad_fkey_in * channel_lookup_share
        + grad_frecep_in * channel_gate_share
        + jnp.concatenate([grad_ffn_prev[:, 1:, :], ffn_back_edge[:, None, :]], axis=1)
    )
    grad_ffn_ln_gain = jnp.sum(grad_ffn_normed * ffn_unit, axis=(0, 1))
    grad_ffn_ln_bias = jnp.sum(grad_ffn_normed, axis=(0, 1))
    grad_after = grad_top + norm_back(grad_ffn_normed, ffn_unit, ffn_inv, channel_norm_scale)

    grad_att_out = mark(grad_after.astype(BF16), fkey_far[1])
    grad_gated = project_back(gate(grad_att_out), emission_matrix)
    grad_num, grad_den, grad_recep, tail = scan_call(
        backward_tails_kernel,
        [grad_gated, key_proj, value_proj, recep_proj, num_state, den_state, back_windows, rate_row, bonus_row],
        [(full, F32), (full, F32), (full, BF16), tails],
    )
    fr = Partial("FR", (flat(ffn_recep_mixed), frecep_far), (flat(grad_frecep), grad_frecep_far))
    gated_tail = gate(mark(tail))
    state, (recep_far, out_far), fr.halves = at_once(
        ready,
        lambda: (
            enter(gated_tail, backward=True),
            send_half_of((flat(grad_recep), flat(grad_att_out))),
            fr.products(),
        ),
    )
    mark(state)

    step = functools.partial(phase, line, ready)
    ou = Partial("OU", (gated, gated_far), (flat(grad_att_out), out_far))
    ar = Partial("AR", recep_side, (flat(grad_recep), recep_far))
    fkey_cross = exchange(gate(fkey_far[1]), CORE)
    fvalue_cross = exchange(gate(fvalue_far[1]), CORE)
    ou.multiply(line)
    ar.multiply(line)
    mark(fkey_cross, fvalue_cross, ar.halves[0])

    def hidden_halves():
        made = hidden_products(
            flat(ffn_key_mixed),
            (*fkey_far, fkey_cross),
            flat(grad_fvalue),
            (*fvalue_far, fvalue_cross),
            channel_lookup_matrix,
            channel_payload_matrix,
        )
        return [Blocks(name, value).first() for name, value in zip(("BV", "BK"), made)]

    halves = step([fr, ou, ar], hidden_halves)
    big_value, big_key = [Blocks(name, None, pair) for name, pair in zip(("BV", "BK"), halves)]
    big_key.forward(line)
    big_value.forward(line)
    grad_key, grad_value, sums = step(
        [ar, ou],
        lambda: scan_call(
            backward_states_kernel,
            [grad_num, grad_den, key_proj, value_proj, num_state, den_state, back_windows, rate_row, bonus_row, state],
            [(full, BF16), (full, BF16), ((16, features), F32)],
        ),
    )
    (key_far, value_far), grad_key_in, grad_value_in, grad_recep_in = step(
        [],
        lambda: (
            send_half_of((flat(grad_key), flat(grad_value))),
            project_back(grad_key, lookup_matrix),
            project_back(grad_value, payload_matrix),
            project_back(grad_recep, gate_matrix),
        ),
    )
    reward_slope = jnp.sum(sums[:8], axis=0)
    grad_time_decay = -decay_rate * jnp.exp(-decay_rate) * jnp.sum(sums[8:], axis=0)
    ak = Partial("AK", key_side, (flat(grad_key), key_far))
    av = Partial("AV", value_side, (flat(grad_value), value_far))
    ak.multiply(line)

    def mixes():
        normed = att_unit_again() * mixer_norm_scale + mixer_norm_offset
        att_delta = normed - with_previous(normed, att_edge, keep)
        att_back = (
            grad_key_in * (1.0 - temporal_lookup_share)
            + grad_value_in * (1.0 - temporal_payload_share)
            + grad_recep_in * (1.0 - temporal_gate_share)
        ) * keep[:, :, None]
        return (
            shifted(att_back[:, 0, :], "seq", -1),
            att_back,
            av.products(),
            jnp.sum(grad_key_in * att_delta, axis=(0, 1)),
            jnp.sum(grad_value_in * att_delta, axis=(0, 1)),
            jnp.sum(grad_recep_in * att_delta, axis=(0, 1)),
            grad_key_in * temporal_lookup_share
            + grad_value_in * temporal_payload_share
            + grad_recep_in * temporal_gate_share,
        )

    big_key.forward(line)
    big_value.forward(line)
    att_back_edge, grad_att_prev, av.halves, grad_mix_key, grad_mix_value, grad_mix_recep, direct = step(
        [ak], mixes
    )
    big_key.forward(line)
    big_value.forward(line)
    two = Stacked(line, [fr, ak])

    def norm_att():
        att_unit = att_unit_again()
        grad_att_normed = direct + jnp.concatenate(
            [grad_att_prev[:, 1:, :], att_back_edge[:, None, :]], axis=1
        )
        grad_tokens = (
            grad_after + norm_back(grad_att_normed, att_unit, att_inv, mixer_norm_scale)
        ).astype(BF16)
        return (
            grad_tokens,
            jnp.sum(grad_att_normed * att_unit, axis=(0, 1)),
            jnp.sum(grad_att_normed, axis=(0, 1)),
        )

    grad_tokens, grad_att_ln_gain, grad_att_ln_bias = step([two, av, ar], norm_att)
    vectors = Vectors(
        jnp.stack(
            [
                grad_att_ln_gain,
                grad_att_ln_bias,
                grad_mix_key,
                grad_mix_value,
                grad_mix_recep,
                grad_time_decay,
                reward_slope,
                grad_ffn_ln_gain,
                grad_ffn_ln_bias,
                grad_ffn_mix_key,
                grad_ffn_mix_recep,
            ]
        )
    )
    step([av, ou, vectors])
    big_key.forward(line)
    big_value.forward(line)
    three, pair = Stacked(line, [two, av]), Stacked(line, [ou, ar])
    step([three, pair, vectors])
    pairs = big_value.arrived(line), big_key.arrived(line)

    (ou_sum, ar_sum), quarters = step(
        [three, vectors],
        lambda: at_once(ready, lambda: (gather(total_of(pair.terms)), join_hidden(*pairs))),
    )
    (fr_sum, ak_sum, av_sum), (got, (value_sum, key_sum)) = step(
        [],
        lambda: gather(
            total_of(three.terms),
            lambda: at_once(ready, lambda: (vectors.hop(), whole_hidden(*quarters))),
        ),
    )
    small = lax.optimization_barrier(got)
    return (
        layer_out,
        grad_tokens,
        *[small[i] for i in range(7)],
        ak_sum,
        av_sum,
        ar_sum,
        ou_sum,
        *[small[i] for i in range(7, 11)],
        key_sum,
        value_sum,
        fr_sum,
    )


def solution(mesh):
    tokens = P("batch", "seq", None)
    vector, matrix = P("seq"), P("seq", None)
    return jax.shard_map(
        shards,
        mesh=mesh,
        in_specs=(tokens, P("batch", None), *([P()] * 18), tokens),
        out_specs=(tokens, tokens, *([vector] * 7), *([matrix] * 4), *([vector] * 4), *([matrix] * 3)),
        check_vma=False,
    )
```

```python
import functools
import math

import jax
import jax.numpy as jnp
from jax import lax
from jax.experimental import pallas as pl
from jax.experimental.pallas import tpu as pltpu
from jax.sharding import PartitionSpec as P

F32, BF16 = jnp.float32, jnp.bfloat16


def shifted(value, axis, distance):
    devices = range(lax.axis_size(axis))
    route = [(i - distance, i) for i in devices if i - distance in devices]
    return lax.ppermute(value, axis, route)


def bit_value(bit):
    axis, place = bit
    return (lax.axis_index(axis) >> place) & 1


def exchange(value, bit):
    axis, place = bit
    return lax.ppermute(value, axis, [(i, i ^ (1 << place)) for i in range(lax.axis_size(axis))])


def pick(value, index, dim):
    return lax.dynamic_index_in_dim(value, index, dim, keepdims=False)


def total_of(terms):
    return functools.reduce(lambda a, b: a + b, terms)


def axis_bits(axis):
    return [(axis, k) for k in range(int(math.log2(lax.axis_size(axis))))]


def at_once(ready, step, *values):
    blank = lambda *v: jax.tree.map(
        lambda x: jnp.zeros(x.shape, x.dtype), jax.eval_shape(step, *v)
    )
    return lax.cond(ready, step, blank, *values)


class Line:
    def __init__(self):
        self.token = None

    def gate(self, value):
        if self.token is None:
            return value
        return lax.optimization_barrier((value, self.token))[0]

    def mark(self, value, *others):
        self.token = (value, *others)
        return value


CORE = ("batch", 0)


def send_half(value):
    half = value.shape[1] // 2
    theirs = lax.dynamic_slice_in_dim(value, (1 - bit_value(CORE)) * half, half, 1)
    return exchange(theirs.astype(F32), CORE)


def send_half_of(values):
    half = values[0].shape[1] // 2
    at = (1 - bit_value(CORE)) * half
    theirs = [lax.dynamic_slice_in_dim(v, at, half, 1).astype(F32) for v in values]
    got = exchange(jnp.concatenate(theirs, axis=0), CORE)
    return jnp.split(got, len(values), axis=0)


def send_whole(value):
    return exchange(value.astype(F32), CORE)


CROSS = ("batch", 1)


def send_across(value):
    value = value.astype(F32)
    return exchange(value, CORE), exchange(value, CROSS)


def hidden_kernel(
    at_ref, *refs, unit,
):
    lefts, grads, (up_a, up_b, down_a, down_b, *outs, left_all, grad_all) = refs[:4], refs[4:8], refs[8:]
    value_send, value_keep, key_send, key_keep = outs
    z = pl.program_id(0) & 1
    tokens = lefts[0].shape[0]

    @pl.when(pl.program_id(0) == 0)
    def _():
        for k in range(4):
            at = pl.ds(k * tokens, tokens)
            left_all[at, :] = lefts[k][...].astype(BF16)
            grad_all[at, :] = grads[k][...].astype(BF16)

    up = jnp.concatenate([up_a[...], up_b[...]], axis=1)
    down = jnp.concatenate([down_a[...], down_b[...]], axis=0)
    first = lambda a, b: lax.dot_general(a, b, (((0,), (0,)), ((), ())), preferred_element_type=F32)

    def products(k):
        at = pl.ds(k * 2 * tokens, 2 * tokens)
        left, grad = left_all[at, :], grad_all[at, :]
        above = jnp.maximum(jnp.dot(left, up, preferred_element_type=F32), 0.0)
        back = lax.dot_general(grad, down, (((1,), (1,)), ((), ())), preferred_element_type=F32)
        return first((above * above).astype(BF16), grad), first((back * (2.0 * above)).astype(BF16), left)

    def put(value, key, add):
        def store(ref, index, part):
            ref[index] = ref[index] + part if add else part

        def values(ref):
            for half in range(2):
                store(ref, (0, half), value[half * unit : (half + 1) * unit])

        def keys(even, odd):
            rows = key.shape[1] // 8
            for s in range(8):
                store((even, odd)[s & 1], s >> 1, key[:, s * rows : (s + 1) * rows])

        pl.when(z == at_ref[1])(lambda: values(value_keep))
        pl.when(z != at_ref[1])(lambda: values(value_send))
        pl.when(at_ref[2] == 0)(lambda: keys(key_keep, key_send))
        pl.when(at_ref[2] != 0)(lambda: keys(key_send, key_keep))

    put(*products(0), False)
    put(*products(1), True)


def hidden_products(left, far_lefts, grad, far_grads, up, down):
    seq, tokens, features = lax.axis_size("seq"), left.shape[0], left.shape[1]
    unit = up.shape[1] // seq // 4
    quarter = 2 * bit_value(CORE) + bit_value(CROSS)
    if unit % 128 or features // seq % 128 or seq != 8:
        up = pick(up.reshape(features, seq, 4, unit), quarter, 2).reshape(features, -1)
        down = pick(down.reshape(seq, 4, unit, features), quarter, 1).reshape(-1, features)
        lefts = jnp.concatenate([left, *[f.astype(BF16) for f in far_lefts]])
        grads = jnp.concatenate([grad, *[f.astype(BF16) for f in far_grads]])
        above = jnp.maximum(jnp.dot(lefts, up, preferred_element_type=F32), 0.0)
        back = lax.dot_general(grads, down, (((1,), (1,)), ((), ())), preferred_element_type=F32)
        first = lambda a, b: lax.dot_general(a, b, (((0,), (0,)), ((), ())), preferred_element_type=F32)
        value = first((above * above).astype(BF16), grads).reshape(seq, unit, features)
        key = first((back * (2.0 * above)).astype(BF16), lefts)
        key = jnp.swapaxes(key.reshape(-1, seq, features // seq), 0, 1)
        return Blocks("BV", value).first(), Blocks("BK", key).first()
    whole = lambda: pl.BlockSpec((tokens, features), lambda i, at: (0, 0), pipeline_mode=pl.Buffered(1))
    ups = [pl.BlockSpec((features, unit), lambda i, at, h=h: (0, 4 * (2 * i + h) + at[0])) for h in (0, 1)]
    downs = [pl.BlockSpec((unit, features), lambda i, at, h=h: (4 * (2 * i + h) + at[0], 0)) for h in (0, 1)]
    at = jnp.stack([quarter, *[bit_value(order_of(name)[0][0]) for name in ("BV", "BK")]])
    halves = [(2, 2, unit, features)] * 2 + [(4, seq * unit, features // seq)] * 2
    value_spec = pl.BlockSpec((1, 2, unit, features), lambda i, at: (i >> 1, 0, 0, 0))
    key_spec = pl.BlockSpec((4, 2 * unit, features // seq), lambda i, at: (0, i, 0))
    made = pl.pallas_call(
        functools.partial(hidden_kernel, unit=unit),
        grid_spec=pltpu.PrefetchScalarGridSpec(
            num_scalar_prefetch=1,
            grid=(seq // 2,),
            in_specs=[whole() for _ in range(8)] + ups + downs,
            out_specs=[value_spec, value_spec, key_spec, key_spec],
            scratch_shapes=[pltpu.VMEM((4 * tokens, features), BF16)] * 2,
        ),
        out_shape=[jax.ShapeDtypeStruct(shape, F32) for shape in halves],
        compiler_params=pltpu.CompilerParams(vmem_limit_bytes=56 * 1024 * 1024),
        cost_estimate=pl.CostEstimate(
            flops=32 * tokens * features * seq * unit,
            bytes_accessed=40 * tokens * features,
            transcendentals=0,
        ),
    )(at.astype(jnp.int32), left, *far_lefts, grad, *far_grads, up, up, down, down)
    made = [x.reshape(2, 2, *x.shape[-2:]) for x in made]
    return made[:2], made[2:]


ORDERS = dict(BV="zywx", BK="yzwx", FR="xyzw", OU="zxyw", AR="yxzw", AK="xyzw", AV="xyzw")


def order_of(name):
    seq = axis_bits("seq")
    places = dict(x=axis_bits("batch")[1:], y=seq[:1], z=seq[1:2], w=seq[2:])
    return [places[letter] for letter in ORDERS[name]]


def halve(terms, dims, bit):
    if bit not in dims:
        total = total_of(terms)
        return total, [total]
    dim, mine = dims.index(bit), bit_value(bit)
    send = total_of([pick(t, 1 - mine, dim) for t in terms])
    return send, [pick(t, mine, dim) for t in terms]


class Blocks:
    halves = None

    def __init__(self, name, value, halves=None):
        self.hops, self.dims = order_of(name), axis_bits("seq")[::-1]
        self.halves, self.terms = halves, None
        if halves is None:
            self.terms = [value.reshape(*((2,) * len(self.dims)), *value.shape[1:])]

    def first(self):
        send, kept = self.split(self.terms)
        return send, kept[0]

    def split(self, terms):
        if self.halves:
            return self.halves[0], [self.halves[1]]
        return halve(terms, self.dims, self.hops[0][0])

    def go(self, sends):
        bits, dims = self.hops[0], list(self.dims)
        got = exchange(sends, bits[0])
        if len(bits) == 1:
            return got
        terms = self.split(self.terms)[1] + [got]
        dims = [d for d in dims if d != bits[0]]
        for bit in bits[1:]:
            send, kept = halve(terms, dims, bit)
            terms = kept + [exchange(send, bit)]
            dims = [d for d in dims if d != bit]
        return total_of(terms)

    def hop(self):
        return self.go(self.split(self.terms)[0])

    def landed(self, got):
        bits = self.hops[0]
        self.terms = self.split(self.terms)[1] + [got] if len(bits) == 1 else [got]
        self.halves = None
        self.dims = [d for d in self.dims if d not in bits]
        self.hops.pop(0)

    def arrived(self, line):
        return self.terms[:-1] + [line.gate(self.terms[-1])]

    def forward(self, line):
        if self.halves:
            send = line.gate(self.halves[0])
        else:
            send = self.split(self.arrived(line))[0]
        self.landed(self.go(line.mark(send)))


def phase(line, ready, jobs, beside=None):
    def step():
        return [job.hop() for job in jobs], beside() if beside else ()

    got, more = at_once(line.gate(ready), step)
    for job, value in zip(jobs, got):
        job.landed(value)
    line.mark(*jax.tree.leaves((got, more)))
    return more


def product_kernel(
    at_ref, left_ref, far_left_ref, right_ref, far_right_ref, send_ref, keep_ref,
    *, rows, cols, group, place,
):
    first = at_ref[0]

    def lefts(blocks):
        cut = lambda ref, js: jnp.concatenate(
            [ref[:, pl.ds(pl.multiple_of(j * rows, 128), rows)] for j in js], axis=1
        )
        return jnp.concatenate([cut(left_ref, blocks), cut(far_left_ref, blocks).astype(BF16)], axis=0)

    def rights(x):
        at = pl.ds(pl.multiple_of(x * cols, 128), cols)
        return jnp.concatenate([right_ref[:, at], far_right_ref[:, at].astype(BF16)], axis=0)

    dot = lambda a, b: lax.dot_general(
        a, b, (((0,), (0,)), ((), ())), preferred_element_type=F32
    )
    for out, value in ((send_ref, 1 - first), (keep_ref, first)):
        if place is None:
            out[0] = dot(lefts(list(range(group))), rights(value))
        else:
            low = 1 << place
            blocks = [(q // low) * 2 * low + q % low + value * low for q in range(group // 2)]
            left = lefts(blocks)
            for x in range(2):
                out[x, 0] = dot(left, rights(x))


class Partial(Blocks):
    def __init__(self, name, left, right):
        self.left, self.right = left, right
        self.hops, self.terms = order_of(name), None
        self.dims = axis_bits("batch")[1:] + axis_bits("seq")[::-1]
        self.blocks = lax.axis_size("seq")
        self.rows = left[0].shape[1] // self.blocks
        self.cols = right[0].shape[1] // 4

    def plain(self):
        half = self.right[0].shape[1] // 2
        own = lax.dynamic_slice_in_dim(self.right[0], bit_value(CORE) * half, half, 1)
        dot = lambda a, b: lax.dot_general(
            a.astype(BF16), b.astype(BF16), (((0,), (0,)), ((), ())), preferred_element_type=F32
        )
        whole = dot(self.left[0], own) + dot(self.left[1], self.right[1])
        lead = (2,) * len(axis_bits("seq"))
        whole = jnp.moveaxis(whole.reshape(*lead, self.rows, 2, self.cols), -2, 0)
        send, kept = halve([whole], self.dims, self.hops[0][0])
        return send, kept[0]

    def kernel(self):
        rows, cols, tokens = self.rows, self.cols, self.left[0].shape[0]
        first = self.hops[0][0]
        place = first[1] if first[0] == "seq" else None
        group = 4
        steps = self.blocks // group
        if place is None:
            block, shape = (1, group * rows, cols), (steps, group * rows, cols)
            out_index = lambda i, at: (i, 0, 0)
        else:
            block, shape = (2, 1, group // 2 * rows, cols), (2, steps, group // 2 * rows, cols)
            out_index = lambda i, at: (0, i, 0, 0)
        out = jax.ShapeDtypeStruct(shape, F32)
        at = jnp.stack([bit_value(first), bit_value(CORE)]).astype(jnp.int32)
        send, kept = pl.pallas_call(
            functools.partial(
                product_kernel, rows=rows, cols=cols, group=group, place=place
            ),
            grid_spec=pltpu.PrefetchScalarGridSpec(
                num_scalar_prefetch=1,
                grid=(steps,),
                in_specs=[
                    pl.BlockSpec((tokens, group * rows), lambda i, at: (0, i)),
                    pl.BlockSpec((tokens, group * rows), lambda i, at: (0, i)),
                    pl.BlockSpec((tokens, 2 * cols), lambda i, at: (0, at[1])),
                    pl.BlockSpec((tokens, 2 * cols), lambda i, at: (0, 0)),
                ],
                out_specs=[pl.BlockSpec(block, out_index)] * 2,
            ),
            out_shape=[out, out],
            compiler_params=scan_params(),
            cost_estimate=pl.CostEstimate(
                flops=8 * tokens * self.blocks * rows * cols,
                bytes_accessed=8 * self.blocks * rows * cols,
                transcendentals=0,
            ),
        )(at, self.left[0], self.left[1], self.right[0], self.right[1])
        lead = (2,) * (len(self.dims) - 1)
        return send.reshape(*lead, rows, cols), kept.reshape(*lead, rows, cols)

    def products(self):
        aligned = self.rows % 128 == 0 and self.blocks % 4 == 0 and len(axis_bits("batch")) == 2
        return self.kernel() if aligned else self.plain()

    def multiply(self, line):
        self.left = (line.gate(self.left[0]), self.left[1])
        self.halves = self.products()
        line.mark(self.halves[0])


class Stacked(Blocks):
    def __init__(self, line, jobs):
        self.hops, self.dims = list(jobs[0].hops), jobs[0].dims
        sums = [total_of(j.arrived(line)) for j in jobs]
        sums = [v if isinstance(j, Stacked) else v[..., None, :, :] for j, v in zip(jobs, sums)]
        self.terms = [jnp.concatenate(sums, axis=-3)]


class Vectors(Blocks):
    def __init__(self, vectors):
        vectors = jnp.pad(vectors, ((0, -vectors.shape[0] % 8), (0, 0)))
        count, seq = vectors.shape[0], lax.axis_size("seq")
        self.dims = axis_bits("seq")[::-1]
        bits = axis_bits("seq")
        self.hops = [[b] for b in axis_bits("batch") + bits[:1]] + [bits[1:]]
        value = jnp.swapaxes(vectors.reshape(count, seq, -1), 0, 1)
        self.terms = [value.reshape(*((2,) * len(self.dims)), count, -1)]

def in_order(own, other, bit, axis):
    first = bit_value(bit) == 0
    return jnp.concatenate(
        [jnp.where(first, own, other), jnp.where(first, other, own)], axis=axis
    )


def gather(own, beside=None):
    other, more = exchange(own, CROSS), None
    if beside:
        other, more = lax.optimization_barrier((other, beside()))
    own = in_order(own, other, CROSS, 2)
    own = in_order(own, exchange(own, CORE), CORE, 2)
    joined = [own[i] for i in range(own.shape[0])]
    return (joined, more) if beside else joined


def join_hidden(values, keys):
    seq = lax.axis_size("seq")
    value = in_order(*values, CROSS, 0)
    key = in_order(*[t.reshape(seq, 1, -1, t.shape[-1]) for t in keys], CROSS, 1)
    return (value, exchange(value, CORE)), (key, exchange(key, CORE))


def whole_hidden(values, keys):
    key = in_order(*keys, CORE, 1)
    return in_order(*values, CORE, 0), jnp.transpose(key.reshape(-1, key.shape[-1]))


def entering(tails, begins, decay_rate, group_len, backward):
    count, mine = lax.axis_size("seq"), lax.axis_index("seq")
    sign, radix = (-1, 4) if backward else (1, 2)

    def gain(lo, hi):
        a, b = (mine + lo, mine + hi) if backward else (mine - hi + 1, mine - lo + 1)
        hit = jnp.any((begins >= a * group_len) & (begins < b * group_len), axis=1, keepdims=True)
        return jnp.where(hit, 0.0, 1.0) * jnp.exp(-float((hi - lo) * group_len) * decay_rate)[None, :]

    reach, window, before = 1, tails, None
    while reach < count:
        got = [
            (j, shifted(window, "seq", sign * j * reach))
            for j in range(1, radix)
            if j * reach < count
        ]
        if before is None:
            before = total_of([v if j == 1 else gain(1, j) * v for j, v in got])
            seen = 1 + len(got)
            window = tails + gain(0, 1) * before if seen < count else None
        else:
            before_more = total_of([gain(1, j * reach) * v for j, v in got])
            seen = reach * (1 + len(got))
            if seen < count:
                window = window + total_of([gain(0, j * reach) * v for j, v in got])
            before = before + before_more
        reach *= radix
    return before


def scan_params():
    return pltpu.CompilerParams(vmem_limit_bytes=48 * 1024 * 1024)


def lane_tiles(width):
    return [slice(i, i + 128) for i in range(0, width, 128)]


WINDOW = {name: k for k, name in enumerate(("keep", "one", "two", "four", "group", "eight", "end"))}


def windows_kernel(sizes_ref, block_ref, ahead_ref, back_ref):
    rows, length, width = ahead_ref.shape[1:]
    t = lax.broadcasted_iota(jnp.int32, (length, width), 0)
    inner = t & 7

    def put(ref, name, equal, inside=None):
        kept = equal if inside is None else equal & inside
        ref[WINDOW[name], row] = jnp.where(kept, 1.0, 0.0)

    for row in range(rows):
        begins, at = [], -block_ref[0]
        for j in range(sizes_ref.shape[1]):
            begins.append(at)
            at = at + sizes_ref[row, j]

        def begun(by):
            return total_of([jnp.where(by >= b, 1, 0) for b in begins])

        here, ahead_of = begun(t), begun(t - 1)
        keep = here == ahead_of
        put(ahead_ref, "keep", keep)
        put(back_ref, "keep", keep)
        for name, n in (("one", 1), ("two", 2), ("four", 4)):
            put(ahead_ref, name, here == begun(t - n), inner >= n)
            put(back_ref, name, begun(t + (n - 1)) == ahead_of, inner <= 7 - n)
        put(ahead_ref, "group", here == begun(t - inner - 1))
        put(back_ref, "group", begun(t - inner + 7) == ahead_of)
        put(ahead_ref, "eight", here == begun(t - 8), t >= 8)
        put(back_ref, "eight", begun(t + 7) == ahead_of, t < length - 8)
        put(ahead_ref, "end", here == begun(jnp.full_like(t, length - 1)))
        put(back_ref, "end", ahead_of == begun(jnp.full_like(t, -1)))


def keep_windows(sizes, length, width):
    block = (lax.axis_index("seq") * length)[None].astype(jnp.int32)
    out = jax.ShapeDtypeStruct((len(WINDOW), sizes.shape[0], length, width), F32)
    return pl.pallas_call(
        windows_kernel,
        out_shape=[out, out],
        in_specs=[pl.BlockSpec(memory_space=pltpu.SMEM)] * 2,
        compiler_params=scan_params(),
        cost_estimate=pl.CostEstimate(flops=100 * out.size, bytes_accessed=8 * out.size, transcendentals=0),
    )(sizes, block)


def powers(rate_ref, tiles):
    return lambda n: [jnp.exp(-n * rate_ref[0:1, t]) for t in tiles]


def inner_place(shape=(8, 128)):
    return lax.broadcasted_iota(jnp.int32, shape, 0)


def spread(row):
    return jnp.broadcast_to(row, (8, 128))


def in_group(value, factors, back):
    for n, factor in zip((1, 2, 4), factors):
        value = value + factor * pltpu.roll(value, 8 - n if back else n, 0)
    return value


def halves_of(ref, row, at, tile):
    value = ref[row, at, tile]
    return value[:8], value[8:]


def windows_at(win_ref, row, at):
    names = ("keep", "one", "two", "four", "group")
    return [dict(zip(names, v)) for v in zip(*[halves_of(win_ref.at[WINDOW[n]], row, at, slice(None)) for n in names])]


def pair_at(p):
    return pl.ds(pl.multiple_of(p * 16, 16), 16)


def forward_tails_kernel(k_ref, v_ref, win_ref, rate_ref, tail_ref):
    rows, length, width = k_ref.shape
    tiles = lane_tiles(width)
    chains = [(r, i, t) for r in range(rows) for i, t in enumerate(tiles)]
    eight = powers(rate_ref, tiles)(8.0)

    def step(p, carry):
        at, out = pair_at(p), []
        windows = [halves_of(win_ref.at[WINDOW["eight"]], r, at, slice(None)) for r in range(rows)]
        for (r, i, t), (num, den) in zip(chains, carry):
            for h, (key, value) in enumerate(zip(halves_of(k_ref, r, at, t), halves_of(v_ref, r, at, t))):
                factor, e = windows[r][h] * eight[i], jnp.exp(key)
                num, den = factor * num + e * value, factor * den + e
            out.append((num, den))
        return tuple(out)

    zero = jnp.zeros((8, 128), F32)
    done = lax.fori_loop(0, length // 16, step, tuple((zero, zero) for _ in chains), unroll=2)
    left = powers(rate_ref, tiles)((7 - inner_place()).astype(F32))
    for (r, i, t), pair in zip(chains, done):
        factor = win_ref[WINDOW["end"], r, pl.ds(length - 8, 8), :] * left[i]
        for q in range(2):
            tail_ref[q, r : r + 1, t] = jnp.sum(factor * pair[q], axis=0, keepdims=True)


def forward_states_kernel(
    k_ref, v_ref, recep_ref, win_ref, rate_ref, bonus_ref, enter_ref, num_ref, den_ref, gated_ref
):
    rows, length, width = k_ref.shape
    tiles = lane_tiles(width)
    chains = [(r, i, t) for r in range(rows) for i, t in enumerate(tiles)]
    power = powers(rate_ref, tiles)
    ones, twos, fours = power(1.0), power(2.0), power(4.0)
    groups = power((1 + inner_place()).astype(F32))
    head = inner_place() == 0

    def step(p, carry):
        at, out = pair_at(p), []
        windows = [windows_at(win_ref, r, at) for r in range(rows)]
        for (r, i, t), states in zip(chains, carry):
            keys, values = halves_of(k_ref, r, at, t), halves_of(v_ref, r, at, t)
            receps, bonus, results = halves_of(recep_ref, r, at, t), bonus_ref[0:1, t], []
            for h in range(2):
                w = windows[r][h]
                factors = (w["one"] * ones[i], w["two"] * twos[i], w["four"] * fours[i])
                group = w["group"] * groups[i]
                e, held, here = jnp.exp(keys[h]), [], []
                for state, item in zip(states, (e * values[h], e)):
                    full = in_group(item, factors, False) + group * state
                    here.append(w["keep"] * jnp.where(head, state, pltpu.roll(full, 1, 0)))
                    held.append(spread(full[7:8]))
                states = held
                first = jnp.exp(bonus + keys[h])
                wkv = (here[0] + first * values[h]) / (here[1] + first)
                results.append((*here, jax.nn.sigmoid(receps[h]) * wkv))
            for ref, two in zip((num_ref, den_ref, gated_ref), zip(*results)):
                ref[r, at, t] = jnp.concatenate(two, axis=0).astype(ref.dtype)
            out.append(tuple(states))
        return tuple(out)

    start = tuple(tuple(spread(enter_ref[q, r : r + 1, t]) for q in range(2)) for r, _, t in chains)
    lax.fori_loop(0, length // 16, step, start)


def backward_tails_kernel(
    grad_ref, k_ref, v_ref, recep_ref, num_ref, den_ref, win_ref, rate_ref, bonus_ref,
    gnum_ref, gden_ref, grecep_ref, tail_ref,
):
    rows, length, width = k_ref.shape
    tiles = lane_tiles(width)
    chains = [(r, i, t) for r in range(rows) for i, t in enumerate(tiles)]
    eight = powers(rate_ref, tiles)(8.0)
    pairs = length // 16

    def step(p, carry):
        at, out = pair_at(pairs - 1 - p), []
        keeps = [halves_of(win_ref.at[WINDOW["keep"]], r, at, slice(None)) for r in range(rows)]
        windows = [halves_of(win_ref.at[WINDOW["eight"]], r, at, slice(None)) for r in range(rows)]
        for (r, i, t), (late_num, late_den) in zip(chains, carry):
            key, value = k_ref[r, at, t], v_ref[r, at, t]
            first = jnp.exp(bonus_ref[0:1, t] + key)
            below = den_ref[r, at, t] + first
            wkv = (num_ref[r, at, t] + first * value) / below
            gate, grad = jax.nn.sigmoid(recep_ref[r, at, t]), grad_ref[r, at, t]
            grecep_ref[r, at, t] = (grad * wkv * (gate * (1.0 - gate))).astype(BF16)
            up = grad * gate / below
            low = -up * wkv
            gnum_ref[r, at, t] = up
            gden_ref[r, at, t] = low
            for h in (1, 0):
                rows_of = slice(8 * h, 8 * h + 8)
                factor, keep = windows[r][h] * eight[i], keeps[r][h]
                late_num = factor * late_num + keep * up[rows_of]
                late_den = factor * late_den + keep * low[rows_of]
            out.append((late_num, late_den))
        return tuple(out)

    zero = jnp.zeros((8, 128), F32)
    done = lax.fori_loop(0, pairs, step, tuple((zero, zero) for _ in chains))
    left = powers(rate_ref, tiles)(inner_place().astype(F32))
    for (r, i, t), pair in zip(chains, done):
        factor = win_ref[WINDOW["end"], r, pl.ds(0, 8), :] * left[i]
        for q in range(2):
            tail_ref[q, r : r + 1, t] = jnp.sum(factor * pair[q], axis=0, keepdims=True)


def backward_states_kernel(
    gnum_ref, gden_ref, k_ref, v_ref, num_ref, den_ref, win_ref, rate_ref, bonus_ref, enter_ref,
    gkey_ref, gvalue_ref, sums_ref,
):
    rows, length, width = k_ref.shape
    tiles = lane_tiles(width)
    chains = [(r, i, t) for r in range(rows) for i, t in enumerate(tiles)]
    power = powers(rate_ref, tiles)
    ones, twos, fours = power(1.0), power(2.0), power(4.0)
    groups = power((8 - inner_place()).astype(F32))
    tail = inner_place() == 7
    pairs = length // 16

    def step(p, carry):
        at, out = pair_at(pairs - 1 - p), []
        windows = [windows_at(win_ref, r, at) for r in range(rows)]
        for (r, i, t), (num_state, den_state, slope, fade) in zip(chains, carry):
            states, parts = (num_state, den_state), []
            keys, values = halves_of(k_ref, r, at, t), halves_of(v_ref, r, at, t)
            ups, lows = halves_of(gnum_ref, r, at, t), halves_of(gden_ref, r, at, t)
            nums, dens = halves_of(num_ref, r, at, t), halves_of(den_ref, r, at, t)
            for h in (1, 0):
                w = windows[r][h]
                factors = (w["one"] * ones[i], w["two"] * twos[i], w["four"] * fours[i])
                group, held, here = w["group"] * groups[i], [], []
                for state, item in zip(states, (ups[h], lows[h])):
                    full = in_group(w["keep"] * item, factors, True) + group * state
                    here.append(jnp.where(tail, state, pltpu.roll(full, 7, 0)))
                    held.append(spread(full[0:1]))
                states = held
                e, first = jnp.exp(keys[h]), jnp.exp(bonus_ref[0:1, t] + keys[h])
                present = first * (ups[h] * values[h] + lows[h])
                slope = slope + present
                fade = fade + nums[h] * here[0] + dens[h] * here[1]
                parts.append(
                    (
                        present + e * (here[0] * values[h] + here[1]),
                        ups[h] * first + here[0] * e,
                    )
                )
            for ref, two in zip((gkey_ref, gvalue_ref), zip(*parts[::-1])):
                ref[r, at, t] = jnp.concatenate(two, axis=0).astype(BF16)
            out.append((*states, slope, fade))
        return tuple(out)

    zero = jnp.zeros((8, 128), F32)
    start = tuple(
        (*[spread(enter_ref[q, r : r + 1, t]) for q in range(2)], zero, zero) for r, _, t in chains
    )
    done = lax.fori_loop(0, pairs, step, start)
    for i, t in enumerate(tiles):
        for q in range(2):
            sums_ref[8 * q : 8 * q + 8, t] = total_of(
                [c[2 + q] for (_, j, _), c in zip(chains, done) if j == i]
            )


def scan_call(kernel, inputs, outputs, width=512):
    features = inputs[0].shape[-1]

    def spec(shape):
        lead = len(shape) - 1
        if shape[-1] == 128 and features != 128:
            return pl.BlockSpec(shape, lambda i: (0,) * (lead + 1))
        return pl.BlockSpec((*shape[:-1], width), lambda i: (0,) * lead + (i,))

    out_shape = [jax.ShapeDtypeStruct(s, d) for s, d in outputs]
    moved = sum(x.size * x.dtype.itemsize for x in [*inputs, *out_shape])
    return pl.pallas_call(
        kernel,
        out_shape=out_shape,
        grid=(features // width,),
        in_specs=[spec(x.shape) for x in inputs],
        out_specs=[spec(s) for s, _ in outputs],
        compiler_params=scan_params(),
        cost_estimate=pl.CostEstimate(
            flops=20 * inputs[0].size, bytes_accessed=moved, transcendentals=inputs[0].size
        ),
    )(*inputs)


def channel_kernel(
    left_ref, recep_ref, up_ref, down_ref, gate_ref, after_ref, top_ref,
    out_ref, fvalue_ref, frecep_ref, fkey_ref, recep_in_ref, above_ref, total_ref,
):
    across = (((1,), (1,)), ((), ()))
    block = up_ref.shape[1]
    step, blocks = pl.program_id(0), pl.num_programs(0) // 2

    def at(i):
        return pl.ds(pl.multiple_of(i * block, block), block)

    def add(ref, first, part):
        @pl.when(step == first)
        def _():
            ref[...] = part

        @pl.when(step > first)
        def _():
            ref[...] += part

    @pl.when(step < blocks)
    def _():
        above = jnp.maximum(jnp.dot(left_ref[...], up_ref[...], preferred_element_type=F32), 0.0)
        above_ref[:, at(step)] = above
        add(total_ref, 0, jnp.dot((above * above).astype(BF16), down_ref[...], preferred_element_type=F32))

    @pl.when(step == blocks - 1)
    def _():
        value = total_ref[...]
        gate = jax.nn.sigmoid(
            jnp.dot(recep_ref[...], gate_ref[...], preferred_element_type=F32)
        )
        top = top_ref[...].astype(F32)
        out_ref[...] = (after_ref[...] + gate * value).astype(BF16)
        fvalue_ref[...] = (top * gate).astype(BF16)
        frecep = (top * value * (gate * (1.0 - gate))).astype(BF16)
        frecep_ref[...] = frecep
        recep_in_ref[...] = lax.dot_general(
            frecep, gate_ref[...], across, preferred_element_type=F32
        )

    @pl.when(step >= blocks)
    def _():
        back = lax.dot_general(fvalue_ref[...], down_ref[...], across, preferred_element_type=F32)
        hidden = (back * (2.0 * above_ref[:, at(step - blocks)])).astype(BF16)
        add(fkey_ref, blocks, lax.dot_general(hidden, up_ref[...], across, preferred_element_type=F32))


def channel_mix(left, recep, up, down, gate, after, top):
    (tokens, features), hidden = left.shape, up.shape[1]
    block = min(1024, hidden)
    blocks = hidden // block
    once = lambda x: pl.BlockSpec(x.shape, lambda i: (0, 0), pipeline_mode=pl.Buffered(1))
    shape = (tokens, features)
    return pl.pallas_call(
        channel_kernel,
        out_shape=[jax.ShapeDtypeStruct(shape, d) for d in (BF16, BF16, BF16, F32, F32)],
        grid=(2 * blocks,),
        in_specs=[
            once(left),
            once(recep),
            pl.BlockSpec((features, block), lambda i: (0, lax.rem(i, blocks))),
            pl.BlockSpec((block, features), lambda i: (lax.rem(i, blocks), 0)),
            once(gate),
            once(after),
            once(top),
        ],
        out_specs=[pl.BlockSpec(shape, lambda i: (0, 0))] * 5,
        scratch_shapes=[pltpu.VMEM((tokens, hidden), F32), pltpu.VMEM(shape, F32)],
        compiler_params=pltpu.CompilerParams(vmem_limit_bytes=56 * 1024 * 1024),
        cost_estimate=pl.CostEstimate(
            flops=8 * tokens * features * (hidden + features // 2),
            bytes_accessed=8 * features * hidden + 20 * tokens * features,
            transcendentals=tokens * features,
        ),
    )(left, recep, up, down, gate, after, top)


def norm_rows(value_rows, gain_vec, bias_vec):
    row_mean = jnp.mean(value_rows, axis=-1, keepdims=True)
    centred = value_rows - row_mean
    inv_std = lax.rsqrt(jnp.mean(centred * centred, axis=-1, keepdims=True) + 1e-05)
    normed = centred * inv_std
    return (normed * gain_vec + bias_vec, normed, inv_std)


def norm_back(grad_in, normed, inv_std, gain_vec):
    scaled = grad_in * gain_vec
    return inv_std * (
        scaled
        - jnp.mean(scaled, axis=-1, keepdims=True)
        - normed * jnp.mean(scaled * normed, axis=-1, keepdims=True)
    )


def project(left_side, right_side):
    return jnp.einsum("rcd,de->rce", left_side, right_side, preferred_element_type=F32)


def project_back(grad_in, right_side):
    return jnp.einsum("rce,de->rcd", grad_in, right_side, preferred_element_type=F32)


def with_previous(value_rows, edge_row, keep):
    earlier = jnp.concatenate([edge_row[:, None, :], value_rows[:, :-1, :]], axis=1)
    return earlier * keep[:, :, None]


def flat(value):
    return value.reshape(-1, value.shape[-1])


def shards(
    incoming_symbols,
    article_sizes,
    mixer_norm_scale,
    mixer_norm_offset,
    temporal_lookup_share,
    temporal_payload_share,
    temporal_gate_share,
    fading_log_rates,
    present_reward_vector,
    lookup_matrix,
    payload_matrix,
    gate_matrix,
    emission_matrix,
    channel_norm_scale,
    channel_norm_offset,
    channel_lookup_share,
    channel_gate_share,
    channel_lookup_matrix,
    channel_payload_matrix,
    channel_gate_matrix,
    final_cotangent,
):
    rows_here, group_len, features = incoming_symbols.shape
    full = (rows_here, group_len, features)
    begins = jnp.cumsum(article_sizes, axis=1) - article_sizes
    position = lax.axis_index("seq") * group_len + jnp.arange(group_len, dtype=jnp.int32)
    starts = jnp.any(position[None, :, None] == begins[:, None, :], axis=2)
    keep = jnp.where(starts, 0.0, 1.0).astype(F32)
    ahead_windows, back_windows = keep_windows(article_sizes, group_len, 128)
    decay_rate = jnp.exp(fading_log_rates)
    rate_row = jnp.broadcast_to(decay_rate[None, :], (8, features))
    bonus_row = jnp.broadcast_to(present_reward_vector[None, :], (8, features))
    ready = article_sizes[0, 0] > 0
    enter = functools.partial(entering, begins=begins, decay_rate=decay_rate, group_len=group_len)

    symbols = incoming_symbols.astype(F32)
    att_last = norm_rows(symbols[:, -1, :], mixer_norm_scale, mixer_norm_offset)[0]
    att_edge = shifted(att_last, "seq", 1)
    att_normed, _, att_inv = norm_rows(symbols, mixer_norm_scale, mixer_norm_offset)
    att_mean = jnp.mean(symbols, axis=-1, keepdims=True)
    att_unit_again = lambda: (incoming_symbols.astype(F32) - att_mean) * att_inv
    att_prev = with_previous(att_normed, att_edge, keep)
    mix = lambda share: (att_normed * share + att_prev * (1.0 - share)).astype(BF16)
    key_mixed = mix(temporal_lookup_share)
    value_mixed = mix(temporal_payload_share)
    recep_mixed = mix(temporal_gate_share)
    key_proj = project(key_mixed, lookup_matrix)
    value_proj = project(value_mixed, payload_matrix)
    recep_proj = project(recep_mixed, gate_matrix)
    tails = ((2, rows_here, features), F32)
    (tail,) = scan_call(
        forward_tails_kernel, [key_proj, value_proj, ahead_windows, rate_row], [tails]
    )
    key_mixed, value_mixed, recep_mixed = map(flat, (key_mixed, value_mixed, recep_mixed))
    state, key_far, value_far, recep_far = at_once(
        ready,
        lambda: (enter(tail, backward=False), *map(send_whole, (key_mixed, value_mixed, recep_mixed))),
    )
    key_side, value_side, recep_side = (
        (key_mixed, key_far), (value_mixed, value_far), (recep_mixed, recep_far)
    )
    num_state, den_state, gated = scan_call(
        forward_states_kernel,
        [key_proj, value_proj, recep_proj, ahead_windows, rate_row, bonus_row, state],
        [(full, F32), (full, F32), (full, BF16)],
    )
    after_att = symbols + project(gated, emission_matrix)

    ffn_normed, ffn_unit, ffn_inv = norm_rows(after_att, channel_norm_scale, channel_norm_offset)
    gated = flat(gated)
    last_rows = ffn_normed[:, -1, :]
    ffn_edge, gated_far = at_once(
        ready, lambda: (shifted(last_rows, "seq", 1), send_whole(gated))
    )
    gated_side = (gated, gated_far)
    ffn_prev = with_previous(ffn_normed, ffn_edge, keep)
    def ffn_mix(share):
        rounded = lax.reduce_precision(ffn_normed * share + ffn_prev * (1.0 - share), 8, 7)
        return rounded.astype(BF16), rounded

    ffn_key_mixed, ffn_key_wide = ffn_mix(channel_lookup_share)
    ffn_recep_mixed, ffn_recep_wide = ffn_mix(channel_gate_share)
    line = Line()
    gate, mark = line.gate, line.mark
    fkey_far = send_across(flat(ffn_key_wide))
    layer_out, grad_fvalue, grad_frecep, grad_fkey_in, grad_frecep_in = channel_mix(
        flat(ffn_key_mixed), flat(ffn_recep_mixed), channel_lookup_matrix, channel_payload_matrix,
        channel_gate_matrix, flat(after_att), flat(final_cotangent),
    )
    layer_out, grad_fkey_in, grad_frecep_in = [
        x.reshape(full) for x in (layer_out, grad_fkey_in, grad_frecep_in)
    ]

    grad_top = final_cotangent.astype(F32)
    mark(grad_fvalue)
    fvalue_far = send_across(flat(grad_fvalue))
    ffn_delta = ffn_normed - ffn_prev
    grad_ffn_mix_key = jnp.sum(grad_fkey_in * ffn_delta, axis=(0, 1))
    grad_ffn_mix_recep = jnp.sum(grad_frecep_in * ffn_delta, axis=(0, 1))
    grad_ffn_prev = mark(
        (grad_fkey_in * (1.0 - channel_lookup_share) + grad_frecep_in * (1.0 - channel_gate_share))
        * keep[:, :, None]
    )
    first_row = gate(grad_ffn_prev[:, 0, :])
    ffn_back_edge, frecep_far, grad_frecep_far = at_once(
        ready,
        lambda: (
            shifted(first_row, "seq", -1),
            send_whole(flat(ffn_recep_wide)),
            send_half(flat(grad_frecep)),
        ),
    )
    mark(ffn_back_edge)
    grad_ffn_normed = (
        grad_fkey_in * channel_lookup_share
        + grad_frecep_in * channel_gate_share
        + jnp.concatenate([grad_ffn_prev[:, 1:, :], ffn_back_edge[:, None, :]], axis=1)
    )
    grad_ffn_ln_gain = jnp.sum(grad_ffn_normed * ffn_unit, axis=(0, 1))
    grad_ffn_ln_bias = jnp.sum(grad_ffn_normed, axis=(0, 1))
    grad_after = grad_top + norm_back(grad_ffn_normed, ffn_unit, ffn_inv, channel_norm_scale)

    grad_att_out = mark(grad_after.astype(BF16), fkey_far[1])
    grad_gated = project_back(gate(grad_att_out), emission_matrix)
    grad_num, grad_den, grad_recep, tail = scan_call(
        backward_tails_kernel,
        [grad_gated, key_proj, value_proj, recep_proj, num_state, den_state, back_windows, rate_row, bonus_row],
        [(full, F32), (full, F32), (full, BF16), tails],
    )
    fr = Partial("FR", (flat(ffn_recep_mixed), frecep_far), (flat(grad_frecep), grad_frecep_far))
    mark(tail, fkey_far[0], fvalue_far[0])
    gated_tail = gate(tail)
    state, (recep_far, out_far), fr.halves = at_once(
        ready,
        lambda: (
            enter(gated_tail, backward=True),
            send_half_of((flat(grad_recep), flat(grad_att_out))),
            fr.products(),
        ),
    )
    mark(state)

    step = functools.partial(phase, line, ready)
    ou = Partial("OU", (gated, gated_far), (flat(grad_att_out), out_far))
    ar = Partial("AR", recep_side, (flat(grad_recep), recep_far))
    fkey_cross = exchange(gate(fkey_far[1]), CORE)
    ou.multiply(line)
    fvalue_cross = exchange(gate(fvalue_far[1]), CORE)
    ar.multiply(line)
    mark(fkey_cross, fvalue_cross, ar.halves[0])

    halves = step(
        [fr, ou, ar],
        lambda: hidden_products(
            flat(ffn_key_mixed),
            (*fkey_far, fkey_cross),
            flat(grad_fvalue),
            (*fvalue_far, fvalue_cross),
            channel_lookup_matrix,
            channel_payload_matrix,
        ),
    )
    big_value, big_key = [Blocks(name, None, pair) for name, pair in zip(("BV", "BK"), halves)]
    big_key.forward(line)
    big_value.forward(line)
    grad_key, grad_value, sums = step(
        [ar, ou],
        lambda: scan_call(
            backward_states_kernel,
            [grad_num, grad_den, key_proj, value_proj, num_state, den_state, back_windows, rate_row, bonus_row, state],
            [(full, BF16), (full, BF16), ((16, features), F32)],
        ),
    )
    (key_far, value_far), grad_key_in, grad_value_in, grad_recep_in = step(
        [],
        lambda: (
            send_half_of((flat(grad_key), flat(grad_value))),
            project_back(grad_key, lookup_matrix),
            project_back(grad_value, payload_matrix),
            project_back(grad_recep, gate_matrix),
        ),
    )
    reward_slope = jnp.sum(sums[:8], axis=0)
    grad_time_decay = -decay_rate * jnp.exp(-decay_rate) * jnp.sum(sums[8:], axis=0)
    ak = Partial("AK", key_side, (flat(grad_key), key_far))
    av = Partial("AV", value_side, (flat(grad_value), value_far))
    ak.multiply(line)

    def mixes():
        normed = att_unit_again() * mixer_norm_scale + mixer_norm_offset
        att_delta = normed - with_previous(normed, att_edge, keep)
        att_back = (
            grad_key_in * (1.0 - temporal_lookup_share)
            + grad_value_in * (1.0 - temporal_payload_share)
            + grad_recep_in * (1.0 - temporal_gate_share)
        ) * keep[:, :, None]
        return (
            shifted(att_back[:, 0, :], "seq", -1),
            att_back,
            av.products(),
            jnp.sum(grad_key_in * att_delta, axis=(0, 1)),
            jnp.sum(grad_value_in * att_delta, axis=(0, 1)),
            jnp.sum(grad_recep_in * att_delta, axis=(0, 1)),
            grad_key_in * temporal_lookup_share
            + grad_value_in * temporal_payload_share
            + grad_recep_in * temporal_gate_share,
        )

    big_key.forward(line)
    big_value.forward(line)
    att_back_edge, grad_att_prev, av.halves, grad_mix_key, grad_mix_value, grad_mix_recep, direct = step(
        [ak], mixes
    )
    big_key.forward(line)
    big_value.forward(line)
    two = Stacked(line, [fr, ak])

    def norm_att():
        att_unit = att_unit_again()
        grad_att_normed = direct + jnp.concatenate(
            [grad_att_prev[:, 1:, :], att_back_edge[:, None, :]], axis=1
        )
        grad_tokens = (
            grad_after + norm_back(grad_att_normed, att_unit, att_inv, mixer_norm_scale)
        ).astype(BF16)
        return (
            grad_tokens,
            jnp.sum(grad_att_normed * att_unit, axis=(0, 1)),
            jnp.sum(grad_att_normed, axis=(0, 1)),
        )

    grad_tokens, grad_att_ln_gain, grad_att_ln_bias = step([two, av, ar], norm_att)
    vectors = Vectors(
        jnp.stack(
            [
                grad_att_ln_gain,
                grad_att_ln_bias,
                grad_mix_key,
                grad_mix_value,
                grad_mix_recep,
                grad_time_decay,
                reward_slope,
                grad_ffn_ln_gain,
                grad_ffn_ln_bias,
                grad_ffn_mix_key,
                grad_ffn_mix_recep,
            ]
        )
    )
    step([av, ou, vectors])
    big_key.forward(line)
    big_value.forward(line)
    three, pair = Stacked(line, [two, av]), Stacked(line, [ou, ar])
    step([three, pair, vectors])
    pairs = big_value.arrived(line), big_key.arrived(line)

    (ou_sum, ar_sum), quarters = step(
        [three, vectors],
        lambda: at_once(ready, lambda: (gather(total_of(pair.terms)), join_hidden(*pairs))),
    )
    (fr_sum, ak_sum, av_sum), (got, (value_sum, key_sum)) = step(
        [],
        lambda: gather(
            total_of(three.terms),
            lambda: at_once(ready, lambda: (vectors.hop(), whole_hidden(*quarters))),
        ),
    )
    small = lax.optimization_barrier(got)
    return (
        layer_out,
        grad_tokens,
        *[small[i] for i in range(7)],
        ak_sum,
        av_sum,
        ar_sum,
        ou_sum,
        *[small[i] for i in range(7, 11)],
        key_sum,
        value_sum,
        fr_sum,
    )


def solution(mesh):
    tokens = P("batch", "seq", None)
    vector, matrix = P("seq"), P("seq", None)
    return jax.shard_map(
        shards,
        mesh=mesh,
        in_specs=(tokens, P("batch", None), *([P()] * 18), tokens),
        out_specs=(tokens, tokens, *([vector] * 7), *([matrix] * 4), *([vector] * 4), *([matrix] * 3)),
        check_vma=False,
    )
```

```python
import functools
import math

import jax
import jax.numpy as jnp
from jax import lax
from jax.experimental import pallas as pl
from jax.experimental.pallas import tpu as pltpu
from jax.sharding import PartitionSpec as P

F32, BF16 = jnp.float32, jnp.bfloat16


def shifted(value, axis, distance):
    devices = range(lax.axis_size(axis))
    route = [(i - distance, i) for i in devices if i - distance in devices]
    return lax.ppermute(value, axis, route)


def bit_value(bit):
    axis, place = bit
    return (lax.axis_index(axis) >> place) & 1


def exchange(value, bit):
    axis, place = bit
    return lax.ppermute(value, axis, [(i, i ^ (1 << place)) for i in range(lax.axis_size(axis))])


def pick(value, index, dim):
    return lax.dynamic_index_in_dim(value, index, dim, keepdims=False)


def total_of(terms):
    return functools.reduce(lambda a, b: a + b, terms)


def axis_bits(axis):
    return [(axis, k) for k in range(int(math.log2(lax.axis_size(axis))))]


def at_once(ready, step, *values):
    blank = lambda *v: jax.tree.map(
        lambda x: jnp.zeros(x.shape, x.dtype), jax.eval_shape(step, *v)
    )
    return lax.cond(ready, step, blank, *values)


class Line:
    def __init__(self):
        self.token = None

    def gate(self, value):
        if self.token is None:
            return value
        return lax.optimization_barrier((value, self.token))[0]

    def mark(self, value, *others):
        self.token = (value, *others)
        return value


CORE = ("batch", 0)


def send_half(value):
    half = value.shape[1] // 2
    theirs = lax.dynamic_slice_in_dim(value, (1 - bit_value(CORE)) * half, half, 1)
    return exchange(theirs.astype(F32), CORE)


def send_half_of(values):
    half = values[0].shape[1] // 2
    at = (1 - bit_value(CORE)) * half
    theirs = [lax.dynamic_slice_in_dim(v, at, half, 1).astype(F32) for v in values]
    got = exchange(jnp.concatenate(theirs, axis=0), CORE)
    return jnp.split(got, len(values), axis=0)


def send_whole(value):
    return exchange(value.astype(F32), CORE)


CROSS = ("batch", 1)


def send_across(value):
    value = value.astype(F32)
    return exchange(value, CORE), exchange(value, CROSS)


def hidden_kernel(
    at_ref, *refs, unit,
):
    lefts, grads, (up_a, up_b, down_a, down_b, *outs, left_all, grad_all) = refs[:4], refs[4:8], refs[8:]
    value_send, value_keep, key_send, key_keep = outs
    z = pl.program_id(0) & 1
    tokens = lefts[0].shape[0]

    @pl.when(pl.program_id(0) == 0)
    def _():
        for k in range(4):
            at = pl.ds(k * tokens, tokens)
            left_all[at, :] = lefts[k][...].astype(BF16)
            grad_all[at, :] = grads[k][...].astype(BF16)

    up = jnp.concatenate([up_a[...], up_b[...]], axis=1)
    down = jnp.concatenate([down_a[...], down_b[...]], axis=0)
    first = lambda a, b: lax.dot_general(a, b, (((0,), (0,)), ((), ())), preferred_element_type=F32)

    def products(k):
        at = pl.ds(k * 2 * tokens, 2 * tokens)
        left, grad = left_all[at, :], grad_all[at, :]
        above = jnp.maximum(jnp.dot(left, up, preferred_element_type=F32), 0.0)
        back = lax.dot_general(grad, down, (((1,), (1,)), ((), ())), preferred_element_type=F32)
        return first((above * above).astype(BF16), grad), first((back * (2.0 * above)).astype(BF16), left)

    def put(value, key, add):
        def store(ref, index, part):
            ref[index] = ref[index] + part if add else part

        def values(ref):
            for half in range(2):
                store(ref, (0, half), value[half * unit : (half + 1) * unit])

        def keys(even, odd):
            rows = key.shape[1] // 8
            for s in range(8):
                store((even, odd)[s & 1], s >> 1, key[:, s * rows : (s + 1) * rows])

        pl.when(z == at_ref[1])(lambda: values(value_keep))
        pl.when(z != at_ref[1])(lambda: values(value_send))
        pl.when(at_ref[2] == 0)(lambda: keys(key_keep, key_send))
        pl.when(at_ref[2] != 0)(lambda: keys(key_send, key_keep))

    put(*products(0), False)
    put(*products(1), True)


def hidden_products(left, far_lefts, grad, far_grads, up, down):
    seq, tokens, features = lax.axis_size("seq"), left.shape[0], left.shape[1]
    unit = up.shape[1] // seq // 4
    quarter = 2 * bit_value(CORE) + bit_value(CROSS)
    if unit % 128 or features // seq % 128 or seq != 8:
        up = pick(up.reshape(features, seq, 4, unit), quarter, 2).reshape(features, -1)
        down = pick(down.reshape(seq, 4, unit, features), quarter, 1).reshape(-1, features)
        lefts = jnp.concatenate([left, *[f.astype(BF16) for f in far_lefts]])
        grads = jnp.concatenate([grad, *[f.astype(BF16) for f in far_grads]])
        above = jnp.maximum(jnp.dot(lefts, up, preferred_element_type=F32), 0.0)
        back = lax.dot_general(grads, down, (((1,), (1,)), ((), ())), preferred_element_type=F32)
        first = lambda a, b: lax.dot_general(a, b, (((0,), (0,)), ((), ())), preferred_element_type=F32)
        value = first((above * above).astype(BF16), grads).reshape(seq, unit, features)
        key = first((back * (2.0 * above)).astype(BF16), lefts)
        key = jnp.swapaxes(key.reshape(-1, seq, features // seq), 0, 1)
        return Blocks("BV", value).first(), Blocks("BK", key).first()
    whole = lambda: pl.BlockSpec((tokens, features), lambda i, at: (0, 0), pipeline_mode=pl.Buffered(1))
    ups = [pl.BlockSpec((features, unit), lambda i, at, h=h: (0, 4 * (2 * i + h) + at[0])) for h in (0, 1)]
    downs = [pl.BlockSpec((unit, features), lambda i, at, h=h: (4 * (2 * i + h) + at[0], 0)) for h in (0, 1)]
    at = jnp.stack([quarter, *[bit_value(order_of(name)[0][0]) for name in ("BV", "BK")]])
    halves = [(2, 2, unit, features)] * 2 + [(4, seq * unit, features // seq)] * 2
    value_spec = pl.BlockSpec((1, 2, unit, features), lambda i, at: (i >> 1, 0, 0, 0))
    key_spec = pl.BlockSpec((4, 2 * unit, features // seq), lambda i, at: (0, i, 0))
    made = pl.pallas_call(
        functools.partial(hidden_kernel, unit=unit),
        grid_spec=pltpu.PrefetchScalarGridSpec(
            num_scalar_prefetch=1,
            grid=(seq // 2,),
            in_specs=[whole() for _ in range(8)] + ups + downs,
            out_specs=[value_spec, value_spec, key_spec, key_spec],
            scratch_shapes=[pltpu.VMEM((4 * tokens, features), BF16)] * 2,
        ),
        out_shape=[jax.ShapeDtypeStruct(shape, F32) for shape in halves],
        compiler_params=pltpu.CompilerParams(vmem_limit_bytes=56 * 1024 * 1024),
        cost_estimate=pl.CostEstimate(
            flops=32 * tokens * features * seq * unit,
            bytes_accessed=40 * tokens * features,
            transcendentals=0,
        ),
    )(at.astype(jnp.int32), left, *far_lefts, grad, *far_grads, up, up, down, down)
    made = [x.reshape(2, 2, *x.shape[-2:]) for x in made]
    return made[:2], made[2:]


ORDERS = dict(BV="zywx", BK="yzwx", FR="xyzw", OU="zxyw", AR="yxzw", AK="xyzw", AV="xyzw")


def order_of(name):
    seq = axis_bits("seq")
    places = dict(x=axis_bits("batch")[1:], y=seq[:1], z=seq[1:2], w=seq[2:])
    return [places[letter] for letter in ORDERS[name]]


def halve(terms, dims, bit):
    if bit not in dims:
        total = total_of(terms)
        return total, [total]
    dim, mine = dims.index(bit), bit_value(bit)
    send = total_of([pick(t, 1 - mine, dim) for t in terms])
    return send, [pick(t, mine, dim) for t in terms]


class Blocks:
    halves = None

    def __init__(self, name, value, halves=None):
        self.hops, self.dims = order_of(name), axis_bits("seq")[::-1]
        self.halves, self.terms = halves, None
        if halves is None:
            self.terms = [value.reshape(*((2,) * len(self.dims)), *value.shape[1:])]

    def first(self):
        send, kept = self.split(self.terms)
        return send, kept[0]

    def split(self, terms):
        if self.halves:
            return self.halves[0], [self.halves[1]]
        return halve(terms, self.dims, self.hops[0][0])

    def go(self, sends):
        bits, dims = self.hops[0], list(self.dims)
        got = exchange(sends, bits[0])
        if len(bits) == 1:
            return got
        terms = self.split(self.terms)[1] + [got]
        dims = [d for d in dims if d != bits[0]]
        for bit in bits[1:]:
            send, kept = halve(terms, dims, bit)
            terms = kept + [exchange(send, bit)]
            dims = [d for d in dims if d != bit]
        return total_of(terms)

    def hop(self):
        return self.go(self.split(self.terms)[0])

    def landed(self, got):
        bits = self.hops[0]
        self.terms = self.split(self.terms)[1] + [got] if len(bits) == 1 else [got]
        self.halves = None
        self.dims = [d for d in self.dims if d not in bits]
        self.hops.pop(0)

    def arrived(self, line):
        return self.terms[:-1] + [line.gate(self.terms[-1])]

    def forward(self, line):
        if self.halves:
            send = line.gate(self.halves[0])
        else:
            send = self.split(self.arrived(line))[0]
        self.landed(self.go(line.mark(send)))


def phase(line, ready, jobs, beside=None):
    def step():
        return [job.hop() for job in jobs], beside() if beside else ()

    got, more = at_once(line.gate(ready), step)
    for job, value in zip(jobs, got):
        job.landed(value)
    line.mark(*jax.tree.leaves((got, more)))
    return more


def product_kernel(
    at_ref, left_ref, far_left_ref, right_ref, far_right_ref, send_ref, keep_ref,
    *, rows, cols, group, place,
):
    first = at_ref[0]

    def lefts(blocks):
        cut = lambda ref, js: jnp.concatenate(
            [ref[:, pl.ds(pl.multiple_of(j * rows, 128), rows)] for j in js], axis=1
        )
        return jnp.concatenate([cut(left_ref, blocks), cut(far_left_ref, blocks).astype(BF16)], axis=0)

    def rights(x):
        at = pl.ds(pl.multiple_of(x * cols, 128), cols)
        return jnp.concatenate([right_ref[:, at], far_right_ref[:, at].astype(BF16)], axis=0)

    dot = lambda a, b: lax.dot_general(
        a, b, (((0,), (0,)), ((), ())), preferred_element_type=F32
    )
    for out, value in ((send_ref, 1 - first), (keep_ref, first)):
        if place is None:
            out[0] = dot(lefts(list(range(group))), rights(value))
        else:
            low = 1 << place
            blocks = [(q // low) * 2 * low + q % low + value * low for q in range(group // 2)]
            left = lefts(blocks)
            for x in range(2):
                out[x, 0] = dot(left, rights(x))


class Partial(Blocks):
    def __init__(self, name, left, right):
        self.left, self.right = left, right
        self.hops, self.terms = order_of(name), None
        self.dims = axis_bits("batch")[1:] + axis_bits("seq")[::-1]
        self.blocks = lax.axis_size("seq")
        self.rows = left[0].shape[1] // self.blocks
        self.cols = right[0].shape[1] // 4

    def plain(self):
        half = self.right[0].shape[1] // 2
        own = lax.dynamic_slice_in_dim(self.right[0], bit_value(CORE) * half, half, 1)
        dot = lambda a, b: lax.dot_general(
            a.astype(BF16), b.astype(BF16), (((0,), (0,)), ((), ())), preferred_element_type=F32
        )
        whole = dot(self.left[0], own) + dot(self.left[1], self.right[1])
        lead = (2,) * len(axis_bits("seq"))
        whole = jnp.moveaxis(whole.reshape(*lead, self.rows, 2, self.cols), -2, 0)
        send, kept = halve([whole], self.dims, self.hops[0][0])
        return send, kept[0]

    def kernel(self):
        rows, cols, tokens = self.rows, self.cols, self.left[0].shape[0]
        first = self.hops[0][0]
        place = first[1] if first[0] == "seq" else None
        group = 4
        steps = self.blocks // group
        if place is None:
            block, shape = (1, group * rows, cols), (steps, group * rows, cols)
            out_index = lambda i, at: (i, 0, 0)
        else:
            block, shape = (2, 1, group // 2 * rows, cols), (2, steps, group // 2 * rows, cols)
            out_index = lambda i, at: (0, i, 0, 0)
        out = jax.ShapeDtypeStruct(shape, F32)
        at = jnp.stack([bit_value(first), bit_value(CORE)]).astype(jnp.int32)
        send, kept = pl.pallas_call(
            functools.partial(
                product_kernel, rows=rows, cols=cols, group=group, place=place
            ),
            grid_spec=pltpu.PrefetchScalarGridSpec(
                num_scalar_prefetch=1,
                grid=(steps,),
                in_specs=[
                    pl.BlockSpec((tokens, group * rows), lambda i, at: (0, i)),
                    pl.BlockSpec((tokens, group * rows), lambda i, at: (0, i)),
                    pl.BlockSpec((tokens, 2 * cols), lambda i, at: (0, at[1])),
                    pl.BlockSpec((tokens, 2 * cols), lambda i, at: (0, 0)),
                ],
                out_specs=[pl.BlockSpec(block, out_index)] * 2,
            ),
            out_shape=[out, out],
            compiler_params=scan_params(),
            cost_estimate=pl.CostEstimate(
                flops=8 * tokens * self.blocks * rows * cols,
                bytes_accessed=8 * self.blocks * rows * cols,
                transcendentals=0,
            ),
        )(at, self.left[0], self.left[1], self.right[0], self.right[1])
        lead = (2,) * (len(self.dims) - 1)
        return send.reshape(*lead, rows, cols), kept.reshape(*lead, rows, cols)

    def products(self):
        aligned = self.rows % 128 == 0 and self.blocks % 4 == 0 and len(axis_bits("batch")) == 2
        return self.kernel() if aligned else self.plain()

    def multiply(self, line):
        self.left = (line.gate(self.left[0]), self.left[1])
        self.halves = self.products()
        line.mark(self.halves[0])


class Stacked(Blocks):
    def __init__(self, line, jobs):
        self.hops, self.dims = list(jobs[0].hops), jobs[0].dims
        sums = [total_of(j.arrived(line)) for j in jobs]
        sums = [v if isinstance(j, Stacked) else v[..., None, :, :] for j, v in zip(jobs, sums)]
        self.terms = [jnp.concatenate(sums, axis=-3)]


class Vectors(Blocks):
    def __init__(self, vectors):
        vectors = jnp.pad(vectors, ((0, -vectors.shape[0] % 8), (0, 0)))
        count, seq = vectors.shape[0], lax.axis_size("seq")
        self.dims = axis_bits("seq")[::-1]
        bits = axis_bits("seq")
        self.hops = [axis_bits("batch")] + [[b] for b in bits[:2]] + [bits[2:]]
        value = jnp.swapaxes(vectors.reshape(count, seq, -1), 0, 1)
        self.terms = [value.reshape(*((2,) * len(self.dims)), count, -1)]

def in_order(own, other, bit, axis):
    first = bit_value(bit) == 0
    return jnp.concatenate(
        [jnp.where(first, own, other), jnp.where(first, other, own)], axis=axis
    )


def gather(own, beside=None):
    other, more = exchange(own, CROSS), None
    if beside:
        other, more = lax.optimization_barrier((other, beside()))
    own = in_order(own, other, CROSS, 2)
    own = in_order(own, exchange(own, CORE), CORE, 2)
    joined = [own[i] for i in range(own.shape[0])]
    return (joined, more) if beside else joined


def join_hidden(values, keys):
    seq = lax.axis_size("seq")
    value = in_order(*values, CROSS, 0)
    key = in_order(*[t.reshape(seq, 1, -1, t.shape[-1]) for t in keys], CROSS, 1)
    return (value, exchange(value, CORE)), (key, exchange(key, CORE))


def whole_hidden(values, keys):
    key = in_order(*keys, CORE, 1)
    return in_order(*values, CORE, 0), jnp.transpose(key.reshape(-1, key.shape[-1]))


def entering(tails, begins, decay_rate, group_len, backward):
    count, mine = lax.axis_size("seq"), lax.axis_index("seq")
    sign, radix = (-1, 4) if backward else (1, 2)

    def gain(lo, hi):
        a, b = (mine + lo, mine + hi) if backward else (mine - hi + 1, mine - lo + 1)
        hit = jnp.any((begins >= a * group_len) & (begins < b * group_len), axis=1, keepdims=True)
        return jnp.where(hit, 0.0, 1.0) * jnp.exp(-float((hi - lo) * group_len) * decay_rate)[None, :]

    reach, window, before = 1, tails, None
    while reach < count:
        got = [
            (j, shifted(window, "seq", sign * j * reach))
            for j in range(1, radix)
            if j * reach < count
        ]
        if before is None:
            before = total_of([v if j == 1 else gain(1, j) * v for j, v in got])
            seen = 1 + len(got)
            window = tails + gain(0, 1) * before if seen < count else None
        else:
            before_more = total_of([gain(1, j * reach) * v for j, v in got])
            seen = reach * (1 + len(got))
            if seen < count:
                window = window + total_of([gain(0, j * reach) * v for j, v in got])
            before = before + before_more
        reach *= radix
    return before


def scan_params():
    return pltpu.CompilerParams(vmem_limit_bytes=48 * 1024 * 1024)


def lane_tiles(width):
    return [slice(i, i + 128) for i in range(0, width, 128)]


WINDOW = {name: k for k, name in enumerate(("keep", "one", "two", "four", "group", "eight", "end"))}


def windows_kernel(sizes_ref, block_ref, ahead_ref, back_ref):
    rows, length, width = ahead_ref.shape[1:]
    t = lax.broadcasted_iota(jnp.int32, (length, width), 0)
    inner = t & 7

    def put(ref, name, equal, inside=None):
        kept = equal if inside is None else equal & inside
        ref[WINDOW[name], row] = jnp.where(kept, 1.0, 0.0)

    for row in range(rows):
        begins, at = [], -block_ref[0]
        for j in range(sizes_ref.shape[1]):
            begins.append(at)
            at = at + sizes_ref[row, j]

        def begun(by):
            return total_of([jnp.where(by >= b, 1, 0) for b in begins])

        here, ahead_of = begun(t), begun(t - 1)
        keep = here == ahead_of
        put(ahead_ref, "keep", keep)
        put(back_ref, "keep", keep)
        for name, n in (("one", 1), ("two", 2), ("four", 4)):
            put(ahead_ref, name, here == begun(t - n), inner >= n)
            put(back_ref, name, begun(t + (n - 1)) == ahead_of, inner <= 7 - n)
        put(ahead_ref, "group", here == begun(t - inner - 1))
        put(back_ref, "group", begun(t - inner + 7) == ahead_of)
        put(ahead_ref, "eight", here == begun(t - 8), t >= 8)
        put(back_ref, "eight", begun(t + 7) == ahead_of, t < length - 8)
        put(ahead_ref, "end", here == begun(jnp.full_like(t, length - 1)))
        put(back_ref, "end", ahead_of == begun(jnp.full_like(t, -1)))


def keep_windows(sizes, length, width):
    block = (lax.axis_index("seq") * length)[None].astype(jnp.int32)
    out = jax.ShapeDtypeStruct((len(WINDOW), sizes.shape[0], length, width), F32)
    return pl.pallas_call(
        windows_kernel,
        out_shape=[out, out],
        in_specs=[pl.BlockSpec(memory_space=pltpu.SMEM)] * 2,
        compiler_params=scan_params(),
        cost_estimate=pl.CostEstimate(flops=100 * out.size, bytes_accessed=8 * out.size, transcendentals=0),
    )(sizes, block)


def powers(rate_ref, tiles):
    return lambda n: [jnp.exp(-n * rate_ref[0:1, t]) for t in tiles]


def inner_place(shape=(8, 128)):
    return lax.broadcasted_iota(jnp.int32, shape, 0)


def spread(row):
    return jnp.broadcast_to(row, (8, 128))


def in_group(value, factors, back):
    for n, factor in zip((1, 2, 4), factors):
        value = value + factor * pltpu.roll(value, 8 - n if back else n, 0)
    return value


def halves_of(ref, row, at, tile):
    value = ref[row, at, tile]
    return value[:8], value[8:]


def windows_at(win_ref, row, at):
    names = ("keep", "one", "two", "four", "group")
    return [dict(zip(names, v)) for v in zip(*[halves_of(win_ref.at[WINDOW[n]], row, at, slice(None)) for n in names])]


def pair_at(p):
    return pl.ds(pl.multiple_of(p * 16, 16), 16)


def forward_tails_kernel(k_ref, v_ref, win_ref, rate_ref, tail_ref):
    rows, length, width = k_ref.shape
    tiles = lane_tiles(width)
    chains = [(r, i, t) for r in range(rows) for i, t in enumerate(tiles)]
    eight = powers(rate_ref, tiles)(8.0)

    def step(p, carry):
        at, out = pair_at(p), []
        windows = [halves_of(win_ref.at[WINDOW["eight"]], r, at, slice(None)) for r in range(rows)]
        for (r, i, t), (num, den) in zip(chains, carry):
            for h, (key, value) in enumerate(zip(halves_of(k_ref, r, at, t), halves_of(v_ref, r, at, t))):
                factor, e = windows[r][h] * eight[i], jnp.exp(key)
                num, den = factor * num + e * value, factor * den + e
            out.append((num, den))
        return tuple(out)

    zero = jnp.zeros((8, 128), F32)
    done = lax.fori_loop(0, length // 16, step, tuple((zero, zero) for _ in chains), unroll=2)
    left = powers(rate_ref, tiles)((7 - inner_place()).astype(F32))
    for (r, i, t), pair in zip(chains, done):
        factor = win_ref[WINDOW["end"], r, pl.ds(length - 8, 8), :] * left[i]
        for q in range(2):
            tail_ref[q, r : r + 1, t] = jnp.sum(factor * pair[q], axis=0, keepdims=True)


def forward_states_kernel(
    k_ref, v_ref, recep_ref, win_ref, rate_ref, bonus_ref, enter_ref, num_ref, den_ref, gated_ref
):
    rows, length, width = k_ref.shape
    tiles = lane_tiles(width)
    chains = [(r, i, t) for r in range(rows) for i, t in enumerate(tiles)]
    power = powers(rate_ref, tiles)
    ones, twos, fours = power(1.0), power(2.0), power(4.0)
    groups = power((1 + inner_place()).astype(F32))
    head = inner_place() == 0

    def step(p, carry):
        at, out = pair_at(p), []
        windows = [windows_at(win_ref, r, at) for r in range(rows)]
        for (r, i, t), states in zip(chains, carry):
            keys, values = halves_of(k_ref, r, at, t), halves_of(v_ref, r, at, t)
            receps, bonus, results = halves_of(recep_ref, r, at, t), bonus_ref[0:1, t], []
            for h in range(2):
                w = windows[r][h]
                factors = (w["one"] * ones[i], w["two"] * twos[i], w["four"] * fours[i])
                group = w["group"] * groups[i]
                e, held, here = jnp.exp(keys[h]), [], []
                for state, item in zip(states, (e * values[h], e)):
                    full = in_group(item, factors, False) + group * state
                    here.append(w["keep"] * jnp.where(head, state, pltpu.roll(full, 1, 0)))
                    held.append(spread(full[7:8]))
                states = held
                first = jnp.exp(bonus + keys[h])
                wkv = (here[0] + first * values[h]) / (here[1] + first)
                results.append((*here, jax.nn.sigmoid(receps[h]) * wkv))
            for ref, two in zip((num_ref, den_ref, gated_ref), zip(*results)):
                ref[r, at, t] = jnp.concatenate(two, axis=0).astype(ref.dtype)
            out.append(tuple(states))
        return tuple(out)

    start = tuple(tuple(spread(enter_ref[q, r : r + 1, t]) for q in range(2)) for r, _, t in chains)
    lax.fori_loop(0, length // 16, step, start)


def backward_tails_kernel(
    grad_ref, k_ref, v_ref, recep_ref, num_ref, den_ref, win_ref, rate_ref, bonus_ref,
    gnum_ref, gden_ref, grecep_ref, tail_ref,
):
    rows, length, width = k_ref.shape
    tiles = lane_tiles(width)
    chains = [(r, i, t) for r in range(rows) for i, t in enumerate(tiles)]
    eight = powers(rate_ref, tiles)(8.0)
    pairs = length // 16

    def step(p, carry):
        at, out = pair_at(pairs - 1 - p), []
        keeps = [halves_of(win_ref.at[WINDOW["keep"]], r, at, slice(None)) for r in range(rows)]
        windows = [halves_of(win_ref.at[WINDOW["eight"]], r, at, slice(None)) for r in range(rows)]
        for (r, i, t), (late_num, late_den) in zip(chains, carry):
            key, value = k_ref[r, at, t], v_ref[r, at, t]
            first = jnp.exp(bonus_ref[0:1, t] + key)
            below = den_ref[r, at, t] + first
            wkv = (num_ref[r, at, t] + first * value) / below
            gate, grad = jax.nn.sigmoid(recep_ref[r, at, t]), grad_ref[r, at, t]
            grecep_ref[r, at, t] = (grad * wkv * (gate * (1.0 - gate))).astype(BF16)
            up = grad * gate / below
            low = -up * wkv
            gnum_ref[r, at, t] = up
            gden_ref[r, at, t] = low
            for h in (1, 0):
                rows_of = slice(8 * h, 8 * h + 8)
                factor, keep = windows[r][h] * eight[i], keeps[r][h]
                late_num = factor * late_num + keep * up[rows_of]
                late_den = factor * late_den + keep * low[rows_of]
            out.append((late_num, late_den))
        return tuple(out)

    zero = jnp.zeros((8, 128), F32)
    done = lax.fori_loop(0, pairs, step, tuple((zero, zero) for _ in chains))
    left = powers(rate_ref, tiles)(inner_place().astype(F32))
    for (r, i, t), pair in zip(chains, done):
        factor = win_ref[WINDOW["end"], r, pl.ds(0, 8), :] * left[i]
        for q in range(2):
            tail_ref[q, r : r + 1, t] = jnp.sum(factor * pair[q], axis=0, keepdims=True)


def backward_states_kernel(
    gnum_ref, gden_ref, k_ref, v_ref, num_ref, den_ref, win_ref, rate_ref, bonus_ref, enter_ref,
    gkey_ref, gvalue_ref, sums_ref,
):
    rows, length, width = k_ref.shape
    tiles = lane_tiles(width)
    chains = [(r, i, t) for r in range(rows) for i, t in enumerate(tiles)]
    power = powers(rate_ref, tiles)
    ones, twos, fours = power(1.0), power(2.0), power(4.0)
    groups = power((8 - inner_place()).astype(F32))
    tail = inner_place() == 7
    pairs = length // 16

    def step(p, carry):
        at, out = pair_at(pairs - 1 - p), []
        windows = [windows_at(win_ref, r, at) for r in range(rows)]
        for (r, i, t), (num_state, den_state, slope, fade) in zip(chains, carry):
            states, parts = (num_state, den_state), []
            keys, values = halves_of(k_ref, r, at, t), halves_of(v_ref, r, at, t)
            ups, lows = halves_of(gnum_ref, r, at, t), halves_of(gden_ref, r, at, t)
            nums, dens = halves_of(num_ref, r, at, t), halves_of(den_ref, r, at, t)
            for h in (1, 0):
                w = windows[r][h]
                factors = (w["one"] * ones[i], w["two"] * twos[i], w["four"] * fours[i])
                group, held, here = w["group"] * groups[i], [], []
                for state, item in zip(states, (ups[h], lows[h])):
                    full = in_group(w["keep"] * item, factors, True) + group * state
                    here.append(jnp.where(tail, state, pltpu.roll(full, 7, 0)))
                    held.append(spread(full[0:1]))
                states = held
                e, first = jnp.exp(keys[h]), jnp.exp(bonus_ref[0:1, t] + keys[h])
                present = first * (ups[h] * values[h] + lows[h])
                slope = slope + present
                fade = fade + nums[h] * here[0] + dens[h] * here[1]
                parts.append(
                    (
                        present + e * (here[0] * values[h] + here[1]),
                        ups[h] * first + here[0] * e,
                    )
                )
            for ref, two in zip((gkey_ref, gvalue_ref), zip(*parts[::-1])):
                ref[r, at, t] = jnp.concatenate(two, axis=0).astype(BF16)
            out.append((*states, slope, fade))
        return tuple(out)

    zero = jnp.zeros((8, 128), F32)
    start = tuple(
        (*[spread(enter_ref[q, r : r + 1, t]) for q in range(2)], zero, zero) for r, _, t in chains
    )
    done = lax.fori_loop(0, pairs, step, start)
    for i, t in enumerate(tiles):
        for q in range(2):
            sums_ref[8 * q : 8 * q + 8, t] = total_of(
                [c[2 + q] for (_, j, _), c in zip(chains, done) if j == i]
            )


def scan_call(kernel, inputs, outputs, width=512):
    features = inputs[0].shape[-1]

    def spec(shape):
        lead = len(shape) - 1
        if shape[-1] == 128 and features != 128:
            return pl.BlockSpec(shape, lambda i: (0,) * (lead + 1))
        return pl.BlockSpec((*shape[:-1], width), lambda i: (0,) * lead + (i,))

    out_shape = [jax.ShapeDtypeStruct(s, d) for s, d in outputs]
    moved = sum(x.size * x.dtype.itemsize for x in [*inputs, *out_shape])
    return pl.pallas_call(
        kernel,
        out_shape=out_shape,
        grid=(features // width,),
        in_specs=[spec(x.shape) for x in inputs],
        out_specs=[spec(s) for s, _ in outputs],
        compiler_params=scan_params(),
        cost_estimate=pl.CostEstimate(
            flops=20 * inputs[0].size, bytes_accessed=moved, transcendentals=inputs[0].size
        ),
    )(*inputs)


def channel_kernel(
    left_ref, recep_ref, up_ref, down_ref, gate_ref, after_ref, top_ref,
    out_ref, fvalue_ref, frecep_ref, fkey_ref, recep_in_ref, above_ref, total_ref,
):
    across = (((1,), (1,)), ((), ()))
    block = up_ref.shape[1]
    step, blocks = pl.program_id(0), pl.num_programs(0) // 2

    def at(i):
        return pl.ds(pl.multiple_of(i * block, block), block)

    def add(ref, first, part):
        @pl.when(step == first)
        def _():
            ref[...] = part

        @pl.when(step > first)
        def _():
            ref[...] += part

    @pl.when(step < blocks)
    def _():
        above = jnp.maximum(jnp.dot(left_ref[...], up_ref[...], preferred_element_type=F32), 0.0)
        above_ref[:, at(step)] = above
        add(total_ref, 0, jnp.dot((above * above).astype(BF16), down_ref[...], preferred_element_type=F32))

    @pl.when(step == blocks - 1)
    def _():
        value = total_ref[...]
        gate = jax.nn.sigmoid(
            jnp.dot(recep_ref[...], gate_ref[...], preferred_element_type=F32)
        )
        top = top_ref[...].astype(F32)
        out_ref[...] = (after_ref[...] + gate * value).astype(BF16)
        fvalue_ref[...] = (top * gate).astype(BF16)
        frecep = (top * value * (gate * (1.0 - gate))).astype(BF16)
        frecep_ref[...] = frecep
        recep_in_ref[...] = lax.dot_general(
            frecep, gate_ref[...], across, preferred_element_type=F32
        )

    @pl.when(step >= blocks)
    def _():
        back = lax.dot_general(fvalue_ref[...], down_ref[...], across, preferred_element_type=F32)
        hidden = (back * (2.0 * above_ref[:, at(step - blocks)])).astype(BF16)
        add(fkey_ref, blocks, lax.dot_general(hidden, up_ref[...], across, preferred_element_type=F32))


def channel_mix(left, recep, up, down, gate, after, top):
    (tokens, features), hidden = left.shape, up.shape[1]
    block = min(1024, hidden)
    blocks = hidden // block
    once = lambda x: pl.BlockSpec(x.shape, lambda i: (0, 0), pipeline_mode=pl.Buffered(1))
    shape = (tokens, features)
    return pl.pallas_call(
        channel_kernel,
        out_shape=[jax.ShapeDtypeStruct(shape, d) for d in (BF16, BF16, BF16, F32, F32)],
        grid=(2 * blocks,),
        in_specs=[
            once(left),
            once(recep),
            pl.BlockSpec((features, block), lambda i: (0, lax.rem(i, blocks))),
            pl.BlockSpec((block, features), lambda i: (lax.rem(i, blocks), 0)),
            once(gate),
            once(after),
            once(top),
        ],
        out_specs=[pl.BlockSpec(shape, lambda i: (0, 0))] * 5,
        scratch_shapes=[pltpu.VMEM((tokens, hidden), F32), pltpu.VMEM(shape, F32)],
        compiler_params=pltpu.CompilerParams(vmem_limit_bytes=56 * 1024 * 1024),
        cost_estimate=pl.CostEstimate(
            flops=8 * tokens * features * (hidden + features // 2),
            bytes_accessed=8 * features * hidden + 20 * tokens * features,
            transcendentals=tokens * features,
        ),
    )(left, recep, up, down, gate, after, top)


def norm_rows(value_rows, gain_vec, bias_vec):
    row_mean = jnp.mean(value_rows, axis=-1, keepdims=True)
    centred = value_rows - row_mean
    inv_std = lax.rsqrt(jnp.mean(centred * centred, axis=-1, keepdims=True) + 1e-05)
    normed = centred * inv_std
    return (normed * gain_vec + bias_vec, normed, inv_std)


def norm_back(grad_in, normed, inv_std, gain_vec):
    scaled = grad_in * gain_vec
    return inv_std * (
        scaled
        - jnp.mean(scaled, axis=-1, keepdims=True)
        - normed * jnp.mean(scaled * normed, axis=-1, keepdims=True)
    )


def project(left_side, right_side):
    return jnp.einsum("rcd,de->rce", left_side, right_side, preferred_element_type=F32)


def project_back(grad_in, right_side):
    return jnp.einsum("rce,de->rcd", grad_in, right_side, preferred_element_type=F32)


def with_previous(value_rows, edge_row, keep):
    earlier = jnp.concatenate([edge_row[:, None, :], value_rows[:, :-1, :]], axis=1)
    return earlier * keep[:, :, None]


def flat(value):
    return value.reshape(-1, value.shape[-1])


def shards(
    incoming_symbols,
    article_sizes,
    mixer_norm_scale,
    mixer_norm_offset,
    temporal_lookup_share,
    temporal_payload_share,
    temporal_gate_share,
    fading_log_rates,
    present_reward_vector,
    lookup_matrix,
    payload_matrix,
    gate_matrix,
    emission_matrix,
    channel_norm_scale,
    channel_norm_offset,
    channel_lookup_share,
    channel_gate_share,
    channel_lookup_matrix,
    channel_payload_matrix,
    channel_gate_matrix,
    final_cotangent,
):
    rows_here, group_len, features = incoming_symbols.shape
    full = (rows_here, group_len, features)
    begins = jnp.cumsum(article_sizes, axis=1) - article_sizes
    position = lax.axis_index("seq") * group_len + jnp.arange(group_len, dtype=jnp.int32)
    starts = jnp.any(position[None, :, None] == begins[:, None, :], axis=2)
    keep = jnp.where(starts, 0.0, 1.0).astype(F32)
    ahead_windows, back_windows = keep_windows(article_sizes, group_len, 128)
    decay_rate = jnp.exp(fading_log_rates)
    rate_row = jnp.broadcast_to(decay_rate[None, :], (8, features))
    bonus_row = jnp.broadcast_to(present_reward_vector[None, :], (8, features))
    ready = article_sizes[0, 0] > 0
    enter = functools.partial(entering, begins=begins, decay_rate=decay_rate, group_len=group_len)

    symbols = incoming_symbols.astype(F32)
    att_last = norm_rows(symbols[:, -1, :], mixer_norm_scale, mixer_norm_offset)[0]
    att_edge = shifted(att_last, "seq", 1)
    att_normed, _, att_inv = norm_rows(symbols, mixer_norm_scale, mixer_norm_offset)
    att_mean = jnp.mean(symbols, axis=-1, keepdims=True)
    att_unit_again = lambda: (incoming_symbols.astype(F32) - att_mean) * att_inv
    att_prev = with_previous(att_normed, att_edge, keep)
    mix = lambda share: (att_normed * share + att_prev * (1.0 - share)).astype(BF16)
    key_mixed = mix(temporal_lookup_share)
    value_mixed = mix(temporal_payload_share)
    recep_mixed = mix(temporal_gate_share)
    key_proj = project(key_mixed, lookup_matrix)
    value_proj = project(value_mixed, payload_matrix)
    recep_proj = project(recep_mixed, gate_matrix)
    tails = ((2, rows_here, features), F32)
    (tail,) = scan_call(
        forward_tails_kernel, [key_proj, value_proj, ahead_windows, rate_row], [tails]
    )
    key_mixed, value_mixed, recep_mixed = map(flat, (key_mixed, value_mixed, recep_mixed))
    state, key_far, value_far, recep_far = at_once(
        ready,
        lambda: (enter(tail, backward=False), *map(send_whole, (key_mixed, value_mixed, recep_mixed))),
    )
    key_side, value_side, recep_side = (
        (key_mixed, key_far), (value_mixed, value_far), (recep_mixed, recep_far)
    )
    num_state, den_state, gated = scan_call(
        forward_states_kernel,
        [key_proj, value_proj, recep_proj, ahead_windows, rate_row, bonus_row, state],
        [(full, F32), (full, F32), (full, BF16)],
    )
    after_att = symbols + project(gated, emission_matrix)

    ffn_normed, ffn_unit, ffn_inv = norm_rows(after_att, channel_norm_scale, channel_norm_offset)
    gated = flat(gated)
    last_rows = ffn_normed[:, -1, :]
    ffn_edge, gated_far = at_once(
        ready, lambda: (shifted(last_rows, "seq", 1), send_whole(gated))
    )
    gated_side = (gated, gated_far)
    ffn_prev = with_previous(ffn_normed, ffn_edge, keep)
    def ffn_mix(share):
        rounded = lax.reduce_precision(ffn_normed * share + ffn_prev * (1.0 - share), 8, 7)
        return rounded.astype(BF16), rounded

    ffn_key_mixed, ffn_key_wide = ffn_mix(channel_lookup_share)
    ffn_recep_mixed, ffn_recep_wide = ffn_mix(channel_gate_share)
    line = Line()
    gate, mark = line.gate, line.mark
    fkey_far = send_across(flat(ffn_key_wide))
    layer_out, grad_fvalue, grad_frecep, grad_fkey_in, grad_frecep_in = channel_mix(
        flat(ffn_key_mixed), flat(ffn_recep_mixed), channel_lookup_matrix, channel_payload_matrix,
        channel_gate_matrix, flat(after_att), flat(final_cotangent),
    )
    layer_out, grad_fkey_in, grad_frecep_in = [
        x.reshape(full) for x in (layer_out, grad_fkey_in, grad_frecep_in)
    ]

    grad_top = final_cotangent.astype(F32)
    mark(grad_fvalue)
    fvalue_far = send_across(flat(grad_fvalue))
    ffn_delta = ffn_normed - ffn_prev
    grad_ffn_mix_key = jnp.sum(grad_fkey_in * ffn_delta, axis=(0, 1))
    grad_ffn_mix_recep = jnp.sum(grad_frecep_in * ffn_delta, axis=(0, 1))
    grad_ffn_prev = mark(
        (grad_fkey_in * (1.0 - channel_lookup_share) + grad_frecep_in * (1.0 - channel_gate_share))
        * keep[:, :, None]
    )
    first_row = gate(grad_ffn_prev[:, 0, :])
    ffn_back_edge, frecep_far, grad_frecep_far = at_once(
        ready,
        lambda: (
            shifted(first_row, "seq", -1),
            send_whole(flat(ffn_recep_wide)),
            send_half(flat(grad_frecep)),
        ),
    )
    mark(ffn_back_edge)
    grad_ffn_normed = (
        grad_fkey_in * channel_lookup_share
        + grad_frecep_in * channel_gate_share
        + jnp.concatenate([grad_ffn_prev[:, 1:, :], ffn_back_edge[:, None, :]], axis=1)
    )
    grad_ffn_ln_gain = jnp.sum(grad_ffn_normed * ffn_unit, axis=(0, 1))
    grad_ffn_ln_bias = jnp.sum(grad_ffn_normed, axis=(0, 1))
    grad_after = grad_top + norm_back(grad_ffn_normed, ffn_unit, ffn_inv, channel_norm_scale)

    grad_att_out = mark(grad_after.astype(BF16), fkey_far[1])
    grad_gated = project_back(gate(grad_att_out), emission_matrix)
    grad_num, grad_den, grad_recep, tail = scan_call(
        backward_tails_kernel,
        [grad_gated, key_proj, value_proj, recep_proj, num_state, den_state, back_windows, rate_row, bonus_row],
        [(full, F32), (full, F32), (full, BF16), tails],
    )
    fr = Partial("FR", (flat(ffn_recep_mixed), frecep_far), (flat(grad_frecep), grad_frecep_far))
    mark(tail, fkey_far[0], fvalue_far[0])
    gated_tail = gate(tail)
    state, (recep_far, out_far), fr.halves = at_once(
        ready,
        lambda: (
            enter(gated_tail, backward=True),
            send_half_of((flat(grad_recep), flat(grad_att_out))),
            fr.products(),
        ),
    )
    mark(state)

    step = functools.partial(phase, line, ready)
    ou = Partial("OU", (gated, gated_far), (flat(grad_att_out), out_far))
    ar = Partial("AR", recep_side, (flat(grad_recep), recep_far))
    fkey_cross = exchange(gate(fkey_far[1]), CORE)
    ou.multiply(line)
    fvalue_cross = exchange(gate(fvalue_far[1]), CORE)
    ar.multiply(line)
    mark(fkey_cross, fvalue_cross, ar.halves[0])

    halves = step(
        [fr, ou, ar],
        lambda: hidden_products(
            flat(ffn_key_mixed),
            (*fkey_far, fkey_cross),
            flat(grad_fvalue),
            (*fvalue_far, fvalue_cross),
            channel_lookup_matrix,
            channel_payload_matrix,
        ),
    )
    big_value, big_key = [Blocks(name, None, pair) for name, pair in zip(("BV", "BK"), halves)]
    big_key.forward(line)
    big_value.forward(line)
    grad_key, grad_value, sums = step(
        [ar, ou],
        lambda: scan_call(
            backward_states_kernel,
            [grad_num, grad_den, key_proj, value_proj, num_state, den_state, back_windows, rate_row, bonus_row, state],
            [(full, BF16), (full, BF16), ((16, features), F32)],
        ),
    )
    (key_far, value_far), grad_key_in, grad_value_in, grad_recep_in = step(
        [],
        lambda: (
            send_half_of((flat(grad_key), flat(grad_value))),
            project_back(grad_key, lookup_matrix),
            project_back(grad_value, payload_matrix),
            project_back(grad_recep, gate_matrix),
        ),
    )
    reward_slope = jnp.sum(sums[:8], axis=0)
    grad_time_decay = -decay_rate * jnp.exp(-decay_rate) * jnp.sum(sums[8:], axis=0)
    ak = Partial("AK", key_side, (flat(grad_key), key_far))
    av = Partial("AV", value_side, (flat(grad_value), value_far))
    ak.multiply(line)

    def mixes():
        normed = att_unit_again() * mixer_norm_scale + mixer_norm_offset
        att_delta = normed - with_previous(normed, att_edge, keep)
        att_back = (
            grad_key_in * (1.0 - temporal_lookup_share)
            + grad_value_in * (1.0 - temporal_payload_share)
            + grad_recep_in * (1.0 - temporal_gate_share)
        ) * keep[:, :, None]
        return (
            shifted(att_back[:, 0, :], "seq", -1),
            att_back,
            av.products(),
            jnp.sum(grad_key_in * att_delta, axis=(0, 1)),
            jnp.sum(grad_value_in * att_delta, axis=(0, 1)),
            jnp.sum(grad_recep_in * att_delta, axis=(0, 1)),
            grad_key_in * temporal_lookup_share
            + grad_value_in * temporal_payload_share
            + grad_recep_in * temporal_gate_share,
        )

    big_key.forward(line)
    big_value.forward(line)
    att_back_edge, grad_att_prev, av.halves, grad_mix_key, grad_mix_value, grad_mix_recep, direct = step(
        [ak], mixes
    )
    big_key.forward(line)
    big_value.forward(line)
    two = Stacked(line, [fr, ak])

    def norm_att():
        att_unit = att_unit_again()
        grad_att_normed = direct + jnp.concatenate(
            [grad_att_prev[:, 1:, :], att_back_edge[:, None, :]], axis=1
        )
        grad_tokens = (
            grad_after + norm_back(grad_att_normed, att_unit, att_inv, mixer_norm_scale)
        ).astype(BF16)
        return (
            grad_tokens,
            jnp.sum(grad_att_normed * att_unit, axis=(0, 1)),
            jnp.sum(grad_att_normed, axis=(0, 1)),
        )

    grad_tokens, grad_att_ln_gain, grad_att_ln_bias = step([two, av, ar], norm_att)
    vectors = Vectors(
        jnp.stack(
            [
                grad_att_ln_gain,
                grad_att_ln_bias,
                grad_mix_key,
                grad_mix_value,
                grad_mix_recep,
                grad_time_decay,
                reward_slope,
                grad_ffn_ln_gain,
                grad_ffn_ln_bias,
                grad_ffn_mix_key,
                grad_ffn_mix_recep,
            ]
        )
    )
    step([av, ou, vectors])
    big_key.forward(line)
    big_value.forward(line)
    three, pair = Stacked(line, [two, av]), Stacked(line, [ou, ar])
    step([three, pair, vectors])
    pairs = big_value.arrived(line), big_key.arrived(line)

    (ou_sum, ar_sum), quarters = step(
        [three, vectors],
        lambda: at_once(ready, lambda: (gather(total_of(pair.terms)), join_hidden(*pairs))),
    )
    (fr_sum, ak_sum, av_sum), (got, (value_sum, key_sum)) = step(
        [],
        lambda: gather(
            total_of(three.terms),
            lambda: at_once(ready, lambda: (vectors.hop(), whole_hidden(*quarters))),
        ),
    )
    vectors.landed(lax.optimization_barrier(got))
    small = total_of(vectors.terms)
    return (
        layer_out,
        grad_tokens,
        *[small[i] for i in range(7)],
        ak_sum,
        av_sum,
        ar_sum,
        ou_sum,
        *[small[i] for i in range(7, 11)],
        key_sum,
        value_sum,
        fr_sum,
    )


def solution(mesh):
    tokens = P("batch", "seq", None)
    vector, matrix = P("seq"), P("seq", None)
    return jax.shard_map(
        shards,
        mesh=mesh,
        in_specs=(tokens, P("batch", None), *([P()] * 18), tokens),
        out_specs=(tokens, tokens, *([vector] * 7), *([matrix] * 4), *([vector] * 4), *([matrix] * 3)),
        check_vma=False,
    )
```

```python
import functools
import math

import jax
import jax.numpy as jnp
from jax import lax
from jax.experimental import pallas as pl
from jax.experimental.pallas import tpu as pltpu
from jax.sharding import PartitionSpec as P

F32, BF16 = jnp.float32, jnp.bfloat16


def shifted(value, axis, distance):
    devices = range(lax.axis_size(axis))
    route = [(i - distance, i) for i in devices if i - distance in devices]
    return lax.ppermute(value, axis, route)


def bit_value(bit):
    axis, place = bit
    return (lax.axis_index(axis) >> place) & 1


def exchange(value, bit):
    axis, place = bit
    return lax.ppermute(value, axis, [(i, i ^ (1 << place)) for i in range(lax.axis_size(axis))])


def pick(value, index, dim):
    return lax.dynamic_index_in_dim(value, index, dim, keepdims=False)


def total_of(terms):
    return functools.reduce(lambda a, b: a + b, terms)


def axis_bits(axis):
    return [(axis, k) for k in range(int(math.log2(lax.axis_size(axis))))]


def at_once(ready, step, *values):
    blank = lambda *v: jax.tree.map(
        lambda x: jnp.zeros(x.shape, x.dtype), jax.eval_shape(step, *v)
    )
    return lax.cond(ready, step, blank, *values)


class Line:
    def __init__(self):
        self.token = None

    def gate(self, value):
        if self.token is None:
            return value
        return lax.optimization_barrier((value, self.token))[0]

    def mark(self, value, *others):
        self.token = (value, *others)
        return value


CORE = ("batch", 0)


def send_half(value):
    half = value.shape[1] // 2
    theirs = lax.dynamic_slice_in_dim(value, (1 - bit_value(CORE)) * half, half, 1)
    return exchange(theirs.astype(F32), CORE)


def send_half_of(values):
    half = values[0].shape[1] // 2
    at = (1 - bit_value(CORE)) * half
    theirs = [lax.dynamic_slice_in_dim(v, at, half, 1).astype(F32) for v in values]
    got = exchange(jnp.concatenate(theirs, axis=0), CORE)
    return jnp.split(got, len(values), axis=0)


def send_whole(value):
    return exchange(value.astype(F32), CORE)


CROSS = ("batch", 1)


def send_across(value):
    value = value.astype(F32)
    return exchange(value, CORE), exchange(value, CROSS)


def hidden_kernel(
    at_ref, *refs, unit,
):
    lefts, grads, (up_a, up_b, down_a, down_b, *outs, left_all, grad_all) = refs[:4], refs[4:8], refs[8:]
    value_send, value_keep, key_send, key_keep = outs
    z = pl.program_id(0) & 1
    tokens = lefts[0].shape[0]

    @pl.when(pl.program_id(0) == 0)
    def _():
        for k in range(4):
            at = pl.ds(k * tokens, tokens)
            left_all[at, :] = lefts[k][...].astype(BF16)
            grad_all[at, :] = grads[k][...].astype(BF16)

    up = jnp.concatenate([up_a[...], up_b[...]], axis=1)
    down = jnp.concatenate([down_a[...], down_b[...]], axis=0)
    first = lambda a, b: lax.dot_general(a, b, (((0,), (0,)), ((), ())), preferred_element_type=F32)

    def products(k):
        at = pl.ds(k * 2 * tokens, 2 * tokens)
        left, grad = left_all[at, :], grad_all[at, :]
        above = jnp.maximum(jnp.dot(left, up, preferred_element_type=F32), 0.0)
        back = lax.dot_general(grad, down, (((1,), (1,)), ((), ())), preferred_element_type=F32)
        return first((above * above).astype(BF16), grad), first((back * (2.0 * above)).astype(BF16), left)

    def put(value, key, add):
        def store(ref, index, part):
            ref[index] = ref[index] + part if add else part

        def values(ref):
            for half in range(2):
                store(ref, (0, half), value[half * unit : (half + 1) * unit])

        def keys(even, odd):
            rows = key.shape[1] // 8
            for s in range(8):
                store((even, odd)[s & 1], s >> 1, key[:, s * rows : (s + 1) * rows])

        pl.when(z == at_ref[1])(lambda: values(value_keep))
        pl.when(z != at_ref[1])(lambda: values(value_send))
        pl.when(at_ref[2] == 0)(lambda: keys(key_keep, key_send))
        pl.when(at_ref[2] != 0)(lambda: keys(key_send, key_keep))

    put(*products(0), False)
    put(*products(1), True)


def hidden_products(left, far_lefts, grad, far_grads, up, down):
    seq, tokens, features = lax.axis_size("seq"), left.shape[0], left.shape[1]
    unit = up.shape[1] // seq // 4
    quarter = 2 * bit_value(CORE) + bit_value(CROSS)
    if unit % 128 or features // seq % 128 or seq != 8:
        up = pick(up.reshape(features, seq, 4, unit), quarter, 2).reshape(features, -1)
        down = pick(down.reshape(seq, 4, unit, features), quarter, 1).reshape(-1, features)
        lefts = jnp.concatenate([left, *[f.astype(BF16) for f in far_lefts]])
        grads = jnp.concatenate([grad, *[f.astype(BF16) for f in far_grads]])
        above = jnp.maximum(jnp.dot(lefts, up, preferred_element_type=F32), 0.0)
        back = lax.dot_general(grads, down, (((1,), (1,)), ((), ())), preferred_element_type=F32)
        first = lambda a, b: lax.dot_general(a, b, (((0,), (0,)), ((), ())), preferred_element_type=F32)
        value = first((above * above).astype(BF16), grads).reshape(seq, unit, features)
        key = first((back * (2.0 * above)).astype(BF16), lefts)
        key = jnp.swapaxes(key.reshape(-1, seq, features // seq), 0, 1)
        return Blocks("BV", value).first(), Blocks("BK", key).first()
    whole = lambda: pl.BlockSpec((tokens, features), lambda i, at: (0, 0), pipeline_mode=pl.Buffered(1))
    ups = [pl.BlockSpec((features, unit), lambda i, at, h=h: (0, 4 * (2 * i + h) + at[0])) for h in (0, 1)]
    downs = [pl.BlockSpec((unit, features), lambda i, at, h=h: (4 * (2 * i + h) + at[0], 0)) for h in (0, 1)]
    at = jnp.stack([quarter, *[bit_value(order_of(name)[0][0]) for name in ("BV", "BK")]])
    halves = [(2, 2, unit, features)] * 2 + [(4, seq * unit, features // seq)] * 2
    value_spec = pl.BlockSpec((1, 2, unit, features), lambda i, at: (i >> 1, 0, 0, 0))
    key_spec = pl.BlockSpec((4, 2 * unit, features // seq), lambda i, at: (0, i, 0))
    made = pl.pallas_call(
        functools.partial(hidden_kernel, unit=unit),
        grid_spec=pltpu.PrefetchScalarGridSpec(
            num_scalar_prefetch=1,
            grid=(seq // 2,),
            in_specs=[whole() for _ in range(8)] + ups + downs,
            out_specs=[value_spec, value_spec, key_spec, key_spec],
            scratch_shapes=[pltpu.VMEM((4 * tokens, features), BF16)] * 2,
        ),
        out_shape=[jax.ShapeDtypeStruct(shape, F32) for shape in halves],
        compiler_params=pltpu.CompilerParams(vmem_limit_bytes=56 * 1024 * 1024),
        cost_estimate=pl.CostEstimate(
            flops=32 * tokens * features * seq * unit,
            bytes_accessed=40 * tokens * features,
            transcendentals=0,
        ),
    )(at.astype(jnp.int32), left, *far_lefts, grad, *far_grads, up, up, down, down)
    made = [x.reshape(2, 2, *x.shape[-2:]) for x in made]
    return made[:2], made[2:]


ORDERS = dict(BV="zywx", BK="yzwx", FR="xyzw", OU="zxyw", AR="yxzw", AK="xyzw", AV="xyzw")


def order_of(name):
    seq = axis_bits("seq")
    places = dict(x=axis_bits("batch")[1:], y=seq[:1], z=seq[1:2], w=seq[2:])
    return [places[letter] for letter in ORDERS[name]]


def halve(terms, dims, bit):
    if bit not in dims:
        total = total_of(terms)
        return total, [total]
    dim, mine = dims.index(bit), bit_value(bit)
    send = total_of([pick(t, 1 - mine, dim) for t in terms])
    return send, [pick(t, mine, dim) for t in terms]


class Blocks:
    halves = None

    def __init__(self, name, value, halves=None):
        self.hops, self.dims = order_of(name), axis_bits("seq")[::-1]
        self.halves, self.terms = halves, None
        if halves is None:
            self.terms = [value.reshape(*((2,) * len(self.dims)), *value.shape[1:])]

    def first(self):
        send, kept = self.split(self.terms)
        return send, kept[0]

    def split(self, terms):
        if self.halves:
            return self.halves[0], [self.halves[1]]
        return halve(terms, self.dims, self.hops[0][0])

    def go(self, sends):
        bits, dims = self.hops[0], list(self.dims)
        got = exchange(sends, bits[0])
        if len(bits) == 1:
            return got
        terms = self.split(self.terms)[1] + [got]
        dims = [d for d in dims if d != bits[0]]
        for bit in bits[1:]:
            send, kept = halve(terms, dims, bit)
            terms = kept + [exchange(send, bit)]
            dims = [d for d in dims if d != bit]
        return total_of(terms)

    def hop(self):
        return self.go(self.split(self.terms)[0])

    def landed(self, got):
        bits = self.hops[0]
        self.terms = self.split(self.terms)[1] + [got] if len(bits) == 1 else [got]
        self.halves = None
        self.dims = [d for d in self.dims if d not in bits]
        self.hops.pop(0)

    def arrived(self, line):
        return self.terms[:-1] + [line.gate(self.terms[-1])]

    def forward(self, line):
        if self.halves:
            send = line.gate(self.halves[0])
        else:
            send = self.split(self.arrived(line))[0]
        self.landed(self.go(line.mark(send)))


def phase(line, ready, jobs, beside=None):
    def step():
        return [job.hop() for job in jobs], beside() if beside else ()

    got, more = at_once(line.gate(ready), step)
    for job, value in zip(jobs, got):
        job.landed(value)
    line.mark(*jax.tree.leaves((got, more)))
    return more


def product_kernel(
    at_ref, left_ref, far_left_ref, right_ref, far_right_ref, send_ref, keep_ref,
    *, rows, cols, group, place,
):
    first = at_ref[0]

    def lefts(blocks):
        cut = lambda ref, js: jnp.concatenate(
            [ref[:, pl.ds(pl.multiple_of(j * rows, 128), rows)] for j in js], axis=1
        )
        return jnp.concatenate([cut(left_ref, blocks), cut(far_left_ref, blocks).astype(BF16)], axis=0)

    def rights(x):
        at = pl.ds(pl.multiple_of(x * cols, 128), cols)
        return jnp.concatenate([right_ref[:, at], far_right_ref[:, at].astype(BF16)], axis=0)

    dot = lambda a, b: lax.dot_general(
        a, b, (((0,), (0,)), ((), ())), preferred_element_type=F32
    )
    for out, value in ((send_ref, 1 - first), (keep_ref, first)):
        if place is None:
            out[0] = dot(lefts(list(range(group))), rights(value))
        else:
            low = 1 << place
            blocks = [(q // low) * 2 * low + q % low + value * low for q in range(group // 2)]
            left = lefts(blocks)
            for x in range(2):
                out[x, 0] = dot(left, rights(x))


class Partial(Blocks):
    def __init__(self, name, left, right):
        self.left, self.right = left, right
        self.hops, self.terms = order_of(name), None
        self.dims = axis_bits("batch")[1:] + axis_bits("seq")[::-1]
        self.blocks = lax.axis_size("seq")
        self.rows = left[0].shape[1] // self.blocks
        self.cols = right[0].shape[1] // 4

    def plain(self):
        half = self.right[0].shape[1] // 2
        own = lax.dynamic_slice_in_dim(self.right[0], bit_value(CORE) * half, half, 1)
        dot = lambda a, b: lax.dot_general(
            a.astype(BF16), b.astype(BF16), (((0,), (0,)), ((), ())), preferred_element_type=F32
        )
        whole = dot(self.left[0], own) + dot(self.left[1], self.right[1])
        lead = (2,) * len(axis_bits("seq"))
        whole = jnp.moveaxis(whole.reshape(*lead, self.rows, 2, self.cols), -2, 0)
        send, kept = halve([whole], self.dims, self.hops[0][0])
        return send, kept[0]

    def kernel(self):
        rows, cols, tokens = self.rows, self.cols, self.left[0].shape[0]
        first = self.hops[0][0]
        place = first[1] if first[0] == "seq" else None
        group = 4
        steps = self.blocks // group
        if place is None:
            block, shape = (1, group * rows, cols), (steps, group * rows, cols)
            out_index = lambda i, at: (i, 0, 0)
        else:
            block, shape = (2, 1, group // 2 * rows, cols), (2, steps, group // 2 * rows, cols)
            out_index = lambda i, at: (0, i, 0, 0)
        out = jax.ShapeDtypeStruct(shape, F32)
        at = jnp.stack([bit_value(first), bit_value(CORE)]).astype(jnp.int32)
        send, kept = pl.pallas_call(
            functools.partial(
                product_kernel, rows=rows, cols=cols, group=group, place=place
            ),
            grid_spec=pltpu.PrefetchScalarGridSpec(
                num_scalar_prefetch=1,
                grid=(steps,),
                in_specs=[
                    pl.BlockSpec((tokens, group * rows), lambda i, at: (0, i)),
                    pl.BlockSpec((tokens, group * rows), lambda i, at: (0, i)),
                    pl.BlockSpec((tokens, 2 * cols), lambda i, at: (0, at[1])),
                    pl.BlockSpec((tokens, 2 * cols), lambda i, at: (0, 0)),
                ],
                out_specs=[pl.BlockSpec(block, out_index)] * 2,
            ),
            out_shape=[out, out],
            compiler_params=scan_params(),
            cost_estimate=pl.CostEstimate(
                flops=8 * tokens * self.blocks * rows * cols,
                bytes_accessed=8 * self.blocks * rows * cols,
                transcendentals=0,
            ),
        )(at, self.left[0], self.left[1], self.right[0], self.right[1])
        lead = (2,) * (len(self.dims) - 1)
        return send.reshape(*lead, rows, cols), kept.reshape(*lead, rows, cols)

    def products(self):
        aligned = self.rows % 128 == 0 and self.blocks % 4 == 0 and len(axis_bits("batch")) == 2
        return self.kernel() if aligned else self.plain()

    def multiply(self, line):
        self.left = (line.gate(self.left[0]), self.left[1])
        self.halves = self.products()
        line.mark(self.halves[0])


class Stacked(Blocks):
    def __init__(self, line, jobs):
        self.hops, self.dims = list(jobs[0].hops), jobs[0].dims
        sums = [total_of(j.arrived(line)) for j in jobs]
        sums = [v if isinstance(j, Stacked) else v[..., None, :, :] for j, v in zip(jobs, sums)]
        self.terms = [jnp.concatenate(sums, axis=-3)]


class Vectors(Blocks):
    def __init__(self, vectors):
        vectors = jnp.pad(vectors, ((0, -vectors.shape[0] % 8), (0, 0)))
        count, seq = vectors.shape[0], lax.axis_size("seq")
        self.dims = axis_bits("seq")[::-1]
        bits = axis_bits("seq")
        self.hops = [axis_bits("batch")] + [[b] for b in bits[:2]] + [bits[2:]]
        value = jnp.swapaxes(vectors.reshape(count, seq, -1), 0, 1)
        self.terms = [value.reshape(*((2,) * len(self.dims)), count, -1)]

def in_order(own, other, bit, axis):
    first = bit_value(bit) == 0
    return jnp.concatenate(
        [jnp.where(first, own, other), jnp.where(first, other, own)], axis=axis
    )


def gather(own, beside=None):
    other, more = exchange(own, CROSS), None
    if beside:
        other, more = lax.optimization_barrier((other, beside()))
    own = in_order(own, other, CROSS, 2)
    own = in_order(own, exchange(own, CORE), CORE, 2)
    joined = [own[i] for i in range(own.shape[0])]
    return (joined, more) if beside else joined


def join_hidden(values, keys):
    seq = lax.axis_size("seq")
    value = in_order(*values, CROSS, 0)
    key = in_order(*[t.reshape(seq, 1, -1, t.shape[-1]) for t in keys], CROSS, 1)
    return (value, exchange(value, CORE)), (key, exchange(key, CORE))


def whole_hidden(values, keys):
    key = in_order(*keys, CORE, 1)
    return in_order(*values, CORE, 0), jnp.transpose(key.reshape(-1, key.shape[-1]))


def entering(tails, begins, decay_rate, group_len, backward):
    count, mine = lax.axis_size("seq"), lax.axis_index("seq")
    sign, radix = (-1, 4) if backward else (1, 2)

    def gain(lo, hi):
        a, b = (mine + lo, mine + hi) if backward else (mine - hi + 1, mine - lo + 1)
        hit = jnp.any((begins >= a * group_len) & (begins < b * group_len), axis=1, keepdims=True)
        return jnp.where(hit, 0.0, 1.0) * jnp.exp(-float((hi - lo) * group_len) * decay_rate)[None, :]

    reach, window, before = 1, tails, None
    while reach < count:
        got = [
            (j, shifted(window, "seq", sign * j * reach))
            for j in range(1, radix)
            if j * reach < count
        ]
        if before is None:
            before = total_of([v if j == 1 else gain(1, j) * v for j, v in got])
            seen = 1 + len(got)
            window = tails + gain(0, 1) * before if seen < count else None
        else:
            before_more = total_of([gain(1, j * reach) * v for j, v in got])
            seen = reach * (1 + len(got))
            if seen < count:
                window = window + total_of([gain(0, j * reach) * v for j, v in got])
            before = before + before_more
        reach *= radix
    return before


def scan_params():
    return pltpu.CompilerParams(vmem_limit_bytes=48 * 1024 * 1024)


def lane_tiles(width):
    return [slice(i, i + 128) for i in range(0, width, 128)]


WINDOW = {name: k for k, name in enumerate(("keep", "one", "two", "four", "group", "eight", "end"))}


def windows_kernel(sizes_ref, block_ref, ahead_ref, back_ref):
    rows, length, width = ahead_ref.shape[1:]
    t = lax.broadcasted_iota(jnp.int32, (length, width), 0)
    inner = t & 7

    def put(ref, name, equal, inside=None):
        kept = equal if inside is None else equal & inside
        ref[WINDOW[name], row] = jnp.where(kept, 1.0, 0.0)

    for row in range(rows):
        begins, at = [], -block_ref[0]
        for j in range(sizes_ref.shape[1]):
            begins.append(at)
            at = at + sizes_ref[row, j]

        def begun(by):
            return total_of([jnp.where(by >= b, 1, 0) for b in begins])

        here, ahead_of = begun(t), begun(t - 1)
        keep = here == ahead_of
        put(ahead_ref, "keep", keep)
        put(back_ref, "keep", keep)
        for name, n in (("one", 1), ("two", 2), ("four", 4)):
            put(ahead_ref, name, here == begun(t - n), inner >= n)
            put(back_ref, name, begun(t + (n - 1)) == ahead_of, inner <= 7 - n)
        put(ahead_ref, "group", here == begun(t - inner - 1))
        put(back_ref, "group", begun(t - inner + 7) == ahead_of)
        put(ahead_ref, "eight", here == begun(t - 8), t >= 8)
        put(back_ref, "eight", begun(t + 7) == ahead_of, t < length - 8)
        put(ahead_ref, "end", here == begun(jnp.full_like(t, length - 1)))
        put(back_ref, "end", ahead_of == begun(jnp.full_like(t, -1)))


def keep_windows(sizes, length, width):
    block = (lax.axis_index("seq") * length)[None].astype(jnp.int32)
    out = jax.ShapeDtypeStruct((len(WINDOW), sizes.shape[0], length, width), F32)
    return pl.pallas_call(
        windows_kernel,
        out_shape=[out, out],
        in_specs=[pl.BlockSpec(memory_space=pltpu.SMEM)] * 2,
        compiler_params=scan_params(),
        cost_estimate=pl.CostEstimate(flops=100 * out.size, bytes_accessed=8 * out.size, transcendentals=0),
    )(sizes, block)


def powers(rate_ref, tiles):
    return lambda n: [jnp.exp(-n * rate_ref[0:1, t]) for t in tiles]


def inner_place(shape=(8, 128)):
    return lax.broadcasted_iota(jnp.int32, shape, 0)


def spread(row):
    return jnp.broadcast_to(row, (8, 128))


def in_group(value, factors, back):
    for n, factor in zip((1, 2, 4), factors):
        value = value + factor * pltpu.roll(value, 8 - n if back else n, 0)
    return value


def halves_of(ref, row, at, tile):
    value = ref[row, at, tile]
    return value[:8], value[8:]


def windows_at(win_ref, row, at):
    names = ("keep", "one", "two", "four", "group")
    return [dict(zip(names, v)) for v in zip(*[halves_of(win_ref.at[WINDOW[n]], row, at, slice(None)) for n in names])]


def pair_at(p):
    return pl.ds(pl.multiple_of(p * 16, 16), 16)


def forward_tails_kernel(k_ref, v_ref, win_ref, rate_ref, tail_ref):
    rows, length, width = k_ref.shape
    tiles = lane_tiles(width)
    chains = [(r, i, t) for r in range(rows) for i, t in enumerate(tiles)]
    eight = powers(rate_ref, tiles)(8.0)

    def step(p, carry):
        at, out = pair_at(p), []
        windows = [halves_of(win_ref.at[WINDOW["eight"]], r, at, slice(None)) for r in range(rows)]
        for (r, i, t), (num, den) in zip(chains, carry):
            for h, (key, value) in enumerate(zip(halves_of(k_ref, r, at, t), halves_of(v_ref, r, at, t))):
                factor, e = windows[r][h] * eight[i], jnp.exp(key)
                num, den = factor * num + e * value, factor * den + e
            out.append((num, den))
        return tuple(out)

    zero = jnp.zeros((8, 128), F32)
    done = lax.fori_loop(0, length // 16, step, tuple((zero, zero) for _ in chains), unroll=2)
    left = powers(rate_ref, tiles)((7 - inner_place()).astype(F32))
    for (r, i, t), pair in zip(chains, done):
        factor = win_ref[WINDOW["end"], r, pl.ds(length - 8, 8), :] * left[i]
        for q in range(2):
            tail_ref[q, r : r + 1, t] = jnp.sum(factor * pair[q], axis=0, keepdims=True)


def forward_states_kernel(
    k_ref, v_ref, recep_ref, win_ref, rate_ref, bonus_ref, enter_ref, num_ref, den_ref, gated_ref
):
    rows, length, width = k_ref.shape
    tiles = lane_tiles(width)
    chains = [(r, i, t) for r in range(rows) for i, t in enumerate(tiles)]
    power = powers(rate_ref, tiles)
    ones, twos, fours = power(1.0), power(2.0), power(4.0)
    groups = power((1 + inner_place()).astype(F32))
    head = inner_place() == 0

    def step(p, carry):
        at, out = pair_at(p), []
        windows = [windows_at(win_ref, r, at) for r in range(rows)]
        for (r, i, t), states in zip(chains, carry):
            keys, values = halves_of(k_ref, r, at, t), halves_of(v_ref, r, at, t)
            receps, bonus, results = halves_of(recep_ref, r, at, t), bonus_ref[0:1, t], []
            for h in range(2):
                w = windows[r][h]
                factors = (w["one"] * ones[i], w["two"] * twos[i], w["four"] * fours[i])
                group = w["group"] * groups[i]
                e, held, here = jnp.exp(keys[h]), [], []
                for state, item in zip(states, (e * values[h], e)):
                    full = in_group(item, factors, False) + group * state
                    here.append(w["keep"] * jnp.where(head, state, pltpu.roll(full, 1, 0)))
                    held.append(spread(full[7:8]))
                states = held
                first = jnp.exp(bonus + keys[h])
                wkv = (here[0] + first * values[h]) / (here[1] + first)
                results.append((*here, jax.nn.sigmoid(receps[h]) * wkv))
            for ref, two in zip((num_ref, den_ref, gated_ref), zip(*results)):
                ref[r, at, t] = jnp.concatenate(two, axis=0).astype(ref.dtype)
            out.append(tuple(states))
        return tuple(out)

    start = tuple(tuple(spread(enter_ref[q, r : r + 1, t]) for q in range(2)) for r, _, t in chains)
    lax.fori_loop(0, length // 16, step, start)


def backward_tails_kernel(
    grad_ref, k_ref, v_ref, recep_ref, num_ref, den_ref, win_ref, rate_ref, bonus_ref,
    gnum_ref, gden_ref, grecep_ref, tail_ref,
):
    rows, length, width = k_ref.shape
    tiles = lane_tiles(width)
    chains = [(r, i, t) for r in range(rows) for i, t in enumerate(tiles)]
    eight = powers(rate_ref, tiles)(8.0)
    pairs = length // 16

    def step(p, carry):
        at, out = pair_at(pairs - 1 - p), []
        keeps = [halves_of(win_ref.at[WINDOW["keep"]], r, at, slice(None)) for r in range(rows)]
        windows = [halves_of(win_ref.at[WINDOW["eight"]], r, at, slice(None)) for r in range(rows)]
        for (r, i, t), (late_num, late_den) in zip(chains, carry):
            key, value = k_ref[r, at, t], v_ref[r, at, t]
            first = jnp.exp(bonus_ref[0:1, t] + key)
            below = den_ref[r, at, t] + first
            wkv = (num_ref[r, at, t] + first * value) / below
            gate, grad = jax.nn.sigmoid(recep_ref[r, at, t]), grad_ref[r, at, t]
            grecep_ref[r, at, t] = (grad * wkv * (gate * (1.0 - gate))).astype(BF16)
            up = grad * gate / below
            low = -up * wkv
            gnum_ref[r, at, t] = up
            gden_ref[r, at, t] = low
            for h in (1, 0):
                rows_of = slice(8 * h, 8 * h + 8)
                factor, keep = windows[r][h] * eight[i], keeps[r][h]
                late_num = factor * late_num + keep * up[rows_of]
                late_den = factor * late_den + keep * low[rows_of]
            out.append((late_num, late_den))
        return tuple(out)

    zero = jnp.zeros((8, 128), F32)
    done = lax.fori_loop(0, pairs, step, tuple((zero, zero) for _ in chains))
    left = powers(rate_ref, tiles)(inner_place().astype(F32))
    for (r, i, t), pair in zip(chains, done):
        factor = win_ref[WINDOW["end"], r, pl.ds(0, 8), :] * left[i]
        for q in range(2):
            tail_ref[q, r : r + 1, t] = jnp.sum(factor * pair[q], axis=0, keepdims=True)


def backward_states_kernel(
    gnum_ref, gden_ref, k_ref, v_ref, num_ref, den_ref, win_ref, rate_ref, bonus_ref, enter_ref,
    gkey_ref, gvalue_ref, sums_ref,
):
    rows, length, width = k_ref.shape
    tiles = lane_tiles(width)
    chains = [(r, i, t) for r in range(rows) for i, t in enumerate(tiles)]
    power = powers(rate_ref, tiles)
    ones, twos, fours = power(1.0), power(2.0), power(4.0)
    groups = power((8 - inner_place()).astype(F32))
    tail = inner_place() == 7
    pairs = length // 16

    def step(p, carry):
        at, out = pair_at(pairs - 1 - p), []
        windows = [windows_at(win_ref, r, at) for r in range(rows)]
        for (r, i, t), (num_state, den_state, slope, fade) in zip(chains, carry):
            states, parts = (num_state, den_state), []
            keys, values = halves_of(k_ref, r, at, t), halves_of(v_ref, r, at, t)
            ups, lows = halves_of(gnum_ref, r, at, t), halves_of(gden_ref, r, at, t)
            nums, dens = halves_of(num_ref, r, at, t), halves_of(den_ref, r, at, t)
            for h in (1, 0):
                w = windows[r][h]
                factors = (w["one"] * ones[i], w["two"] * twos[i], w["four"] * fours[i])
                group, held, here = w["group"] * groups[i], [], []
                for state, item in zip(states, (ups[h], lows[h])):
                    full = in_group(w["keep"] * item, factors, True) + group * state
                    here.append(jnp.where(tail, state, pltpu.roll(full, 7, 0)))
                    held.append(spread(full[0:1]))
                states = held
                e, first = jnp.exp(keys[h]), jnp.exp(bonus_ref[0:1, t] + keys[h])
                present = first * (ups[h] * values[h] + lows[h])
                slope = slope + present
                fade = fade + nums[h] * here[0] + dens[h] * here[1]
                parts.append(
                    (
                        present + e * (here[0] * values[h] + here[1]),
                        ups[h] * first + here[0] * e,
                    )
                )
            for ref, two in zip((gkey_ref, gvalue_ref), zip(*parts[::-1])):
                ref[r, at, t] = jnp.concatenate(two, axis=0).astype(BF16)
            out.append((*states, slope, fade))
        return tuple(out)

    zero = jnp.zeros((8, 128), F32)
    start = tuple(
        (*[spread(enter_ref[q, r : r + 1, t]) for q in range(2)], zero, zero) for r, _, t in chains
    )
    done = lax.fori_loop(0, pairs, step, start)
    for i, t in enumerate(tiles):
        for q in range(2):
            sums_ref[8 * q : 8 * q + 8, t] = total_of(
                [c[2 + q] for (_, j, _), c in zip(chains, done) if j == i]
            )


def scan_call(kernel, inputs, outputs, width=512):
    features = inputs[0].shape[-1]

    def spec(shape):
        lead = len(shape) - 1
        if shape[-1] == 128 and features != 128:
            return pl.BlockSpec(shape, lambda i: (0,) * (lead + 1))
        return pl.BlockSpec((*shape[:-1], width), lambda i: (0,) * lead + (i,))

    out_shape = [jax.ShapeDtypeStruct(s, d) for s, d in outputs]
    moved = sum(x.size * x.dtype.itemsize for x in [*inputs, *out_shape])
    return pl.pallas_call(
        kernel,
        out_shape=out_shape,
        grid=(features // width,),
        in_specs=[spec(x.shape) for x in inputs],
        out_specs=[spec(s) for s, _ in outputs],
        compiler_params=scan_params(),
        cost_estimate=pl.CostEstimate(
            flops=20 * inputs[0].size, bytes_accessed=moved, transcendentals=inputs[0].size
        ),
    )(*inputs)


def channel_kernel(
    left_ref, recep_ref, up_ref, down_ref, gate_ref, after_ref, top_ref,
    out_ref, fvalue_ref, frecep_ref, fkey_ref, recep_in_ref, above_ref, total_ref,
):
    across = (((1,), (1,)), ((), ()))
    block = up_ref.shape[1]
    step, blocks = pl.program_id(0), pl.num_programs(0) // 2

    def at(i):
        return pl.ds(pl.multiple_of(i * block, block), block)

    def add(ref, first, part):
        @pl.when(step == first)
        def _():
            ref[...] = part

        @pl.when(step > first)
        def _():
            ref[...] += part

    @pl.when(step < blocks)
    def _():
        above = jnp.maximum(jnp.dot(left_ref[...], up_ref[...], preferred_element_type=F32), 0.0)
        above_ref[:, at(step)] = above
        add(total_ref, 0, jnp.dot((above * above).astype(BF16), down_ref[...], preferred_element_type=F32))

    @pl.when(step == blocks - 1)
    def _():
        value = total_ref[...]
        gate = jax.nn.sigmoid(
            jnp.dot(recep_ref[...], gate_ref[...], preferred_element_type=F32)
        )
        top = top_ref[...].astype(F32)
        out_ref[...] = (after_ref[...] + gate * value).astype(BF16)
        fvalue_ref[...] = (top * gate).astype(BF16)
        frecep = (top * value * (gate * (1.0 - gate))).astype(BF16)
        frecep_ref[...] = frecep
        recep_in_ref[...] = lax.dot_general(
            frecep, gate_ref[...], across, preferred_element_type=F32
        )

    @pl.when(step >= blocks)
    def _():
        back = lax.dot_general(fvalue_ref[...], down_ref[...], across, preferred_element_type=F32)
        hidden = (back * (2.0 * above_ref[:, at(step - blocks)])).astype(BF16)
        add(fkey_ref, blocks, lax.dot_general(hidden, up_ref[...], across, preferred_element_type=F32))


def channel_mix(left, recep, up, down, gate, after, top):
    (tokens, features), hidden = left.shape, up.shape[1]
    block = min(1024, hidden)
    blocks = hidden // block
    once = lambda x: pl.BlockSpec(x.shape, lambda i: (0, 0), pipeline_mode=pl.Buffered(1))
    shape = (tokens, features)
    return pl.pallas_call(
        channel_kernel,
        out_shape=[jax.ShapeDtypeStruct(shape, d) for d in (BF16, BF16, BF16, F32, F32)],
        grid=(2 * blocks,),
        in_specs=[
            once(left),
            once(recep),
            pl.BlockSpec((features, block), lambda i: (0, lax.rem(i, blocks))),
            pl.BlockSpec((block, features), lambda i: (lax.rem(i, blocks), 0)),
            once(gate),
            once(after),
            once(top),
        ],
        out_specs=[pl.BlockSpec(shape, lambda i: (0, 0))] * 5,
        scratch_shapes=[pltpu.VMEM((tokens, hidden), F32), pltpu.VMEM(shape, F32)],
        compiler_params=pltpu.CompilerParams(vmem_limit_bytes=56 * 1024 * 1024),
        cost_estimate=pl.CostEstimate(
            flops=8 * tokens * features * (hidden + features // 2),
            bytes_accessed=8 * features * hidden + 20 * tokens * features,
            transcendentals=tokens * features,
        ),
    )(left, recep, up, down, gate, after, top)


def norm_rows(value_rows, gain_vec, bias_vec):
    row_mean = jnp.mean(value_rows, axis=-1, keepdims=True)
    centred = value_rows - row_mean
    inv_std = lax.rsqrt(jnp.mean(centred * centred, axis=-1, keepdims=True) + 1e-05)
    normed = centred * inv_std
    return (normed * gain_vec + bias_vec, normed, inv_std)


def norm_back(grad_in, normed, inv_std, gain_vec):
    scaled = grad_in * gain_vec
    return inv_std * (
        scaled
        - jnp.mean(scaled, axis=-1, keepdims=True)
        - normed * jnp.mean(scaled * normed, axis=-1, keepdims=True)
    )


def project(left_side, right_side):
    return jnp.einsum("rcd,de->rce", left_side, right_side, preferred_element_type=F32)


def project_back(grad_in, right_side):
    return jnp.einsum("rce,de->rcd", grad_in, right_side, preferred_element_type=F32)


def with_previous(value_rows, edge_row, keep):
    earlier = jnp.concatenate([edge_row[:, None, :], value_rows[:, :-1, :]], axis=1)
    return earlier * keep[:, :, None]


def flat(value):
    return value.reshape(-1, value.shape[-1])


def shards(
    incoming_symbols,
    article_sizes,
    mixer_norm_scale,
    mixer_norm_offset,
    temporal_lookup_share,
    temporal_payload_share,
    temporal_gate_share,
    fading_log_rates,
    present_reward_vector,
    lookup_matrix,
    payload_matrix,
    gate_matrix,
    emission_matrix,
    channel_norm_scale,
    channel_norm_offset,
    channel_lookup_share,
    channel_gate_share,
    channel_lookup_matrix,
    channel_payload_matrix,
    channel_gate_matrix,
    final_cotangent,
):
    rows_here, group_len, features = incoming_symbols.shape
    full = (rows_here, group_len, features)
    begins = jnp.cumsum(article_sizes, axis=1) - article_sizes
    position = lax.axis_index("seq") * group_len + jnp.arange(group_len, dtype=jnp.int32)
    starts = jnp.any(position[None, :, None] == begins[:, None, :], axis=2)
    keep = jnp.where(starts, 0.0, 1.0).astype(F32)
    ahead_windows, back_windows = keep_windows(article_sizes, group_len, 128)
    decay_rate = jnp.exp(fading_log_rates)
    rate_row = jnp.broadcast_to(decay_rate[None, :], (8, features))
    bonus_row = jnp.broadcast_to(present_reward_vector[None, :], (8, features))
    ready = article_sizes[0, 0] > 0
    enter = functools.partial(entering, begins=begins, decay_rate=decay_rate, group_len=group_len)

    symbols = incoming_symbols.astype(F32)
    att_last = norm_rows(symbols[:, -1, :], mixer_norm_scale, mixer_norm_offset)[0]
    att_edge = shifted(att_last, "seq", 1)
    att_normed, _, att_inv = norm_rows(symbols, mixer_norm_scale, mixer_norm_offset)
    att_mean = jnp.mean(symbols, axis=-1, keepdims=True)
    att_unit_again = lambda: (incoming_symbols.astype(F32) - att_mean) * att_inv
    att_prev = with_previous(att_normed, att_edge, keep)
    mix = lambda share: lax.reduce_precision(att_normed * share + att_prev * (1.0 - share), 8, 7)
    att_wide = [mix(s) for s in (temporal_lookup_share, temporal_payload_share, temporal_gate_share)]
    key_mixed, value_mixed, recep_mixed = [x.astype(BF16) for x in att_wide]
    key_proj = project(key_mixed, lookup_matrix)
    value_proj = project(value_mixed, payload_matrix)
    recep_proj = project(recep_mixed, gate_matrix)
    tails = ((2, rows_here, features), F32)
    (tail,) = scan_call(
        forward_tails_kernel, [key_proj, value_proj, ahead_windows, rate_row], [tails]
    )
    key_mixed, value_mixed, recep_mixed = map(flat, (key_mixed, value_mixed, recep_mixed))
    state, key_far, value_far, recep_far = at_once(
        ready,
        lambda: (enter(tail, backward=False), *map(send_whole, map(flat, att_wide))),
    )
    key_side, value_side, recep_side = (
        (key_mixed, key_far), (value_mixed, value_far), (recep_mixed, recep_far)
    )
    num_state, den_state, gated = scan_call(
        forward_states_kernel,
        [key_proj, value_proj, recep_proj, ahead_windows, rate_row, bonus_row, state],
        [(full, F32), (full, F32), (full, BF16)],
    )
    after_att = symbols + project(gated, emission_matrix)

    ffn_normed, ffn_unit, ffn_inv = norm_rows(after_att, channel_norm_scale, channel_norm_offset)
    gated = flat(gated)
    last_rows = ffn_normed[:, -1, :]
    ffn_edge, gated_far = at_once(
        ready, lambda: (shifted(last_rows, "seq", 1), send_whole(gated))
    )
    gated_side = (gated, gated_far)
    ffn_prev = with_previous(ffn_normed, ffn_edge, keep)
    def ffn_mix(share):
        rounded = lax.reduce_precision(ffn_normed * share + ffn_prev * (1.0 - share), 8, 7)
        return rounded.astype(BF16), rounded

    ffn_key_mixed, ffn_key_wide = ffn_mix(channel_lookup_share)
    ffn_recep_mixed, ffn_recep_wide = ffn_mix(channel_gate_share)
    line = Line()
    gate, mark = line.gate, line.mark
    fkey_far = send_across(flat(ffn_key_wide))
    layer_out, grad_fvalue, grad_frecep, grad_fkey_in, grad_frecep_in = channel_mix(
        flat(ffn_key_mixed), flat(ffn_recep_mixed), channel_lookup_matrix, channel_payload_matrix,
        channel_gate_matrix, flat(after_att), flat(final_cotangent),
    )
    layer_out, grad_fkey_in, grad_frecep_in = [
        x.reshape(full) for x in (layer_out, grad_fkey_in, grad_frecep_in)
    ]

    grad_top = final_cotangent.astype(F32)
    mark(grad_fvalue)
    fvalue_far = send_across(flat(grad_fvalue))
    ffn_delta = ffn_normed - ffn_prev
    grad_ffn_mix_key = jnp.sum(grad_fkey_in * ffn_delta, axis=(0, 1))
    grad_ffn_mix_recep = jnp.sum(grad_frecep_in * ffn_delta, axis=(0, 1))
    grad_ffn_prev = mark(
        (grad_fkey_in * (1.0 - channel_lookup_share) + grad_frecep_in * (1.0 - channel_gate_share))
        * keep[:, :, None]
    )
    first_row = gate(grad_ffn_prev[:, 0, :])
    ffn_back_edge, frecep_far, grad_frecep_far = at_once(
        ready,
        lambda: (
            shifted(first_row, "seq", -1),
            send_whole(flat(ffn_recep_wide)),
            send_half(flat(grad_frecep)),
        ),
    )
    mark(ffn_back_edge)
    grad_ffn_normed = (
        grad_fkey_in * channel_lookup_share
        + grad_frecep_in * channel_gate_share
        + jnp.concatenate([grad_ffn_prev[:, 1:, :], ffn_back_edge[:, None, :]], axis=1)
    )
    grad_ffn_ln_gain = jnp.sum(grad_ffn_normed * ffn_unit, axis=(0, 1))
    grad_ffn_ln_bias = jnp.sum(grad_ffn_normed, axis=(0, 1))
    grad_after = grad_top + norm_back(grad_ffn_normed, ffn_unit, ffn_inv, channel_norm_scale)

    grad_att_out = mark(grad_after.astype(BF16), fkey_far[1])
    grad_gated = project_back(gate(grad_att_out), emission_matrix)
    grad_num, grad_den, grad_recep, tail = scan_call(
        backward_tails_kernel,
        [grad_gated, key_proj, value_proj, recep_proj, num_state, den_state, back_windows, rate_row, bonus_row],
        [(full, F32), (full, F32), (full, BF16), tails],
    )
    fr = Partial("FR", (flat(ffn_recep_mixed), frecep_far), (flat(grad_frecep), grad_frecep_far))
    mark(tail, fkey_far[0], fvalue_far[0])
    gated_tail = gate(tail)
    state, (recep_far, out_far), fr.halves = at_once(
        ready,
        lambda: (
            enter(gated_tail, backward=True),
            send_half_of((flat(grad_recep), flat(grad_att_out))),
            fr.products(),
        ),
    )
    mark(state)

    step = functools.partial(phase, line, ready)
    ou = Partial("OU", (gated, gated_far), (flat(grad_att_out), out_far))
    ar = Partial("AR", recep_side, (flat(grad_recep), recep_far))
    fkey_cross = exchange(gate(fkey_far[1]), CORE)
    ou.multiply(line)
    fvalue_cross = exchange(gate(fvalue_far[1]), CORE)
    ar.multiply(line)
    mark(fkey_cross, fvalue_cross, ar.halves[0])

    halves = step(
        [fr, ou, ar],
        lambda: hidden_products(
            flat(ffn_key_mixed),
            (*fkey_far, fkey_cross),
            flat(grad_fvalue),
            (*fvalue_far, fvalue_cross),
            channel_lookup_matrix,
            channel_payload_matrix,
        ),
    )
    big_value, big_key = [Blocks(name, None, pair) for name, pair in zip(("BV", "BK"), halves)]
    big_key.forward(line)
    big_value.forward(line)
    grad_key, grad_value, sums = step(
        [ar, ou],
        lambda: scan_call(
            backward_states_kernel,
            [grad_num, grad_den, key_proj, value_proj, num_state, den_state, back_windows, rate_row, bonus_row, state],
            [(full, BF16), (full, BF16), ((16, features), F32)],
        ),
    )
    (key_far, value_far), grad_key_in, grad_value_in, grad_recep_in = step(
        [],
        lambda: (
            send_half_of((flat(grad_key), flat(grad_value))),
            project_back(grad_key, lookup_matrix),
            project_back(grad_value, payload_matrix),
            project_back(grad_recep, gate_matrix),
        ),
    )
    reward_slope = jnp.sum(sums[:8], axis=0)
    grad_time_decay = -decay_rate * jnp.exp(-decay_rate) * jnp.sum(sums[8:], axis=0)
    ak = Partial("AK", key_side, (flat(grad_key), key_far))
    av = Partial("AV", value_side, (flat(grad_value), value_far))
    ak.multiply(line)

    def mixes():
        normed = att_unit_again() * mixer_norm_scale + mixer_norm_offset
        att_delta = normed - with_previous(normed, att_edge, keep)
        att_back = (
            grad_key_in * (1.0 - temporal_lookup_share)
            + grad_value_in * (1.0 - temporal_payload_share)
            + grad_recep_in * (1.0 - temporal_gate_share)
        ) * keep[:, :, None]
        return (
            shifted(att_back[:, 0, :], "seq", -1),
            att_back,
            av.products(),
            jnp.sum(grad_key_in * att_delta, axis=(0, 1)),
            jnp.sum(grad_value_in * att_delta, axis=(0, 1)),
            jnp.sum(grad_recep_in * att_delta, axis=(0, 1)),
            grad_key_in * temporal_lookup_share
            + grad_value_in * temporal_payload_share
            + grad_recep_in * temporal_gate_share,
        )

    big_key.forward(line)
    big_value.forward(line)
    att_back_edge, grad_att_prev, av.halves, grad_mix_key, grad_mix_value, grad_mix_recep, direct = step(
        [ak], mixes
    )
    big_key.forward(line)
    big_value.forward(line)
    two = Stacked(line, [fr, ak])

    def norm_att():
        att_unit = att_unit_again()
        grad_att_normed = direct + jnp.concatenate(
            [grad_att_prev[:, 1:, :], att_back_edge[:, None, :]], axis=1
        )
        grad_tokens = (
            grad_after + norm_back(grad_att_normed, att_unit, att_inv, mixer_norm_scale)
        ).astype(BF16)
        return (
            grad_tokens,
            jnp.sum(grad_att_normed * att_unit, axis=(0, 1)),
            jnp.sum(grad_att_normed, axis=(0, 1)),
        )

    grad_tokens, grad_att_ln_gain, grad_att_ln_bias = step([two, av, ar], norm_att)
    vectors = Vectors(
        jnp.stack(
            [
                grad_att_ln_gain,
                grad_att_ln_bias,
                grad_mix_key,
                grad_mix_value,
                grad_mix_recep,
                grad_time_decay,
                reward_slope,
                grad_ffn_ln_gain,
                grad_ffn_ln_bias,
                grad_ffn_mix_key,
                grad_ffn_mix_recep,
            ]
        )
    )
    step([av, ou, vectors])
    big_key.forward(line)
    big_value.forward(line)
    three, pair = Stacked(line, [two, av]), Stacked(line, [ou, ar])
    step([three, pair, vectors])
    pairs = big_value.arrived(line), big_key.arrived(line)

    (ou_sum, ar_sum), quarters = step(
        [three, vectors],
        lambda: at_once(ready, lambda: (gather(total_of(pair.terms)), join_hidden(*pairs))),
    )
    (fr_sum, ak_sum, av_sum), (got, (value_sum, key_sum)) = step(
        [],
        lambda: gather(
            total_of(three.terms),
            lambda: at_once(ready, lambda: (vectors.hop(), whole_hidden(*quarters))),
        ),
    )
    vectors.landed(lax.optimization_barrier(got))
    small = total_of(vectors.terms)
    return (
        layer_out,
        grad_tokens,
        *[small[i] for i in range(7)],
        ak_sum,
        av_sum,
        ar_sum,
        ou_sum,
        *[small[i] for i in range(7, 11)],
        key_sum,
        value_sum,
        fr_sum,
    )


def solution(mesh):
    tokens = P("batch", "seq", None)
    vector, matrix = P("seq"), P("seq", None)
    return jax.shard_map(
        shards,
        mesh=mesh,
        in_specs=(tokens, P("batch", None), *([P()] * 18), tokens),
        out_specs=(tokens, tokens, *([vector] * 7), *([matrix] * 4), *([vector] * 4), *([matrix] * 3)),
        check_vma=False,
    )
```
